32 devices in a mesh: segment: 2 (over y), rows: 16 (over z, x, core).
Axes of the slice: x: 2, y: 2, z: 4, core: 2. Of those that a mesh axis runs over, the one named last changes fastest.
Arguments:
- incoming: bfloat16 [2, 64, 128, 128], P('segment', 'rows'), may hold values from -6 to 6
- cotangent: bfloat16 [2, 64, 128, 128], P('segment', 'rows'), may hold values from -6 to 6
- main_weight: bfloat16 [2, 3, 3, 128, 128], P('segment'), may hold values from -0.1875 to 0.1875
- second_weight: bfloat16 [2, 3, 3, 128, 128], P('segment'), may hold values from -0.1875 to 0.1875
Outputs:
- output: bfloat16 [2, 64, 128, 128], P('segment', 'rows')
- input_grad: bfloat16 [2, 64, 128, 128], P('segment', 'rows')
- main_grad: float32 [2, 3, 3, 128, 128], P('segment')
- second_grad: float32 [2, 3, 3, 128, 128], P('segment')
The draws below stay inside these ranges and needn't reach their ends.
All inputs are finite; a program needn't handle non-finite values.
Results may differ from the reference program's by a relative error of at most 0.011.
Values may be sent and summed in bfloat16 or wider, within the bound.
No kernel may reach another device: no remote copies, remote signals or barrier semaphores. Data moves between devices by JAX's collectives and lax.ppermute only.
A program may use at most 64 MiB of HBM per device.

```python
import math
import jax
import jax.numpy as jnp
from jax import lax

C = 128
W = 128
H = 64
N_SEGMENT = 2


def levels(rng, shape, shards, low, high):
    level = 1.0
    for axis_at, shards_of in shards:
        draws = jax.random.uniform(jax.random.fold_in(jax.random.fold_in(rng, 6), axis_at), (shards_of,), jnp.float32, low / len(shards), high / len(shards))
        level = level * jnp.repeat(jnp.exp(draws), shape[axis_at] // shards_of).reshape((-1,) + (1,) * (len(shape) - 1 - axis_at))
    return level


def scatter_about(stream_key, shape, scale, bound, split=(), kind=jnp.bfloat16):
    entries = jax.random.normal(stream_key, shape, jnp.float32) * scale
    if len(split) > 0:
        entries = levels(stream_key, shape, split, -0.22, 0.18) * entries
    return jnp.clip(entries, min=-bound, max=bound).astype(kind)


def setup_inputs(seed: int = 0) -> dict:
    seeds = jax.random.split(jax.random.key(seed), 5)
    return {
        "incoming": scatter_about(seeds[0], (N_SEGMENT, H, W, C), 1.0, 6.0, ((0, 2), (1, 16))),
        "cotangent": scatter_about(seeds[1], (N_SEGMENT, H, W, C), 1.0, 6.0, ((0, 2), (1, 16))),
        "main_weight": scatter_about(seeds[2], (N_SEGMENT, 3, 3, C, C), (9 * C) ** -0.5, 0.1875, ((0, 2),)),
        "second_weight": scatter_about(seeds[3], (N_SEGMENT, 3, 3, C, C), (9 * C) ** -0.5, 0.1875, ((0, 2),)),
    }


def silu(values):
    return values * jax.nn.sigmoid(values)

def slope(values):
    gate_value = jax.nn.sigmoid(values)
    return gate_value * (1.0 + values * (1.0 - gate_value))

def rimmed(field):
    return jnp.pad(field, ((1, 1), (0, 0), (0, 0)))

def widen(padded):
    breadth = padded.shape[1]
    widened = jnp.pad(padded, ((0, 0), (1, 1), (0, 0)))
    return jnp.concatenate([widened[:, 0:breadth], widened[:, 1:breadth + 1], widened[:, 2:breadth + 2]], axis=-1)

def convolve(padded, weight):
    stacked = widen(padded)
    height = padded.shape[0] - 2
    breadth = padded.shape[1]
    inner_dim = stacked.shape[-1]
    summed = jnp.zeros((height * breadth, weight.shape[-1]), jnp.float32)
    for offset in range(3):
        summed = summed + jnp.dot(stacked[offset:offset + height].reshape(-1, inner_dim), weight[offset].reshape(inner_dim, -1), preferred_element_type=jnp.float32)
    return summed.reshape(height, breadth, -1)

def transpose_conv(padded, weight):
    return convolve(padded, jnp.flip(weight, (0, 1)).transpose(0, 1, 3, 2))

def weight_grad(padded, gradient):
    stacked = widen(padded)
    height = gradient.shape[0]
    inner_dim = stacked.shape[-1]
    outer_dim = gradient.shape[-1]
    pieces = []
    for offset in range(3):
        product = lax.dot_general(stacked[offset:offset + height].reshape(-1, inner_dim), gradient.reshape(-1, outer_dim), (((0,), (0,)), ((), ())), preferred_element_type=jnp.float32)
        pieces.append(product.reshape(3, -1, outer_dim))
    return jnp.stack(pieces)

def reference(incoming, cotangent, main_weight, second_weight):
    segments = incoming.shape[0]
    factor = 1.0 / math.sqrt(H * W)
    outputs = [None] * segments
    inputs_back = [None] * segments
    firsts = [None] * segments
    seconds = [None] * segments
    for encoder_segment in range(segments // 2):
        decoder_segment = encoder_segment + segments // 2
        source_enc = incoming[encoder_segment]
        source_dec = incoming[decoder_segment]
        first_pre = convolve(rimmed(source_enc), main_weight[encoder_segment])
        hidden = silu(first_pre).astype(jnp.bfloat16)
        encoder_pre = convolve(rimmed(hidden), second_weight[encoder_segment])
        skip = silu(encoder_pre).astype(jnp.bfloat16)
        decoder_pre = convolve(rimmed(source_dec), main_weight[decoder_segment]) + convolve(rimmed(skip), second_weight[decoder_segment])
        outputs[encoder_segment] = skip
        outputs[decoder_segment] = silu(decoder_pre).astype(jnp.bfloat16)
        decoder_grad = (cotangent[decoder_segment].astype(jnp.float32) * slope(decoder_pre)).astype(jnp.bfloat16)
        skip_grad = transpose_conv(rimmed(decoder_grad), second_weight[decoder_segment]).astype(jnp.bfloat16)
        inputs_back[decoder_segment] = transpose_conv(rimmed(decoder_grad), main_weight[decoder_segment]).astype(jnp.bfloat16)
        firsts[decoder_segment] = weight_grad(rimmed(source_dec), decoder_grad) * factor
        seconds[decoder_segment] = weight_grad(rimmed(skip), decoder_grad) * factor
        encoder_grad = ((cotangent[encoder_segment].astype(jnp.float32) + skip_grad.astype(jnp.float32)) * slope(encoder_pre)).astype(jnp.bfloat16)
        hidden_grad = (transpose_conv(rimmed(encoder_grad), second_weight[encoder_segment]) * slope(first_pre)).astype(jnp.bfloat16)
        inputs_back[encoder_segment] = transpose_conv(rimmed(hidden_grad), main_weight[encoder_segment]).astype(jnp.bfloat16)
        firsts[encoder_segment] = weight_grad(rimmed(source_enc), hidden_grad) * factor
        seconds[encoder_segment] = weight_grad(rimmed(hidden), encoder_grad) * factor
    return (jnp.stack(outputs), jnp.stack(inputs_back), jnp.stack(firsts), jnp.stack(seconds))
```

```python
import math

import jax
import jax.numpy as jnp
from jax import lax
from jax.sharding import PartitionSpec as P


def padded_2(block, sides, width):
    for axis, dim in sides:
        count = lax.axis_size(axis)
        here = lax.axis_index(axis)
        forward = [(i, (i + 1) % count) for i in range(count)]
        backward = [(target, source) for source, target in forward]
        low = lax.ppermute(
            lax.slice_in_dim(block, block.shape[dim] - width, None, axis=dim), axis, forward
        )
        high = lax.ppermute(lax.slice_in_dim(block, 0, width, axis=dim), axis, backward)
        low = jnp.where(here > 0, low, jnp.zeros_like(low))
        high = jnp.where(here < count - 1, high, jnp.zeros_like(high))
        block = jnp.concatenate([low, block, high], axis=dim)
    return block


def partner(array, axis, apart):
    return lax.ppermute(array, axis, [(i, i ^ 1 << apart) for i in range(lax.axis_size(axis))])


def silu(values):
    return values * jax.nn.sigmoid(values)


def slope(values):
    gate_value = jax.nn.sigmoid(values)
    return gate_value * (1.0 + values * (1.0 - gate_value))


def widen(padded):
    breadth = padded.shape[1]
    widened = jnp.pad(padded, ((0, 0), (1, 1), (0, 0)))
    return jnp.concatenate(
        [widened[:, 0:breadth], widened[:, 1 : breadth + 1], widened[:, 2 : breadth + 2]], axis=-1
    )


def convolve(padded, weight):
    stacked = widen(padded)
    height = padded.shape[0] - 2
    breadth = padded.shape[1]
    inner_dim = stacked.shape[-1]
    summed = jnp.zeros((height * breadth, weight.shape[-1]), jnp.float32)
    for offset in range(3):
        summed = summed + jnp.dot(
            stacked[offset : offset + height].reshape(-1, inner_dim),
            weight[offset].reshape(inner_dim, -1),
            preferred_element_type=jnp.float32,
        )
    return summed.reshape(height, breadth, -1)


def transpose_conv(padded, weight):
    return convolve(padded, jnp.flip(weight, (0, 1)).transpose(0, 1, 3, 2))


def weight_grad(padded, gradient):
    stacked = widen(padded)
    height = gradient.shape[0]
    inner_dim = stacked.shape[-1]
    outer_dim = gradient.shape[-1]
    pieces = []
    for offset in range(3):
        product = lax.dot_general(
            stacked[offset : offset + height].reshape(-1, inner_dim),
            gradient.reshape(-1, outer_dim),
            (((0,), (0,)), ((), ())),
            preferred_element_type=jnp.float32,
        )
        pieces.append(product.reshape(3, -1, outer_dim))
    return jnp.stack(pieces)


def margin(field):
    return padded_2(field, (("rows", 0),), 1)


def mirror(field, top_bit):
    return partner(field, "segment", top_bit)


def total(terms, axis):
    count = lax.axis_size(axis)
    here = lax.axis_index(axis)
    bits = count.bit_length() - 1
    current = terms
    for bit in range(bits):
        swap = [(i, i ^ (1 << bit)) for i in range(count)]
        upper = (here >> bit) & 1
        half = current.shape[0] // 2
        kept = lax.dynamic_slice_in_dim(current, upper * half, half, 0)
        sent = lax.dynamic_slice_in_dim(current, (1 - upper) * half, half, 0)
        got = lax.ppermute(sent.astype(jnp.bfloat16), axis, swap)
        current = kept + got.astype(jnp.float32)
    current = current.astype(jnp.bfloat16)
    for bit in reversed(range(bits)):
        swap = [(i, i ^ (1 << bit)) for i in range(count)]
        upper = ((here >> bit) & 1) == 1
        got = lax.ppermute(current, axis, swap)
        current = jnp.concatenate(
            [jnp.where(upper, got, current), jnp.where(upper, current, got)], axis=0
        )
    return current.astype(jnp.float32)


def body(incoming, cotangent, main_weight, second_weight):
    source = incoming[0]
    upstream = cotangent[0]
    first_kernel = main_weight[0]
    second_kernel = second_weight[0]
    strip_rows, columns, channels = source.shape
    segments = lax.axis_size("segment")
    top_bit = segments.bit_length() - 2
    encoder = lax.axis_index("segment") < segments // 2
    nothing = jnp.zeros((strip_rows, columns, channels), jnp.float32)
    source_rim = margin(source)
    first_pre = convolve(source_rim, first_kernel)
    hidden = silu(first_pre).astype(jnp.bfloat16)
    hidden_rim = margin(hidden)
    encoder_pre = lax.cond(encoder, lambda: convolve(hidden_rim, second_kernel), lambda: nothing)
    skip_rim = margin(mirror(silu(encoder_pre).astype(jnp.bfloat16), top_bit))
    skip_pre = lax.cond(encoder, lambda: nothing, lambda: convolve(skip_rim, second_kernel))
    final_pre = jnp.where(encoder, encoder_pre, first_pre + skip_pre)
    output = silu(final_pre).astype(jnp.bfloat16)
    decoder_grad = (upstream.astype(jnp.float32) * slope(final_pre)).astype(jnp.bfloat16)
    decoder_rim = margin(decoder_grad)
    skip_grad, decoder_input = lax.cond(
        encoder,
        lambda: (nothing, nothing),
        lambda: (
            transpose_conv(decoder_rim, second_kernel),
            transpose_conv(decoder_rim, first_kernel),
        ),
    )
    returned = mirror(skip_grad.astype(jnp.bfloat16), top_bit)
    encoder_grad = (
        (upstream.astype(jnp.float32) + returned.astype(jnp.float32)) * slope(encoder_pre)
    ).astype(jnp.bfloat16)
    encoder_rim = margin(encoder_grad)
    hidden_back = lax.cond(
        encoder, lambda: transpose_conv(encoder_rim, second_kernel), lambda: nothing
    )
    hidden_grad = (hidden_back * slope(first_pre)).astype(jnp.bfloat16)
    hidden_grad_rim = margin(hidden_grad)
    encoder_input = lax.cond(
        encoder, lambda: transpose_conv(hidden_grad_rim, first_kernel), lambda: nothing
    )
    input_grad = jnp.where(encoder, encoder_input, decoder_input).astype(jnp.bfloat16)
    first_terms = weight_grad(source_rim, jnp.where(encoder, hidden_grad, decoder_grad))
    second_terms = weight_grad(
        jnp.where(encoder, hidden_rim, skip_rim), jnp.where(encoder, encoder_grad, decoder_grad)
    )
    shape = first_terms.shape
    flat = total(
        jnp.concatenate(
            [first_terms.reshape(-1, shape[-1]), second_terms.reshape(-1, shape[-1])], axis=0
        ),
        "rows",
    )
    first_sum, second_sum = flat.reshape((2,) + shape)
    factor = 1.0 / math.sqrt(strip_rows * lax.axis_size("rows") * columns)
    return (output[None], input_grad[None], (first_sum * factor)[None], (second_sum * factor)[None])


def solution(mesh):
    return jax.shard_map(
        body,
        mesh=mesh,
        in_specs=(
            P("segment", "rows", None, None),
            P("segment", "rows", None, None),
            P("segment", None, None, None, None),
            P("segment", None, None, None, None),
        ),
        out_specs=(
            P("segment", "rows", None, None),
            P("segment", "rows", None, None),
            P("segment", None, None, None, None),
            P("segment", None, None, None, None),
        ),
        check_vma=False,
    )
```

```python
import functools
import math

import jax
import jax.numpy as jnp
from jax import lax
from jax.experimental import pallas as pl
from jax.experimental.pallas import tpu as pltpu
from jax.sharding import PartitionSpec as P

BF16 = jnp.bfloat16
F32 = jnp.float32
TAPS = [(ty, tx) for ty in range(3) for tx in range(3)]


def silu(values):
    return values * jax.nn.sigmoid(values)


def slope(values):
    gate_value = jax.nn.sigmoid(values)
    return gate_value * (1.0 + values * (1.0 - gate_value))


def place(wide, row, values):
    columns, channels = values.shape
    column = lax.broadcasted_iota(jnp.int32, (columns, channels), 0)
    left = jnp.where(column == 0, 0.0, pltpu.roll(values, 1, 0))
    right = jnp.where(column == columns - 1, 0.0, pltpu.roll(values, columns - 1, 0))
    wide[row, :, 0:channels] = left.astype(BF16)
    wide[row, :, channels : 2 * channels] = values.astype(BF16)
    wide[row, :, 2 * channels : 3 * channels] = right.astype(BF16)


def stacked(wide, start, rows):
    parts = [wide[start + ty : start + ty + rows] for ty in range(3)]
    return jnp.concatenate([part.reshape(rows * part.shape[1], part.shape[2]) for part in parts], axis=1)


def conv(wide, start, rows, kernel):
    lhs = stacked(wide, start, rows)
    out = jnp.dot(lhs, kernel[...].reshape(-1, kernel.shape[-1]), preferred_element_type=F32)
    return out.reshape(rows, -1, out.shape[-1])


def conv_back(wide, start, rows, kernel):
    lhs = stacked(wide, start, rows)
    rhs = jnp.concatenate([kernel[2 - ty, 2 - tx] for ty, tx in TAPS], axis=1)
    out = lax.dot_general(lhs, rhs, (((1,), (1,)), ((), ())), preferred_element_type=F32)
    return out.reshape(rows, -1, out.shape[-1])


def conv_weight(field, wide, start, store):
    rows, columns, channels = field.shape
    lhs = field.reshape(rows * columns, channels)
    for ty in range(3):
        rhs = wide[start + 2 - ty : start + 2 - ty + rows]
        out = lax.dot_general(
            lhs, rhs.reshape(rows * columns, -1), (((0,), (0,)), ((), ())), preferred_element_type=F32
        )
        for tx in range(3):
            store(ty, tx, out[:, (2 - tx) * channels : (3 - tx) * channels])


def here(segments):
    row = lax.axis_index("rows")
    return lax.axis_index("segment") < segments // 2, row, lax.rem(row, 2) == 0


def inside(row, strips, own, offset):
    if offset < 0:
        return row > 0
    if offset >= own:
        return row < strips - 1
    return None


def masked(values, keep):
    return values if keep is None else jnp.where(keep, values, 0.0)


def front_kernel(segments, strips, x, x_core, x_other, main, second, pre1, pre2, hid, skip, xw, hw):
    encoder, row, even = here(segments)
    own = x.shape[0]
    core_at = jnp.where(even, 2 * own, 0)
    other_at = jnp.where(even, 0, 2 * own)
    core_in = jnp.where(even, row < strips - 1, row > 0)
    other_in = jnp.where(even, row > 0, row < strips - 1)
    for i in range(own):
        place(xw, own + i, x[i].astype(F32))
        place(xw, core_at + i, masked(x_core[i].astype(F32), core_in))
        place(xw, other_at + i, masked(x_other[i].astype(F32), other_in))

    @pl.when(encoder)
    def _():
        first = conv(xw, 0, own + 6, main)
        pre1[...] = first[2 : own + 4]
        for i in range(own + 6):
            value = masked(silu(first[i]), inside(row, strips, own, i - 3))
            place(hw, i, value)
            if 3 <= i < own + 3:
                hid[i - 3] = value.astype(BF16)
        final = conv(hw, 0, own + 4, second)
        pre2[...] = final
        for i in range(own + 4):
            skip[i] = masked(silu(final[i]), inside(row, strips, own, i - 2)).astype(BF16)

    @pl.when(jnp.logical_not(encoder))
    def _():
        pre1[...] = conv(xw, 2, own + 2, main)


def middle_kernel(
    segments, strips, skip_here, skip_there, pre1, g, g_core, g_other, second, out, grad, back, edge_core, edge_other, yw, gw
):
    encoder, row, even = here(segments)
    own = g.shape[0]

    @pl.when(encoder)
    def _():
        out[...] = skip_here[2 : own + 2]

    @pl.when(jnp.logical_not(encoder))
    def _():
        for i in range(own + 4):
            place(yw, i, skip_there[i].astype(F32))
        pre = pre1[...] + conv(yw, 0, own + 4 - 2, second)
        for i in range(own + 2):
            if i == 0:
                upstream = jnp.where(even, g_other[own - 1].astype(F32), g_core[own - 1].astype(F32))
            elif i == own + 1:
                upstream = jnp.where(even, g_core[0].astype(F32), g_other[0].astype(F32))
            else:
                upstream = g[i - 1].astype(F32)
                out[i - 1] = silu(pre[i]).astype(BF16)
            value = masked(upstream * slope(pre[i]), inside(row, strips, own, i - 1))
            place(gw, i, value)
            grad[i] = value.astype(BF16)
        back[...] = conv_back(gw, 0, own, second).astype(BF16)
        edge_core[...] = jnp.where(even, back[own - 2 : own], back[0:2])
        edge_other[...] = jnp.where(even, back[0:2], back[own - 2 : own])


def end_kernel(
    segments, strips, x, g, g_core, g_other, back, back_core, back_other, pre1, pre2, hid, skip_there, grad, main, second,
    input_grad, kept, sent, ew, hw,
):
    encoder, row, even = here(segments)
    own = x.shape[0]

    def store(first):
        keep = jnp.logical_xor(even, not first)

        def put(ty, tx, values):
            @pl.when(keep)
            def _():
                kept[ty, tx] = values

            @pl.when(jnp.logical_not(keep))
            def _():
                sent[ty, tx] = values.astype(BF16)

        return put

    @pl.when(encoder)
    def _():
        for i in range(own + 4):
            if i < 2:
                upstream = jnp.where(even, g_other[own - 2 + i].astype(F32), g_core[own - 2 + i].astype(F32))
                returned = jnp.where(even, back_other[i].astype(F32), back_core[i].astype(F32))
            elif i >= own + 2:
                upstream = jnp.where(even, g_core[i - own - 2].astype(F32), g_other[i - own - 2].astype(F32))
                returned = jnp.where(
                    even, back_core[i - own - 2].astype(F32), back_other[i - own - 2].astype(F32)
                )
            else:
                upstream = g[i - 2].astype(F32)
                returned = back[i - 2].astype(F32)
            value = (upstream + returned) * slope(pre2[i])
            place(ew, i, masked(value, inside(row, strips, own, i - 2)))
        hidden_back = conv_back(ew, 0, own + 2, second)
        for i in range(own + 2):
            value = hidden_back[i] * slope(pre1[i])
            place(hw, i, masked(value, inside(row, strips, own, i - 1)))
        conv_weight(hid[...], ew, 1, store(False))

    @pl.when(jnp.logical_not(encoder))
    def _():
        for i in range(own + 2):
            place(hw, i, grad[i].astype(F32))
        conv_weight(skip_there[2 : own + 2], hw, 0, store(False))

    conv_weight(x[...], hw, 0, store(True))
    input_grad[...] = conv_back(hw, 0, own, main).astype(BF16)


def call(kernel, outs, scratch, args, flops):
    moved = sum(math.prod(a.shape) * a.dtype.itemsize for a in list(args) + outs)
    return pl.pallas_call(
        kernel,
        out_shape=outs,
        in_specs=[pl.BlockSpec(memory_space=pltpu.VMEM)] * len(args),
        out_specs=[pl.BlockSpec(memory_space=pltpu.VMEM)] * len(outs),
        scratch_shapes=scratch,
        cost_estimate=pl.CostEstimate(flops=flops, bytes_accessed=moved, transcendentals=0),
        compiler_params=pltpu.CompilerParams(vmem_limit_bytes=32 * 1024 * 1024),
    )(*args)


def body(incoming, cotangent, main_weight, second_weight):
    x, g, main, second = incoming[0], cotangent[0], main_weight[0], second_weight[0]
    own, columns, channels = x.shape
    segments, strips = lax.axis_size("segment"), lax.axis_size("rows")
    half = segments // 2
    row = lax.axis_index("rows")
    even = row % 2 == 0
    everyone = [(s, r) for s in range(segments) for r in range(strips)]

    def core(r):
        return r ^ 1

    def other(r):
        neighbour = r - 1 if r % 2 == 0 else r + 1
        return neighbour if 0 <= neighbour < strips else r

    def same(r):
        return r

    def swap(array, across, to):
        pairs = [
            (s * strips + r, ((s + half) % segments if across else s) * strips + to(r)) for s, r in everyone
        ]
        return lax.ppermute(array, ("segment", "rows"), pairs)

    def like(rows, dtype):
        return jax.ShapeDtypeStruct((rows, columns, channels), dtype)

    def wide(rows):
        return pltpu.VMEM((rows, columns, 3 * channels), BF16)

    work = 2 * columns * 9 * channels * channels
    x_other = swap(x, False, other)
    x_core = swap(x, False, core)
    g_other = swap(g, False, other)
    g_core = swap(g, False, core)
    pre1, pre2, hid, skip_here = call(
        functools.partial(front_kernel, segments, strips),
        [like(own + 2, F32), like(own + 4, F32), like(own, BF16), like(own + 4, BF16)],
        [wide(3 * own), wide(own + 6)],
        (x, x_core, x_other, main, second),
        work * (2 * own + 10),
    )
    skip_there = swap(skip_here, True, same)
    output, grad, back, edge_core, edge_other = call(
        functools.partial(middle_kernel, segments, strips),
        [like(own, BF16), like(own + 2, BF16), like(own, BF16), like(2, BF16), like(2, BF16)],
        [wide(own + 4), wide(own + 2)],
        (skip_here, skip_there, pre1, g, g_core, g_other, second),
        work * (2 * own + 2),
    )
    back_own = swap(back, True, same)
    back_other = swap(edge_other, True, other)
    back_core = swap(edge_core, True, core)
    taps = (3, 3, channels, channels)
    input_grad, kept, sent = call(
        functools.partial(end_kernel, segments, strips),
        [like(own, BF16), jax.ShapeDtypeStruct(taps, F32), jax.ShapeDtypeStruct(taps, BF16)],
        [wide(own + 4), wide(own + 2)],
        (x, g, g_core, g_other, back_own, back_core, back_other, pre1, pre2, hid, skip_there, grad, main, second),
        work * (4 * own + 2),
    )
    chips = strips // 2
    groups = [list(range(0, strips, 2)), list(range(1, strips, 2))]
    mine = (kept + swap(sent, False, core).astype(F32)).astype(BF16)
    mine = mine.reshape(chips, -1, channels)
    mine = lax.all_to_all(mine, "rows", 0, 0, axis_index_groups=groups)
    mine = jnp.sum(mine.astype(F32), axis=0).astype(BF16)
    mine = jnp.broadcast_to(mine[None], (chips,) + mine.shape)
    mine = lax.all_to_all(mine, "rows", 0, 0, axis_index_groups=groups).reshape(taps)
    theirs = swap(mine, False, core)
    factor = 1.0 / math.sqrt(own * strips * columns)
    first_sum = jnp.where(even, mine, theirs).astype(F32) * factor
    second_sum = jnp.where(even, theirs, mine).astype(F32) * factor
    return (output[None], input_grad[None], first_sum[None], second_sum[None])


def solution(mesh):
    field = P("segment", "rows", None, None)
    weight = P("segment", None, None, None, None)
    return jax.shard_map(
        body,
        mesh=mesh,
        in_specs=(field, field, weight, weight),
        out_specs=(field, field, weight, weight),
        check_vma=False,
    )
```

```python
import functools
import math

import jax
import jax.numpy as jnp
from jax import lax
from jax.experimental import pallas as pl
from jax.experimental.pallas import tpu as pltpu
from jax.sharding import PartitionSpec as P

BF16 = jnp.bfloat16
F32 = jnp.float32
TAPS = [(ty, tx) for ty in range(3) for tx in range(3)]


def silu(values):
    return values * jax.nn.sigmoid(values)


def slope(values):
    gate_value = jax.nn.sigmoid(values)
    return gate_value * (1.0 + values * (1.0 - gate_value))


def place(wide, row, values):
    columns, channels = values.shape
    column = lax.broadcasted_iota(jnp.int32, (columns, channels), 0)
    left = jnp.where(column == 0, 0.0, pltpu.roll(values, 1, 0))
    right = jnp.where(column == columns - 1, 0.0, pltpu.roll(values, columns - 1, 0))
    wide[row, :, 0:channels] = left.astype(BF16)
    wide[row, :, channels : 2 * channels] = values.astype(BF16)
    wide[row, :, 2 * channels : 3 * channels] = right.astype(BF16)


def stacked(wide, start, rows):
    parts = [wide[start + ty : start + ty + rows] for ty in range(3)]
    return jnp.concatenate([part.reshape(rows * part.shape[1], part.shape[2]) for part in parts], axis=1)


def conv(wide, start, rows, kernel):
    lhs = stacked(wide, start, rows)
    out = jnp.dot(lhs, kernel[...].reshape(-1, kernel.shape[-1]), preferred_element_type=F32)
    return out.reshape(rows, -1, out.shape[-1])


def conv_back(wide, start, rows, kernel):
    lhs = stacked(wide, start, rows)
    rhs = jnp.concatenate([kernel[2 - ty, 2 - tx] for ty, tx in TAPS], axis=1)
    out = lax.dot_general(lhs, rhs, (((1,), (1,)), ((), ())), preferred_element_type=F32)
    return out.reshape(rows, -1, out.shape[-1])


def conv_weight(field, wide, start, store):
    rows, columns, channels = field.shape
    lhs = field.reshape(rows * columns, channels)
    for ty in range(3):
        rhs = wide[start + 2 - ty : start + 2 - ty + rows]
        out = lax.dot_general(
            lhs, rhs.reshape(rows * columns, -1), (((0,), (0,)), ((), ())), preferred_element_type=F32
        )
        for tx in range(3):
            store(ty, tx, out[:, (2 - tx) * channels : (3 - tx) * channels])


def here(segments):
    row = lax.axis_index("rows")
    return lax.axis_index("segment") < segments // 2, row, lax.rem(row, 2) == 0


def inside(row, strips, own, offset):
    if offset < 0:
        return row > 0
    if offset >= own:
        return row < strips - 1
    return None


def masked(values, keep):
    return values if keep is None else jnp.where(keep, values, 0.0)


def early_kernel(x, main, second, xw, mid):
    own = x.shape[0]
    for i in range(own):
        place(xw, i, x[i].astype(F32))
    mid[...] = conv(xw, 0, own - 2, main)


def front_kernel(segments, strips, xo, mid, x_core, x_other, main, second, pre1, pre2, hid, skip, xw, hw):
    encoder, row, even = here(segments)
    own = xo.shape[0]
    core_at = jnp.where(even, 2 * own, 0)
    other_at = jnp.where(even, 0, 2 * own)
    core_in = jnp.where(even, row < strips - 1, row > 0)
    other_in = jnp.where(even, row > 0, row < strips - 1)
    xw[own : 2 * own] = xo[...]
    for i in range(own):
        place(xw, core_at + i, masked(x_core[i].astype(F32), core_in))
        place(xw, other_at + i, masked(x_other[i].astype(F32), other_in))

    @pl.when(encoder)
    def _():
        above = conv(xw, 0, 4, main)
        below = conv(xw, own + 2, 4, main)
        pre1[0:2] = above[2:4]
        pre1[2:own] = mid[...]
        pre1[own : own + 2] = below[0:2]
        for i in range(own + 6):
            first = above[i] if i < 4 else below[i - own - 2] if i >= own + 2 else mid[i - 4]
            value = masked(silu(first), inside(row, strips, own, i - 3))
            place(hw, i, value)
            if 3 <= i < own + 3:
                hid[i - 3] = value.astype(BF16)
        final = conv(hw, 0, own + 4, second)
        pre2[...] = final
        for i in range(own + 4):
            skip[i] = masked(silu(final[i]), inside(row, strips, own, i - 2)).astype(BF16)

    @pl.when(jnp.logical_not(encoder))
    def _():
        pre1[0:2] = conv(xw, 2, 2, main)
        pre1[2:own] = mid[...]
        pre1[own : own + 2] = conv(xw, own + 2, 2, main)


def middle_kernel(
    segments, strips, skip_here, skip_there, pre1, g, g_core, g_other, second, out, grad, back, edge_core, edge_other, yw, gw
):
    encoder, row, even = here(segments)
    own = g.shape[0]

    @pl.when(encoder)
    def _():
        out[...] = skip_here[2 : own + 2]

    @pl.when(jnp.logical_not(encoder))
    def _():
        for i in range(own + 4):
            place(yw, i, skip_there[i].astype(F32))
        pre = pre1[...] + conv(yw, 0, own + 4 - 2, second)
        for i in range(own + 2):
            if i == 0:
                upstream = jnp.where(even, g_other[1].astype(F32), g_core[1].astype(F32))
            elif i == own + 1:
                upstream = jnp.where(even, g_core[0].astype(F32), g_other[0].astype(F32))
            else:
                upstream = g[i - 1].astype(F32)
                out[i - 1] = silu(pre[i]).astype(BF16)
            value = masked(upstream * slope(pre[i]), inside(row, strips, own, i - 1))
            place(gw, i, value)
            grad[i] = value.astype(BF16)
        back[...] = conv_back(gw, 0, own, second).astype(BF16)
        edge_core[...] = jnp.where(even, back[own - 2 : own], back[0:2])
        edge_other[...] = jnp.where(even, back[0:2], back[own - 2 : own])


def end_kernel(
    segments, strips, x, g, g_core, g_other, back, back_core, back_other, pre1, pre2, hid, skip_there, grad, second,
    kept, sent, hw, ew,
):
    encoder, row, even = here(segments)
    own = x.shape[0]

    def store(first):
        keep = jnp.logical_xor(even, not first)

        def put(ty, tx, values):
            @pl.when(keep)
            def _():
                kept[ty, tx] = values

            @pl.when(jnp.logical_not(keep))
            def _():
                sent[ty, tx] = values.astype(BF16)

        return put

    @pl.when(encoder)
    def _():
        for i in range(own + 4):
            if i < 2:
                upstream = jnp.where(even, g_other[i].astype(F32), g_core[i].astype(F32))
                returned = jnp.where(even, back_other[i].astype(F32), back_core[i].astype(F32))
            elif i >= own + 2:
                upstream = jnp.where(even, g_core[i - own - 2].astype(F32), g_other[i - own - 2].astype(F32))
                returned = jnp.where(
                    even, back_core[i - own - 2].astype(F32), back_other[i - own - 2].astype(F32)
                )
            else:
                upstream = g[i - 2].astype(F32)
                returned = back[i - 2].astype(F32)
            value = (upstream + returned) * slope(pre2[i])
            place(ew, i, masked(value, inside(row, strips, own, i - 2)))
        hidden_back = conv_back(ew, 0, own + 2, second)
        for i in range(own + 2):
            value = hidden_back[i] * slope(pre1[i])
            place(hw, i, masked(value, inside(row, strips, own, i - 1)))
        conv_weight(hid[...], ew, 1, store(False))

    @pl.when(jnp.logical_not(encoder))
    def _():
        for i in range(own + 2):
            place(hw, i, grad[i].astype(F32))
        conv_weight(skip_there[2 : own + 2], hw, 0, store(False))

    conv_weight(x[...], hw, 0, store(True))


def input_kernel(hw, main, input_grad):
    input_grad[...] = conv_back(hw, 0, input_grad.shape[0], main).astype(BF16)


def pack_kernel(strips, kept, got, mine, *sends):
    chip = lax.axis_index("rows") // 2
    mine[...] = kept[chip] + got[chip].astype(F32)
    for k, send in enumerate(sends):
        at = jnp.bitwise_xor(chip, k + 1)
        send[...] = (kept[at] + got[at].astype(F32)).astype(BF16)


def unpack_kernel(strips, mine, *rest):
    gots, out = rest[:-1], rest[-1]
    chip = lax.axis_index("rows") // 2
    out[chip] = mine[...]
    for k, got in enumerate(gots):
        out[jnp.bitwise_xor(chip, k + 1)] = got[...]


def call(kernel, outs, scratch, args, flops):
    moved = sum(math.prod(a.shape) * a.dtype.itemsize for a in list(args) + outs)
    return pl.pallas_call(
        kernel,
        out_shape=outs,
        in_specs=[pl.BlockSpec(memory_space=pltpu.VMEM)] * len(args),
        out_specs=[pl.BlockSpec(memory_space=pltpu.VMEM)] * len(outs),
        scratch_shapes=scratch,
        cost_estimate=pl.CostEstimate(flops=flops, bytes_accessed=moved, transcendentals=0),
        compiler_params=pltpu.CompilerParams(vmem_limit_bytes=32 * 1024 * 1024),
    )(*args)


def body(incoming, cotangent, main_weight, second_weight):
    x, g, main, second = incoming[0], cotangent[0], main_weight[0], second_weight[0]
    own, columns, channels = x.shape
    segments, strips = lax.axis_size("segment"), lax.axis_size("rows")
    half = segments // 2
    row = lax.axis_index("rows")
    even = row % 2 == 0
    everyone = [(s, r) for s in range(segments) for r in range(strips)]

    def core(r):
        return r ^ 1

    def other(r):
        neighbour = r - 1 if r % 2 == 0 else r + 1
        return neighbour if 0 <= neighbour < strips else r

    def same(r):
        return r

    def swap(array, across, to):
        pairs = [
            (s * strips + r, ((s + half) % segments if across else s) * strips + to(r)) for s, r in everyone
        ]
        return lax.ppermute(array, ("segment", "rows"), pairs)

    def like(rows, dtype):
        return jax.ShapeDtypeStruct((rows, columns, channels), dtype)

    def wide(rows):
        return pltpu.VMEM((rows, columns, 3 * channels), BF16)

    def wide_out(rows):
        return jax.ShapeDtypeStruct((rows, columns, 3 * channels), BF16)

    work = 2 * columns * 9 * channels * channels
    x_other = swap(x, False, other)
    x_core = swap(x, False, core)
    xo, mid = call(
        early_kernel,
        [wide_out(own), like(own - 2, F32)],
        [],
        (x, main, second),
        work * (own - 2),
    )
    pre1, pre2, hid, skip_here = call(
        functools.partial(front_kernel, segments, strips),
        [like(own + 2, F32), like(own + 4, F32), like(own, BF16), like(own + 4, BF16)],
        [wide(3 * own), wide(own + 6)],
        (xo, mid, x_core, x_other, main, second),
        work * (2 * own + 8),
    )
    g_core = swap(jnp.where(even, g[own - 2 :], g[:2]), False, core)
    g_other = swap(jnp.where(even, g[:2], g[own - 2 :]), False, other)
    skip_there = swap(skip_here, True, same)
    output, grad, back, edge_core, edge_other = call(
        functools.partial(middle_kernel, segments, strips),
        [like(own, BF16), like(own + 2, BF16), like(own, BF16), like(2, BF16), like(2, BF16)],
        [wide(own + 4), wide(own + 2)],
        (skip_here, skip_there, pre1, g, g_core, g_other, second),
        work * (2 * own + 2),
    )
    back_own = swap(back, True, same)
    back_other = swap(edge_other, True, other)
    back_core = swap(edge_core, True, core)
    taps = (3, 3, channels, channels)
    kept, sent, last = call(
        functools.partial(end_kernel, segments, strips),
        [jax.ShapeDtypeStruct(taps, F32), jax.ShapeDtypeStruct(taps, BF16), wide_out(own + 2)],
        [wide(own + 4)],
        (x, g, g_core, g_other, back_own, back_core, back_other, pre1, pre2, hid, skip_there, grad, second),
        work * (3 * own + 2),
    )
    (input_grad,) = call(input_kernel, [like(own, BF16)], [], (last, main), work * own)
    chips = strips // 2
    chunk = (9 * channels // chips, channels)
    jumps = range(1, chips)
    got = swap(sent, False, core)
    mine, *sends = call(
        functools.partial(pack_kernel, strips),
        [jax.ShapeDtypeStruct(chunk, F32)] + [jax.ShapeDtypeStruct(chunk, BF16) for _ in jumps],
        [],
        (kept.reshape((chips,) + chunk), got.reshape((chips,) + chunk)),
        kept.size,
    )
    gots = [swap(send, False, lambda r, k=k: r ^ (2 * k)) for k, send in zip(jumps, sends)]
    mine = sum((got.astype(F32) for got in gots), mine).astype(BF16)
    gots = [swap(mine, False, lambda r, k=k: r ^ (2 * k)) for k in jumps]
    (mine,) = call(
        functools.partial(unpack_kernel, strips),
        [jax.ShapeDtypeStruct((chips,) + chunk, BF16)],
        [],
        (mine, *gots),
        kept.size,
    )
    mine = mine.reshape(taps)
    theirs = swap(mine, False, core)
    factor = 1.0 / math.sqrt(own * strips * columns)
    first_sum = jnp.where(even, mine, theirs).astype(F32) * factor
    second_sum = jnp.where(even, theirs, mine).astype(F32) * factor
    return (output[None], input_grad[None], first_sum[None], second_sum[None])


def solution(mesh):
    field = P("segment", "rows", None, None)
    weight = P("segment", None, None, None, None)
    return jax.shard_map(
        body,
        mesh=mesh,
        in_specs=(field, field, weight, weight),
        out_specs=(field, field, weight, weight),
        check_vma=False,
    )
```

```python
import functools
import math

import jax
import jax.numpy as jnp
from jax import lax
from jax.experimental import pallas as pl
from jax.experimental.pallas import tpu as pltpu
from jax.sharding import PartitionSpec as P

BF16 = jnp.bfloat16
F32 = jnp.float32
TAPS = [(ty, tx) for ty in range(3) for tx in range(3)]


def silu(values):
    return values * jax.nn.sigmoid(values)


def slope(values):
    gate_value = jax.nn.sigmoid(values)
    return gate_value * (1.0 + values * (1.0 - gate_value))


def place(wide, row, values):
    columns, channels = values.shape
    column = lax.broadcasted_iota(jnp.int32, (columns, channels), 0)
    left = jnp.where(column == 0, 0.0, pltpu.roll(values, 1, 0))
    right = jnp.where(column == columns - 1, 0.0, pltpu.roll(values, columns - 1, 0))
    wide[row, :, 0:channels] = left.astype(BF16)
    wide[row, :, channels : 2 * channels] = values.astype(BF16)
    wide[row, :, 2 * channels : 3 * channels] = right.astype(BF16)


def stacked(wide, start, rows):
    parts = [wide[start + ty : start + ty + rows] for ty in range(3)]
    return jnp.concatenate([part.reshape(rows * part.shape[1], part.shape[2]) for part in parts], axis=1)


def conv(wide, start, rows, kernel):
    lhs = stacked(wide, start, rows)
    out = jnp.dot(lhs, kernel[...].reshape(-1, kernel.shape[-1]), preferred_element_type=F32)
    return out.reshape(rows, -1, out.shape[-1])


def conv_back(wide, start, rows, kernel):
    lhs = stacked(wide, start, rows)
    rhs = jnp.concatenate([kernel[2 - ty, 2 - tx] for ty, tx in TAPS], axis=1)
    out = lax.dot_general(lhs, rhs, (((1,), (1,)), ((), ())), preferred_element_type=F32)
    return out.reshape(rows, -1, out.shape[-1])


def conv_weight(field, wide, start, store):
    rows, columns, channels = field.shape
    lhs = field.reshape(rows * columns, channels)
    for ty in range(3):
        rhs = wide[start + 2 - ty : start + 2 - ty + rows]
        out = lax.dot_general(
            lhs, rhs.reshape(rows * columns, -1), (((0,), (0,)), ((), ())), preferred_element_type=F32
        )
        for tx in range(3):
            store(ty, tx, out[:, (2 - tx) * channels : (3 - tx) * channels])


def here(segments):
    row = lax.axis_index("rows")
    return lax.axis_index("segment") < segments // 2, row, lax.rem(row, 2) == 0


def inside(row, strips, own, offset):
    if offset < 0:
        return row > 0
    if offset >= own:
        return row < strips - 1
    return None


def masked(values, keep):
    return values if keep is None else jnp.where(keep, values, 0.0)


def early_kernel(x, main, second, xw, mid):
    own = x.shape[0]
    for i in range(own):
        place(xw, i, x[i].astype(F32))
    mid[...] = conv(xw, 0, own - 2, main)


def front_kernel(segments, strips, xo, mid, x_core, x_other, main, second, pre1, pre2, hid, skip, xw, hw):
    encoder, row, even = here(segments)
    own = xo.shape[0]
    core_at = jnp.where(even, 2 * own, 0)
    other_at = jnp.where(even, 0, 2 * own)
    core_in = jnp.where(even, row < strips - 1, row > 0)
    other_in = jnp.where(even, row > 0, row < strips - 1)
    xw[own : 2 * own] = xo[...]
    for i in range(own):
        place(xw, core_at + i, masked(x_core[i].astype(F32), core_in))
        place(xw, other_at + i, masked(x_other[i].astype(F32), other_in))

    @pl.when(encoder)
    def _():
        above = conv(xw, 0, 4, main)
        below = conv(xw, own + 2, 4, main)
        pre1[0:2] = above[2:4]
        pre1[2:own] = mid[...]
        pre1[own : own + 2] = below[0:2]
        for i in range(own + 6):
            first = above[i] if i < 4 else below[i - own - 2] if i >= own + 2 else mid[i - 4]
            value = masked(silu(first), inside(row, strips, own, i - 3))
            place(hw, i, value)
            if 3 <= i < own + 3:
                hid[i - 3] = value.astype(BF16)
        final = conv(hw, 0, own + 4, second)
        pre2[...] = final
        for i in range(own + 4):
            skip[i] = masked(silu(final[i]), inside(row, strips, own, i - 2)).astype(BF16)

    @pl.when(jnp.logical_not(encoder))
    def _():
        pre1[0:2] = conv(xw, 2, 2, main)
        pre1[2:own] = mid[...]
        pre1[own : own + 2] = conv(xw, own + 2, 2, main)


def middle_kernel(
    segments, strips, skip_here, skip_there, pre1, g, g_core, g_other, second, out, gw, back, edge_core, edge_other, yw
):
    encoder, row, even = here(segments)
    own = g.shape[0]

    @pl.when(encoder)
    def _():
        out[...] = skip_here[2 : own + 2]

    @pl.when(jnp.logical_not(encoder))
    def _():
        for i in range(own + 4):
            place(yw, i, skip_there[i].astype(F32))
        pre = pre1[...] + conv(yw, 0, own + 4 - 2, second)
        for i in range(own + 2):
            if i == 0:
                upstream = jnp.where(even, g_other[1].astype(F32), g_core[1].astype(F32))
            elif i == own + 1:
                upstream = jnp.where(even, g_core[0].astype(F32), g_other[0].astype(F32))
            else:
                upstream = g[i - 1].astype(F32)
                out[i - 1] = silu(pre[i]).astype(BF16)
            value = masked(upstream * slope(pre[i]), inside(row, strips, own, i - 1))
            place(gw, i, value)
        back[...] = conv_back(gw, 0, own, second).astype(BF16)
        edge_core[...] = jnp.where(even, back[own - 2 : own], back[0:2])
        edge_other[...] = jnp.where(even, back[0:2], back[own - 2 : own])


def store(even, kept, sent):
    def put(ty, tx, values):
        half = values.shape[0] // 2
        kept[ty, tx] = jnp.where(even, values[:half], values[half:])
        sent[ty, tx] = jnp.where(even, values[half:], values[:half]).astype(BF16)

    return put


def second_kernel(
    segments, strips, g, g_core, g_other, back, back_core, back_other, pre2, hid, skip_there, gw, kept, sent, ew
):
    encoder, row, even = here(segments)
    own = g.shape[0]

    @pl.when(encoder)
    def _():
        for i in range(own + 4):
            if i < 2:
                upstream = jnp.where(even, g_other[i].astype(F32), g_core[i].astype(F32))
                returned = jnp.where(even, back_other[i].astype(F32), back_core[i].astype(F32))
            elif i >= own + 2:
                k = i - own - 2
                upstream = jnp.where(even, g_core[k].astype(F32), g_other[k].astype(F32))
                returned = jnp.where(even, back_core[k].astype(F32), back_other[k].astype(F32))
            else:
                upstream = g[i - 2].astype(F32)
                returned = back[i - 2].astype(F32)
            value = (upstream + returned) * slope(pre2[i])
            place(ew, i, masked(value, inside(row, strips, own, i - 2)))
        conv_weight(hid[...], ew, 1, store(even, kept, sent))

    @pl.when(jnp.logical_not(encoder))
    def _():
        conv_weight(skip_there[2 : own + 2], gw, 0, store(even, kept, sent))


def main_kernel(segments, strips, x, pre1, ew, gw, second, kept, sent, hw):
    encoder, row, even = here(segments)
    own = x.shape[0]

    @pl.when(encoder)
    def _():
        hidden_back = conv_back(ew, 0, own + 2, second)
        for i in range(own + 2):
            value = hidden_back[i] * slope(pre1[i])
            place(hw, i, masked(value, inside(row, strips, own, i - 1)))

    @pl.when(jnp.logical_not(encoder))
    def _():
        hw[...] = gw[...]

    conv_weight(x[...], hw, 0, store(even, kept, sent))


def input_kernel(hw, main, input_grad):
    input_grad[...] = conv_back(hw, 0, input_grad.shape[0], main).astype(BF16)


def call(kernel, outs, scratch, args, flops):
    moved = sum(math.prod(a.shape) * a.dtype.itemsize for a in list(args) + outs)
    return pl.pallas_call(
        kernel,
        out_shape=outs,
        in_specs=[pl.BlockSpec(memory_space=pltpu.VMEM)] * len(args),
        out_specs=[pl.BlockSpec(memory_space=pltpu.VMEM)] * len(outs),
        scratch_shapes=scratch,
        cost_estimate=pl.CostEstimate(flops=flops, bytes_accessed=moved, transcendentals=0),
        compiler_params=pltpu.CompilerParams(vmem_limit_bytes=32 * 1024 * 1024),
    )(*args)


def body(incoming, cotangent, main_weight, second_weight):
    x, g, main, second = incoming[0], cotangent[0], main_weight[0], second_weight[0]
    own, columns, channels = x.shape
    segments, strips = lax.axis_size("segment"), lax.axis_size("rows")
    half = segments // 2
    row = lax.axis_index("rows")
    even = row % 2 == 0
    everyone = [(s, r) for s in range(segments) for r in range(strips)]

    def core(r):
        return r ^ 1

    def other(r):
        neighbour = r - 1 if r % 2 == 0 else r + 1
        return neighbour if 0 <= neighbour < strips else r

    def same(r):
        return r

    def swap(array, across, to):
        pairs = [
            (s * strips + r, ((s + half) % segments if across else s) * strips + to(r)) for s, r in everyone
        ]
        return lax.ppermute(array, ("segment", "rows"), pairs)

    def like(rows, dtype):
        return jax.ShapeDtypeStruct((rows, columns, channels), dtype)

    def wide(rows):
        return pltpu.VMEM((rows, columns, 3 * channels), BF16)

    def wide_out(rows):
        return jax.ShapeDtypeStruct((rows, columns, 3 * channels), BF16)

    work = 2 * columns * 9 * channels * channels
    x_other = swap(x, False, other)
    x_core = swap(x, False, core)
    xo, mid = call(
        early_kernel,
        [wide_out(own), like(own - 2, F32)],
        [],
        (x, main, second),
        work * (own - 2),
    )
    pre1, pre2, hid, skip_here = call(
        functools.partial(front_kernel, segments, strips),
        [like(own + 2, F32), like(own + 4, F32), like(own, BF16), like(own + 4, BF16)],
        [wide(3 * own), wide(own + 6)],
        (xo, mid, x_core, x_other, main, second),
        work * (2 * own + 8),
    )
    g_core = swap(jnp.where(even, g[own - 2 :], g[:2]), False, core)
    g_other = swap(jnp.where(even, g[:2], g[own - 2 :]), False, other)
    skip_there = swap(skip_here, True, same)
    output, gw, back, edge_core, edge_other = call(
        functools.partial(middle_kernel, segments, strips),
        [like(own, BF16), wide_out(own + 2), like(own, BF16), like(2, BF16), like(2, BF16)],
        [wide(own + 4)],
        (skip_here, skip_there, pre1, g, g_core, g_other, second),
        work * (2 * own + 2),
    )
    back_own = swap(back, True, same)
    back_other = swap(edge_other, True, other)
    back_core = swap(edge_core, True, core)
    halves = (3, 3, channels // 2, channels)
    terms = [jax.ShapeDtypeStruct(halves, F32), jax.ShapeDtypeStruct(halves, BF16)]
    kept2, sent2, ew = call(
        functools.partial(second_kernel, segments, strips),
        terms + [wide_out(own + 4)],
        [],
        (g, g_core, g_other, back_own, back_core, back_other, pre2, hid, skip_there, gw),
        work * own,
    )
    kept1, sent1, hw = call(
        functools.partial(main_kernel, segments, strips),
        terms + [wide_out(own + 2)],
        [],
        (x, pre1, ew, gw, second),
        work * (2 * own + 2),
    )
    (input_grad,) = call(input_kernel, [like(own, BF16)], [], (hw, main), work * own)
    factor = 1.0 / math.sqrt(own * strips * columns)

    def jump(array, bit):
        return swap(array, False, lambda r: r ^ (1 << bit))

    def total(kept, sent):
        bits = strips.bit_length() - 1
        current = kept + jump(sent, 0).astype(F32)
        split = [0]
        for bit in range(1, bits):
            half = current.shape[2] // 2
            if half >= 16:
                upper = (row >> bit) & 1
                mine = lax.dynamic_slice_in_dim(current, upper * half, half, 2)
                sent = lax.dynamic_slice_in_dim(current, (1 - upper) * half, half, 2).astype(BF16)
                current = mine + jump(sent, bit).astype(F32)
                split.append(bit)
            else:
                mine = lax.optimization_barrier(current.astype(BF16))
                current = mine.astype(F32) + jump(mine, bit).astype(F32)
        mine = lax.optimization_barrier(current.astype(BF16))
        for bit in reversed(split):
            upper = ((row >> bit) & 1) == 1
            got = jump(mine, bit)
            mine = jnp.concatenate([jnp.where(upper, got, mine), jnp.where(upper, mine, got)], axis=2)
        return mine.astype(F32) * factor

    second_sum = total(kept2, sent2)
    first_sum = total(kept1, sent1)
    return (output[None], input_grad[None], first_sum[None], second_sum[None])


def solution(mesh):
    field = P("segment", "rows", None, None)
    weight = P("segment", None, None, None, None)
    return jax.shard_map(
        body,
        mesh=mesh,
        in_specs=(field, field, weight, weight),
        out_specs=(field, field, weight, weight),
        check_vma=False,
    )
```

```python
import functools
import math

import jax
import jax.numpy as jnp
from jax import lax
from jax.experimental import pallas as pl
from jax.experimental.pallas import tpu as pltpu
from jax.sharding import PartitionSpec as P

BF16 = jnp.bfloat16
F32 = jnp.float32
TAPS = [(ty, tx) for ty in range(3) for tx in range(3)]


def silu(values):
    return values * jax.nn.sigmoid(values)


def slope(values):
    gate_value = jax.nn.sigmoid(values)
    return gate_value * (1.0 + values * (1.0 - gate_value))


def place(wide, row, values):
    columns, channels = values.shape
    column = lax.broadcasted_iota(jnp.int32, (columns, channels), 0)
    left = jnp.where(column == 0, 0.0, pltpu.roll(values, 1, 0))
    right = jnp.where(column == columns - 1, 0.0, pltpu.roll(values, columns - 1, 0))
    wide[row, :, 0:channels] = left.astype(BF16)
    wide[row, :, channels : 2 * channels] = values.astype(BF16)
    wide[row, :, 2 * channels : 3 * channels] = right.astype(BF16)


def stacked(wide, start, rows):
    parts = [wide[start + ty : start + ty + rows] for ty in range(3)]
    return jnp.concatenate([part.reshape(rows * part.shape[1], part.shape[2]) for part in parts], axis=1)


def conv(wide, start, rows, kernel):
    lhs = stacked(wide, start, rows)
    out = jnp.dot(lhs, kernel[...].reshape(-1, kernel.shape[-1]), preferred_element_type=F32)
    return out.reshape(rows, -1, out.shape[-1])


def conv_back(wide, start, rows, kernel):
    lhs = stacked(wide, start, rows)
    rhs = jnp.concatenate([kernel[2 - ty, 2 - tx] for ty, tx in TAPS], axis=1)
    out = lax.dot_general(lhs, rhs, (((1,), (1,)), ((), ())), preferred_element_type=F32)
    return out.reshape(rows, -1, out.shape[-1])


def conv_weight(field, wide, start, store):
    rows, columns, channels = field.shape
    lhs = field.reshape(rows * columns, channels)
    for ty in range(3):
        rhs = wide[start + 2 - ty : start + 2 - ty + rows]
        out = lax.dot_general(
            lhs, rhs.reshape(rows * columns, -1), (((0,), (0,)), ((), ())), preferred_element_type=F32
        )
        for tx in range(3):
            store(ty, tx, out[:, (2 - tx) * channels : (3 - tx) * channels])


def here(segments):
    row = lax.axis_index("rows")
    return lax.axis_index("segment") < segments // 2, row, lax.rem(row, 2) == 0


def inside(row, strips, own, offset):
    if offset < 0:
        return row > 0
    if offset >= own:
        return row < strips - 1
    return None


def masked(values, keep):
    return values if keep is None else jnp.where(keep, values, 0.0)


def early_kernel(x, main, second, xw, mid):
    own = x.shape[0]
    for i in range(own):
        place(xw, i, x[i].astype(F32))
    mid[...] = conv(xw, 0, own - 2, main)


def front_kernel(segments, strips, xo, mid, x_core, x_other, main, second, pre1, pre2, hid, skip, xw, hw):
    encoder, row, even = here(segments)
    own = xo.shape[0]
    core_at = jnp.where(even, 2 * own, 0)
    other_at = jnp.where(even, 0, 2 * own)
    core_in = jnp.where(even, row < strips - 1, row > 0)
    other_in = jnp.where(even, row > 0, row < strips - 1)
    xw[own : 2 * own] = xo[...]
    for i in range(own):
        place(xw, core_at + i, masked(x_core[i].astype(F32), core_in))
        place(xw, other_at + i, masked(x_other[i].astype(F32), other_in))

    @pl.when(encoder)
    def _():
        above = conv(xw, 0, 4, main)
        below = conv(xw, own + 2, 4, main)
        pre1[0:2] = above[2:4]
        pre1[2:own] = mid[...]
        pre1[own : own + 2] = below[0:2]
        for i in range(own + 6):
            first = above[i] if i < 4 else below[i - own - 2] if i >= own + 2 else mid[i - 4]
            value = masked(silu(first), inside(row, strips, own, i - 3))
            place(hw, i, value)
            if 3 <= i < own + 3:
                hid[i - 3] = value.astype(BF16)
        final = conv(hw, 0, own + 4, second)
        pre2[...] = final
        for i in range(own + 4):
            skip[i] = masked(silu(final[i]), inside(row, strips, own, i - 2)).astype(BF16)

    @pl.when(jnp.logical_not(encoder))
    def _():
        pre1[0:2] = conv(xw, 2, 2, main)
        pre1[2:own] = mid[...]
        pre1[own : own + 2] = conv(xw, own + 2, 2, main)


def middle_kernel(
    segments, strips, skip_here, skip_there, pre1, g, g_core, g_other, second, out, gw, back, edge_core, edge_other, yw
):
    encoder, row, even = here(segments)
    own = g.shape[0]

    @pl.when(encoder)
    def _():
        out[...] = skip_here[2 : own + 2]

    @pl.when(jnp.logical_not(encoder))
    def _():
        for i in range(own + 4):
            place(yw, i, skip_there[i].astype(F32))
        pre = pre1[...] + conv(yw, 0, own + 4 - 2, second)
        for i in range(own + 2):
            if i == 0:
                upstream = jnp.where(even, g_other[1].astype(F32), g_core[1].astype(F32))
            elif i == own + 1:
                upstream = jnp.where(even, g_core[0].astype(F32), g_other[0].astype(F32))
            else:
                upstream = g[i - 1].astype(F32)
                out[i - 1] = silu(pre[i]).astype(BF16)
            value = masked(upstream * slope(pre[i]), inside(row, strips, own, i - 1))
            place(gw, i, value)
        back[...] = conv_back(gw, 0, own, second).astype(BF16)
        edge_core[...] = jnp.where(even, back[own - 2 : own], back[0:2])
        edge_other[...] = jnp.where(even, back[0:2], back[own - 2 : own])


def store(even, kept, sent):
    def put(ty, tx, values):
        half = values.shape[0] // 2
        kept[ty, tx] = jnp.where(even, values[:half], values[half:])
        sent[ty, tx] = jnp.where(even, values[half:], values[:half]).astype(BF16)

    return put


def second_kernel(
    segments, strips, g, g_core, g_other, back, back_core, back_other, pre2, hid, skip_there, gw, kept, sent, ew
):
    encoder, row, even = here(segments)
    own = g.shape[0]

    @pl.when(encoder)
    def _():
        for i in range(own + 4):
            if i < 2:
                upstream = jnp.where(even, g_other[i].astype(F32), g_core[i].astype(F32))
                returned = jnp.where(even, back_other[i].astype(F32), back_core[i].astype(F32))
            elif i >= own + 2:
                k = i - own - 2
                upstream = jnp.where(even, g_core[k].astype(F32), g_other[k].astype(F32))
                returned = jnp.where(even, back_core[k].astype(F32), back_other[k].astype(F32))
            else:
                upstream = g[i - 2].astype(F32)
                returned = back[i - 2].astype(F32)
            value = (upstream + returned) * slope(pre2[i])
            place(ew, i, masked(value, inside(row, strips, own, i - 2)))
        conv_weight(hid[...], ew, 1, store(even, kept, sent))

    @pl.when(jnp.logical_not(encoder))
    def _():
        conv_weight(skip_there[2 : own + 2], gw, 0, store(even, kept, sent))


def main_kernel(segments, strips, x, pre1, ew, gw, second, kept, sent, hw):
    encoder, row, even = here(segments)
    own = x.shape[0]

    @pl.when(encoder)
    def _():
        hidden_back = conv_back(ew, 0, own + 2, second)
        for i in range(own + 2):
            value = hidden_back[i] * slope(pre1[i])
            place(hw, i, masked(value, inside(row, strips, own, i - 1)))

    @pl.when(jnp.logical_not(encoder))
    def _():
        hw[...] = gw[...]

    conv_weight(x[...], hw, 0, store(even, kept, sent))


def input_kernel(hw, main, input_grad):
    input_grad[...] = conv_back(hw, 0, input_grad.shape[0], main).astype(BF16)


def quarters(rows):
    quad = lax.rem(lax.axis_index("rows") // 2, 4)
    return [pl.ds(pl.multiple_of(jnp.bitwise_xor(quad, k) * rows, rows), rows) for k in range(4)]


def pack_kernel(kept1, got1, kept2, got2, mine, *sends):
    for k, rows in enumerate(quarters(mine.shape[3])):
        for t, (kept, got) in enumerate(((kept1, got1), (kept2, got2))):
            value = kept[:, :, rows, :] + got[:, :, rows, :].astype(F32)
            if k == 0:
                mine[t] = value
            else:
                sends[k - 1][t] = value.astype(BF16)


def unpack_kernel(mine, *rest):
    out = rest[-1]
    for got, rows in zip((mine,) + rest[:-1], quarters(mine.shape[3])):
        out[:, :, :, rows, :] = got[...]


def last_kernel(factor, mine, theirs, *outs):
    even = lax.rem(lax.axis_index("rows"), 2) == 0
    rows = mine.shape[3]
    own_at = pl.ds(pl.multiple_of(jnp.where(even, 0, rows), rows), rows)
    their_at = pl.ds(pl.multiple_of(jnp.where(even, rows, 0), rows), rows)
    for t, out in enumerate(outs):
        out[:, :, own_at, :] = mine[t].astype(F32) * factor
        out[:, :, their_at, :] = theirs[t].astype(F32) * factor


def call(kernel, outs, scratch, args, flops):
    moved = sum(math.prod(a.shape) * a.dtype.itemsize for a in list(args) + outs)
    return pl.pallas_call(
        kernel,
        out_shape=outs,
        in_specs=[pl.BlockSpec(memory_space=pltpu.VMEM)] * len(args),
        out_specs=[pl.BlockSpec(memory_space=pltpu.VMEM)] * len(outs),
        scratch_shapes=scratch,
        cost_estimate=pl.CostEstimate(flops=flops, bytes_accessed=moved, transcendentals=0),
        compiler_params=pltpu.CompilerParams(vmem_limit_bytes=32 * 1024 * 1024),
    )(*args)


def body(incoming, cotangent, main_weight, second_weight):
    x, g, main, second = incoming[0], cotangent[0], main_weight[0], second_weight[0]
    own, columns, channels = x.shape
    segments, strips = lax.axis_size("segment"), lax.axis_size("rows")
    half = segments // 2
    row = lax.axis_index("rows")
    even = row % 2 == 0
    everyone = [(s, r) for s in range(segments) for r in range(strips)]

    def core(r):
        return r ^ 1

    def other(r):
        neighbour = r - 1 if r % 2 == 0 else r + 1
        return neighbour if 0 <= neighbour < strips else r

    def same(r):
        return r

    def swap(array, across, to):
        pairs = [
            (s * strips + r, ((s + half) % segments if across else s) * strips + to(r)) for s, r in everyone
        ]
        return lax.ppermute(array, ("segment", "rows"), pairs)

    def like(rows, dtype):
        return jax.ShapeDtypeStruct((rows, columns, channels), dtype)

    def wide(rows):
        return pltpu.VMEM((rows, columns, 3 * channels), BF16)

    def wide_out(rows):
        return jax.ShapeDtypeStruct((rows, columns, 3 * channels), BF16)

    work = 2 * columns * 9 * channels * channels
    x_other = swap(x, False, other)
    x_core = swap(x, False, core)
    xo, mid = call(
        early_kernel,
        [wide_out(own), like(own - 2, F32)],
        [],
        (x, main, second),
        work * (own - 2),
    )
    pre1, pre2, hid, skip_here = call(
        functools.partial(front_kernel, segments, strips),
        [like(own + 2, F32), like(own + 4, F32), like(own, BF16), like(own + 4, BF16)],
        [wide(3 * own), wide(own + 6)],
        (xo, mid, x_core, x_other, main, second),
        work * (2 * own + 8),
    )
    g_core = swap(jnp.where(even, g[own - 2 :], g[:2]), False, core)
    g_other = swap(jnp.where(even, g[:2], g[own - 2 :]), False, other)
    skip_there = swap(skip_here, True, same)
    output, gw, back, edge_core, edge_other = call(
        functools.partial(middle_kernel, segments, strips),
        [like(own, BF16), wide_out(own + 2), like(own, BF16), like(2, BF16), like(2, BF16)],
        [wide(own + 4)],
        (skip_here, skip_there, pre1, g, g_core, g_other, second),
        work * (2 * own + 2),
    )
    back_own = swap(back, True, same)
    back_other = swap(edge_other, True, other)
    back_core = swap(edge_core, True, core)
    taps = (3, 3, channels, channels)
    halves = (3, 3, channels // 2, channels)
    terms = [jax.ShapeDtypeStruct(halves, F32), jax.ShapeDtypeStruct(halves, BF16)]
    kept2, sent2, ew = call(
        functools.partial(second_kernel, segments, strips),
        terms + [wide_out(own + 4)],
        [],
        (g, g_core, g_other, back_own, back_core, back_other, pre2, hid, skip_there, gw),
        work * own,
    )
    kept1, sent1, hw = call(
        functools.partial(main_kernel, segments, strips),
        terms + [wide_out(own + 2)],
        [],
        (x, pre1, ew, gw, second),
        work * (2 * own + 2),
    )
    (input_grad,) = call(input_kernel, [like(own, BF16)], [], (hw, main), work * own)
    factor = 1.0 / math.sqrt(own * strips * columns)

    def jump(array, bit, times=1):
        return swap(array, False, lambda r: r ^ (times << bit))

    bits = strips.bit_length() - 1
    quarter = (2, 3, 3, channels // 8, channels)
    got2, got1 = jump(sent2, 0), jump(sent1, 0)
    mine, *sends = call(
        pack_kernel,
        [jax.ShapeDtypeStruct(quarter, F32)] + [jax.ShapeDtypeStruct(quarter, BF16)] * 3,
        [],
        (kept1, got1, kept2, got2),
        kept1.size,
    )
    for k, send in enumerate(sends):
        mine = mine + jump(send, 1, k + 1).astype(F32)
    for bit in range(3, bits):
        rounded = lax.optimization_barrier(mine.astype(BF16))
        mine = rounded.astype(F32) + jump(rounded, bit).astype(F32)
    mine = lax.optimization_barrier(mine.astype(BF16))
    gots = [jump(mine, 1, k) for k in range(1, 4)]
    (mine,) = call(
        unpack_kernel,
        [jax.ShapeDtypeStruct((2,) + halves, BF16)],
        [],
        (mine, *gots),
        kept1.size,
    )
    theirs = jump(mine, 0)
    first_sum, second_sum = call(
        functools.partial(last_kernel, factor), [jax.ShapeDtypeStruct(taps, F32)] * 2, [], (mine, theirs), kept1.size
    )
    return (output[None], input_grad[None], first_sum[None], second_sum[None])


def solution(mesh):
    field = P("segment", "rows", None, None)
    weight = P("segment", None, None, None, None)
    return jax.shard_map(
        body,
        mesh=mesh,
        in_specs=(field, field, weight, weight),
        out_specs=(field, field, weight, weight),
        check_vma=False,
    )
```

```python
import functools
import math

import jax
import jax.numpy as jnp
from jax import lax
from jax.experimental import pallas as pl
from jax.experimental.pallas import tpu as pltpu
from jax.sharding import PartitionSpec as P

BF16 = jnp.bfloat16
F32 = jnp.float32
TAPS = [(ty, tx) for ty in range(3) for tx in range(3)]


def silu(values):
    return values * jax.nn.sigmoid(values)


def slope(values):
    gate_value = jax.nn.sigmoid(values)
    return gate_value * (1.0 + values * (1.0 - gate_value))


def place(wide, row, values):
    columns, channels = values.shape
    column = lax.broadcasted_iota(jnp.int32, (columns, channels), 0)
    left = jnp.where(column == 0, 0.0, pltpu.roll(values, 1, 0))
    right = jnp.where(column == columns - 1, 0.0, pltpu.roll(values, columns - 1, 0))
    wide[row, :, 0:channels] = left.astype(BF16)
    wide[row, :, channels : 2 * channels] = values.astype(BF16)
    wide[row, :, 2 * channels : 3 * channels] = right.astype(BF16)


def stacked(wide, start, rows):
    parts = [wide[start + ty : start + ty + rows] for ty in range(3)]
    return jnp.concatenate([part.reshape(rows * part.shape[1], part.shape[2]) for part in parts], axis=1)


def conv(wide, start, rows, kernel):
    lhs = stacked(wide, start, rows)
    out = jnp.dot(lhs, kernel[...].reshape(-1, kernel.shape[-1]), preferred_element_type=F32)
    return out.reshape(rows, -1, out.shape[-1])


def conv_back(wide, start, rows, kernel):
    lhs = stacked(wide, start, rows)
    rhs = jnp.concatenate([kernel[2 - ty, 2 - tx] for ty, tx in TAPS], axis=1)
    out = lax.dot_general(lhs, rhs, (((1,), (1,)), ((), ())), preferred_element_type=F32)
    return out.reshape(rows, -1, out.shape[-1])


def conv_weight(field, wide, start, store):
    rows, columns, channels = field.shape
    lhs = field.reshape(rows * columns, channels)
    for ty in range(3):
        rhs = wide[start + 2 - ty : start + 2 - ty + rows]
        out = lax.dot_general(
            lhs, rhs.reshape(rows * columns, -1), (((0,), (0,)), ((), ())), preferred_element_type=F32
        )
        for tx in range(3):
            store(ty, tx, out[:, (2 - tx) * channels : (3 - tx) * channels])


def here(segments):
    row = lax.axis_index("rows")
    return lax.axis_index("segment") < segments // 2, row, lax.rem(row, 2) == 0


def inside(row, strips, own, offset):
    if offset < 0:
        return row > 0
    if offset >= own:
        return row < strips - 1
    return None


def masked(values, keep):
    return values if keep is None else jnp.where(keep, values, 0.0)


def early_kernel(x, main, second, xw, mid):
    own = x.shape[0]
    for i in range(own):
        place(xw, i, x[i].astype(F32))
    mid[...] = conv(xw, 0, own - 2, main)


def front_kernel(segments, strips, xo, mid, x_core, x_other, main, second, pre1, pre2, hid, skip, xw, hw):
    encoder, row, even = here(segments)
    own = xo.shape[0]
    core_at = jnp.where(even, 2 * own, 0)
    other_at = jnp.where(even, 0, 2 * own)
    core_in = jnp.where(even, row < strips - 1, row > 0)
    other_in = jnp.where(even, row > 0, row < strips - 1)
    xw[own : 2 * own] = xo[...]
    for i in range(own):
        place(xw, core_at + i, masked(x_core[i].astype(F32), core_in))
        place(xw, other_at + i, masked(x_other[i].astype(F32), other_in))

    @pl.when(encoder)
    def _():
        above = conv(xw, 0, 4, main)
        below = conv(xw, own + 2, 4, main)
        pre1[0:2] = above[2:4]
        pre1[2:own] = mid[...]
        pre1[own : own + 2] = below[0:2]
        for i in range(own + 6):
            first = above[i] if i < 4 else below[i - own - 2] if i >= own + 2 else mid[i - 4]
            value = masked(silu(first), inside(row, strips, own, i - 3))
            place(hw, i, value)
            if 3 <= i < own + 3:
                hid[i - 3] = value.astype(BF16)
        final = conv(hw, 0, own + 4, second)
        pre2[...] = final
        for i in range(own + 4):
            skip[i] = masked(silu(final[i]), inside(row, strips, own, i - 2)).astype(BF16)

    @pl.when(jnp.logical_not(encoder))
    def _():
        pre1[0:2] = conv(xw, 2, 2, main)
        pre1[2:own] = mid[...]
        pre1[own : own + 2] = conv(xw, own + 2, 2, main)


def middle_kernel(
    segments, strips, skip_here, skip_there, pre1, g, g_core, g_other, second, out, gw, back, edge_core, edge_other, yw
):
    encoder, row, even = here(segments)
    own = g.shape[0]

    @pl.when(encoder)
    def _():
        out[...] = skip_here[2 : own + 2]

    @pl.when(jnp.logical_not(encoder))
    def _():
        for i in range(own + 4):
            place(yw, i, skip_there[i].astype(F32))
        pre = pre1[...] + conv(yw, 0, own + 4 - 2, second)
        for i in range(own + 2):
            if i == 0:
                upstream = jnp.where(even, g_other[1].astype(F32), g_core[1].astype(F32))
            elif i == own + 1:
                upstream = jnp.where(even, g_core[0].astype(F32), g_other[0].astype(F32))
            else:
                upstream = g[i - 1].astype(F32)
                out[i - 1] = silu(pre[i]).astype(BF16)
            value = masked(upstream * slope(pre[i]), inside(row, strips, own, i - 1))
            place(gw, i, value)
        back[...] = conv_back(gw, 0, own, second).astype(BF16)
        edge_core[...] = jnp.where(even, back[own - 2 : own], back[0:2])
        edge_other[...] = jnp.where(even, back[0:2], back[own - 2 : own])


def store(even, kept, sent):
    def put(ty, tx, values):
        half = values.shape[0] // 2
        kept[ty, tx] = jnp.where(even, values[:half], values[half:])
        sent[ty, tx] = jnp.where(even, values[half:], values[:half]).astype(BF16)

    return put


def second_kernel(
    segments, strips, g, g_core, g_other, back, back_core, back_other, pre2, hid, skip_there, gw, kept, sent, ew
):
    encoder, row, even = here(segments)
    own = g.shape[0]

    @pl.when(encoder)
    def _():
        for i in range(own + 4):
            if i < 2:
                upstream = jnp.where(even, g_other[i].astype(F32), g_core[i].astype(F32))
                returned = jnp.where(even, back_other[i].astype(F32), back_core[i].astype(F32))
            elif i >= own + 2:
                k = i - own - 2
                upstream = jnp.where(even, g_core[k].astype(F32), g_other[k].astype(F32))
                returned = jnp.where(even, back_core[k].astype(F32), back_other[k].astype(F32))
            else:
                upstream = g[i - 2].astype(F32)
                returned = back[i - 2].astype(F32)
            value = (upstream + returned) * slope(pre2[i])
            place(ew, i, masked(value, inside(row, strips, own, i - 2)))
        conv_weight(hid[...], ew, 1, store(even, kept, sent))

    @pl.when(jnp.logical_not(encoder))
    def _():
        conv_weight(skip_there[2 : own + 2], gw, 0, store(even, kept, sent))


def main_kernel(segments, strips, x, pre1, ew, gw, second, kept, sent, hw):
    encoder, row, even = here(segments)
    own = x.shape[0]

    @pl.when(encoder)
    def _():
        hidden_back = conv_back(ew, 0, own + 2, second)
        for i in range(own + 2):
            value = hidden_back[i] * slope(pre1[i])
            place(hw, i, masked(value, inside(row, strips, own, i - 1)))

    @pl.when(jnp.logical_not(encoder))
    def _():
        hw[...] = gw[...]

    conv_weight(x[...], hw, 0, store(even, kept, sent))


def input_kernel(hw, main, input_grad):
    input_grad[...] = conv_back(hw, 0, input_grad.shape[0], main).astype(BF16)


def quarters(rows):
    quad = lax.rem(lax.axis_index("rows") // 2, 4)
    return [pl.ds(pl.multiple_of(jnp.bitwise_xor(quad, k) * rows, rows), rows) for k in range(4)]


def pack_kernel(kept1, got1, kept2, got2, mine, *sends):
    for k, rows in enumerate(quarters(mine.shape[3])):
        for t, (kept, got) in enumerate(((kept1, got1), (kept2, got2))):
            value = kept[:, :, rows, :] + got[:, :, rows, :].astype(F32)
            if k == 0:
                mine[t] = value
            else:
                sends[k - 1][t] = value.astype(BF16)


def unpack_kernel(mine, *rest):
    out = rest[-1]
    for got, rows in zip((mine,) + rest[:-1], quarters(mine.shape[3])):
        out[:, :, :, rows, :] = got[...]


def last_kernel(factor, mine, theirs, *outs):
    even = lax.rem(lax.axis_index("rows"), 2) == 0
    rows = mine.shape[3]
    own_at = pl.ds(pl.multiple_of(jnp.where(even, 0, rows), rows), rows)
    their_at = pl.ds(pl.multiple_of(jnp.where(even, rows, 0), rows), rows)
    for t, out in enumerate(outs):
        out[:, :, own_at, :] = mine[t].astype(F32) * factor
        out[:, :, their_at, :] = theirs[t].astype(F32) * factor


def call(kernel, outs, scratch, args, flops):
    moved = sum(math.prod(a.shape) * a.dtype.itemsize for a in list(args) + outs)
    return pl.pallas_call(
        kernel,
        out_shape=outs,
        in_specs=[pl.BlockSpec(memory_space=pltpu.VMEM)] * len(args),
        out_specs=[pl.BlockSpec(memory_space=pltpu.VMEM)] * len(outs),
        scratch_shapes=scratch,
        cost_estimate=pl.CostEstimate(flops=flops, bytes_accessed=moved, transcendentals=0),
        compiler_params=pltpu.CompilerParams(vmem_limit_bytes=32 * 1024 * 1024),
    )(*args)


def body(incoming, cotangent, main_weight, second_weight):
    x, g, main, second = incoming[0], cotangent[0], main_weight[0], second_weight[0]
    own, columns, channels = x.shape
    segments, strips = lax.axis_size("segment"), lax.axis_size("rows")
    half = segments // 2
    row = lax.axis_index("rows")
    even = row % 2 == 0
    everyone = [(s, r) for s in range(segments) for r in range(strips)]

    def core(r):
        return r ^ 1

    def other(r):
        neighbour = r - 1 if r % 2 == 0 else r + 1
        return neighbour if 0 <= neighbour < strips else r

    def same(r):
        return r

    def swap(array, to):
        pairs = [(s * strips + r, s * strips + to(r)) for s, r in everyone]
        return lax.ppermute(array, ("segment", "rows"), pairs)

    def down(array):
        pairs = [(s * strips + r, (s + half) * strips + r) for s, r in everyone if s < half]
        return lax.ppermute(array, ("segment", "rows"), pairs)

    def up(array, to):
        pairs = [(s * strips + r, (s - half) * strips + to(r)) for s, r in everyone if s >= half]
        return lax.ppermute(array, ("segment", "rows"), pairs)

    def like(rows, dtype):
        return jax.ShapeDtypeStruct((rows, columns, channels), dtype)

    def wide(rows):
        return pltpu.VMEM((rows, columns, 3 * channels), BF16)

    def wide_out(rows):
        return jax.ShapeDtypeStruct((rows, columns, 3 * channels), BF16)

    work = 2 * columns * 9 * channels * channels
    x_other = swap(x, other)
    x_core = swap(x, core)
    xo, mid = call(
        early_kernel,
        [wide_out(own), like(own - 2, F32)],
        [],
        (x, main, second),
        work * (own - 2),
    )
    pre1, pre2, hid, skip_here = call(
        functools.partial(front_kernel, segments, strips),
        [like(own + 2, F32), like(own + 4, F32), like(own, BF16), like(own + 4, BF16)],
        [wide(3 * own), wide(own + 6)],
        (xo, mid, x_core, x_other, main, second),
        work * (2 * own + 8),
    )
    g_core = swap(jnp.where(even, g[own - 2 :], g[:2]), core)
    g_other = swap(jnp.where(even, g[:2], g[own - 2 :]), other)
    skip_there = down(skip_here)
    output, gw, back, edge_core, edge_other = call(
        functools.partial(middle_kernel, segments, strips),
        [like(own, BF16), wide_out(own + 2), like(own, BF16), like(2, BF16), like(2, BF16)],
        [wide(own + 4)],
        (skip_here, skip_there, pre1, g, g_core, g_other, second),
        work * (2 * own + 2),
    )
    back_own = up(back, same)
    back_other = up(edge_other, other)
    back_core = up(edge_core, core)
    taps = (3, 3, channels, channels)
    halves = (3, 3, channels // 2, channels)
    terms = [jax.ShapeDtypeStruct(halves, F32), jax.ShapeDtypeStruct(halves, BF16)]
    kept2, sent2, ew = call(
        functools.partial(second_kernel, segments, strips),
        terms + [wide_out(own + 4)],
        [],
        (g, g_core, g_other, back_own, back_core, back_other, pre2, hid, skip_there, gw),
        work * own,
    )
    kept1, sent1, hw = call(
        functools.partial(main_kernel, segments, strips),
        terms + [wide_out(own + 2)],
        [],
        (x, pre1, ew, gw, second),
        work * (2 * own + 2),
    )
    (input_grad,) = call(input_kernel, [like(own, BF16)], [], (hw, main), work * own)
    factor = 1.0 / math.sqrt(own * strips * columns)

    def jump(array, bit, times=1):
        return swap(array, lambda r: r ^ (times << bit))

    bits = strips.bit_length() - 1
    quarter = (2, 3, 3, channels // 8, channels)
    got2, got1 = jump(sent2, 0), jump(sent1, 0)
    mine, *sends = call(
        pack_kernel,
        [jax.ShapeDtypeStruct(quarter, F32)] + [jax.ShapeDtypeStruct(quarter, BF16)] * 3,
        [],
        (kept1, got1, kept2, got2),
        kept1.size,
    )
    for k, send in enumerate(sends):
        mine = mine + jump(send, 1, k + 1).astype(F32)
    for bit in range(3, bits):
        rounded = lax.optimization_barrier(mine.astype(BF16))
        mine = rounded.astype(F32) + jump(rounded, bit).astype(F32)
    mine = lax.optimization_barrier(mine.astype(BF16))
    gots = [jump(mine, 1, k) for k in range(1, 4)]
    (mine,) = call(
        unpack_kernel,
        [jax.ShapeDtypeStruct((2,) + halves, BF16)],
        [],
        (mine, *gots),
        kept1.size,
    )
    theirs = jump(mine, 0)
    first_sum, second_sum = call(
        functools.partial(last_kernel, factor), [jax.ShapeDtypeStruct(taps, F32)] * 2, [], (mine, theirs), kept1.size
    )
    return (output[None], input_grad[None], first_sum[None], second_sum[None])


def solution(mesh):
    field = P("segment", "rows", None, None)
    weight = P("segment", None, None, None, None)
    return jax.shard_map(
        body,
        mesh=mesh,
        in_specs=(field, field, weight, weight),
        out_specs=(field, field, weight, weight),
        check_vma=False,
    )
```

```python
import functools
import math

import jax
import jax.numpy as jnp
from jax import lax
from jax.experimental import pallas as pl
from jax.experimental.pallas import tpu as pltpu
from jax.sharding import PartitionSpec as P

BF16 = jnp.bfloat16
F32 = jnp.float32
TAPS = [(ty, tx) for ty in range(3) for tx in range(3)]


TURNS = ((1, 2), (2, 1), (3, 3))


def silu(values):
    return values * jax.nn.sigmoid(values)


def slope(values):
    gate_value = jax.nn.sigmoid(values)
    return gate_value * (1.0 + values * (1.0 - gate_value))


def place(wide, row, values):
    columns, channels = values.shape
    column = lax.broadcasted_iota(jnp.int32, (columns, channels), 0)
    left = jnp.where(column == 0, 0.0, pltpu.roll(values, 1, 0))
    right = jnp.where(column == columns - 1, 0.0, pltpu.roll(values, columns - 1, 0))
    wide[row, :, 0:channels] = left.astype(BF16)
    wide[row, :, channels : 2 * channels] = values.astype(BF16)
    wide[row, :, 2 * channels : 3 * channels] = right.astype(BF16)


def stacked(wide, start, rows):
    parts = [wide[start + ty : start + ty + rows] for ty in range(3)]
    return jnp.concatenate([part.reshape(rows * part.shape[1], part.shape[2]) for part in parts], axis=1)


def conv(wide, start, rows, kernel):
    lhs = stacked(wide, start, rows)
    out = jnp.dot(lhs, kernel[...].reshape(-1, kernel.shape[-1]), preferred_element_type=F32)
    return out.reshape(rows, -1, out.shape[-1])


def conv_back(wide, start, rows, kernel):
    lhs = stacked(wide, start, rows)
    rhs = jnp.concatenate([kernel[2 - ty, 2 - tx] for ty, tx in TAPS], axis=1)
    out = lax.dot_general(lhs, rhs, (((1,), (1,)), ((), ())), preferred_element_type=F32)
    return out.reshape(rows, -1, out.shape[-1])


def conv_weight(field, wide, start, store):
    rows, columns, channels = field.shape
    lhs = field.reshape(rows * columns, channels)
    for ty in range(3):
        rhs = wide[start + 2 - ty : start + 2 - ty + rows]
        out = lax.dot_general(
            lhs, rhs.reshape(rows * columns, -1), (((0,), (0,)), ((), ())), preferred_element_type=F32
        )
        for tx in range(3):
            store(ty, tx, out[:, (2 - tx) * channels : (3 - tx) * channels])


def here(segments):
    row = lax.axis_index("rows")
    return lax.axis_index("segment") < segments // 2, row, lax.rem(row, 2) == 0


def inside(row, strips, own, offset):
    if offset < 0:
        return row > 0
    if offset >= own:
        return row < strips - 1
    return None


def masked(values, keep):
    return values if keep is None else jnp.where(keep, values, 0.0)


def early_kernel(x, main, second, xw, mid):
    own = x.shape[0]
    for i in range(own):
        place(xw, i, x[i].astype(F32))
    mid[...] = conv(xw, 0, own - 2, main)


def front_kernel(segments, strips, xo, mid, x_core, x_other, main, second, pre1, pre2, hid, skip, xw, hw):
    encoder, row, even = here(segments)
    own = xo.shape[0]
    core_at = jnp.where(even, 2 * own, 0)
    other_at = jnp.where(even, 0, 2 * own)
    core_in = jnp.where(even, row < strips - 1, row > 0)
    other_in = jnp.where(even, row > 0, row < strips - 1)
    xw[own : 2 * own] = xo[...]
    for i in range(own):
        place(xw, core_at + i, masked(x_core[i].astype(F32), core_in))
        place(xw, other_at + i, masked(x_other[i].astype(F32), other_in))

    @pl.when(encoder)
    def _():
        above = conv(xw, 0, 4, main)
        below = conv(xw, own + 2, 4, main)
        pre1[0:2] = above[2:4]
        pre1[2:own] = mid[...]
        pre1[own : own + 2] = below[0:2]
        for i in range(own + 6):
            first = above[i] if i < 4 else below[i - own - 2] if i >= own + 2 else mid[i - 4]
            value = masked(silu(first), inside(row, strips, own, i - 3))
            place(hw, i, value)
            if 3 <= i < own + 3:
                hid[i - 3] = value.astype(BF16)
        final = conv(hw, 0, own + 4, second)
        pre2[...] = final
        for i in range(own + 4):
            skip[i] = masked(silu(final[i]), inside(row, strips, own, i - 2)).astype(BF16)

    @pl.when(jnp.logical_not(encoder))
    def _():
        pre1[0:2] = conv(xw, 2, 2, main)
        pre1[2:own] = mid[...]
        pre1[own : own + 2] = conv(xw, own + 2, 2, main)


def middle_kernel(
    segments, strips, skip_here, skip_there, pre1, g, g_core, g_other, second, out, gw, back, edge_core, edge_other, yw
):
    encoder, row, even = here(segments)
    own = g.shape[0]

    @pl.when(encoder)
    def _():
        out[...] = skip_here[2 : own + 2]

    @pl.when(jnp.logical_not(encoder))
    def _():
        for i in range(own + 4):
            place(yw, i, skip_there[i].astype(F32))
        pre = pre1[...] + conv(yw, 0, own + 4 - 2, second)
        for i in range(own + 2):
            if i == 0:
                upstream = jnp.where(even, g_other[own - 1].astype(F32), g_core[own - 1].astype(F32))
            elif i == own + 1:
                upstream = jnp.where(even, g_core[0].astype(F32), g_other[0].astype(F32))
            else:
                upstream = g[i - 1].astype(F32)
                out[i - 1] = silu(pre[i]).astype(BF16)
            value = masked(upstream * slope(pre[i]), inside(row, strips, own, i - 1))
            place(gw, i, value)
        back[...] = conv_back(gw, 0, own, second).astype(BF16)
        edge_core[...] = jnp.where(even, back[own - 2 : own], back[0:2])
        edge_other[...] = jnp.where(even, back[0:2], back[own - 2 : own])


def store(even, kept, sent):
    def put(ty, tx, values):
        half = values.shape[0] // 2
        kept[ty, tx] = jnp.where(even, values[:half], values[half:])
        sent[ty, tx] = jnp.where(even, values[half:], values[:half]).astype(BF16)

    return put


def second_kernel(
    segments, strips, g, g_core, g_other, back, back_core, back_other, pre2, hid, skip_there, gw, kept, sent, ew
):
    encoder, row, even = here(segments)
    own = g.shape[0]

    @pl.when(encoder)
    def _():
        for i in range(own + 4):
            if i < 2:
                upstream = jnp.where(even, g_other[own - 2 + i].astype(F32), g_core[own - 2 + i].astype(F32))
                returned = jnp.where(even, back_other[i].astype(F32), back_core[i].astype(F32))
            elif i >= own + 2:
                k = i - own - 2
                upstream = jnp.where(even, g_core[k].astype(F32), g_other[k].astype(F32))
                returned = jnp.where(even, back_core[k].astype(F32), back_other[k].astype(F32))
            else:
                upstream = g[i - 2].astype(F32)
                returned = back[i - 2].astype(F32)
            value = (upstream + returned) * slope(pre2[i])
            place(ew, i, masked(value, inside(row, strips, own, i - 2)))
        conv_weight(hid[...], ew, 1, store(even, kept, sent))

    @pl.when(jnp.logical_not(encoder))
    def _():
        conv_weight(skip_there[2 : own + 2], gw, 0, store(even, kept, sent))


def main_kernel(segments, strips, x, pre1, ew, gw, second, kept, sent, hw):
    encoder, row, even = here(segments)
    own = x.shape[0]

    @pl.when(encoder)
    def _():
        hidden_back = conv_back(ew, 0, own + 2, second)
        for i in range(own + 2):
            value = hidden_back[i] * slope(pre1[i])
            place(hw, i, masked(value, inside(row, strips, own, i - 1)))

    @pl.when(jnp.logical_not(encoder))
    def _():
        hw[...] = gw[...]

    conv_weight(x[...], hw, 0, store(even, kept, sent))


def input_kernel(hw, main, out, input_grad, output):
    output[...] = out[...]
    input_grad[...] = conv_back(hw, 0, input_grad.shape[0], main).astype(BF16)


def quarters(rows):
    at = lax.axis_index("rows")
    quad = lax.rem(at // 2, 4)
    partners = [jnp.bitwise_xor(quad, jnp.where(lax.rem(at, 2) == 0, *turn)) for turn in TURNS]
    return [pl.ds(pl.multiple_of(partner * rows, rows), rows) for partner in [quad] + partners]


def pack_kernel(kept1, got1, kept2, got2, mine, *sends):
    for k, rows in enumerate(quarters(mine.shape[3])):
        for t, (kept, got) in enumerate(((kept1, got1), (kept2, got2))):
            value = kept[:, :, rows, :] + got[:, :, rows, :].astype(F32)
            if k == 0:
                mine[t] = value
            else:
                sends[k - 1][t] = value.astype(BF16)


def unpack_kernel(mine, *rest):
    out = rest[-1]
    for got, rows in zip((mine,) + rest[:-1], quarters(mine.shape[3])):
        out[:, :, :, rows, :] = got[...]


def last_kernel(factor, mine, theirs, *outs):
    even = lax.rem(lax.axis_index("rows"), 2) == 0
    rows = mine.shape[3]
    own_at = pl.ds(pl.multiple_of(jnp.where(even, 0, rows), rows), rows)
    their_at = pl.ds(pl.multiple_of(jnp.where(even, rows, 0), rows), rows)
    for t, out in enumerate(outs):
        out[:, :, own_at, :] = mine[t].astype(F32) * factor
        out[:, :, their_at, :] = theirs[t].astype(F32) * factor


def call(kernel, outs, scratch, args, flops):
    moved = sum(math.prod(a.shape) * a.dtype.itemsize for a in list(args) + outs)
    return pl.pallas_call(
        kernel,
        out_shape=outs,
        in_specs=[pl.BlockSpec(memory_space=pltpu.VMEM)] * len(args),
        out_specs=[pl.BlockSpec(memory_space=pltpu.VMEM)] * len(outs),
        scratch_shapes=scratch,
        cost_estimate=pl.CostEstimate(flops=flops, bytes_accessed=moved, transcendentals=0),
        compiler_params=pltpu.CompilerParams(vmem_limit_bytes=32 * 1024 * 1024),
    )(*args)


def body(incoming, cotangent, main_weight, second_weight):
    x, g, main, second = incoming[0], cotangent[0], main_weight[0], second_weight[0]
    own, columns, channels = x.shape
    segments, strips = lax.axis_size("segment"), lax.axis_size("rows")
    half = segments // 2
    row = lax.axis_index("rows")
    even = row % 2 == 0
    everyone = [(s, r) for s in range(segments) for r in range(strips)]

    def core(r):
        return r ^ 1

    def other(r):
        neighbour = r - 1 if r % 2 == 0 else r + 1
        return neighbour if 0 <= neighbour < strips else r

    def same(r):
        return r

    def swap(array, across, to):
        pairs = [
            (s * strips + r, ((s + half) % segments if across else s) * strips + to(r)) for s, r in everyone
        ]
        return lax.ppermute(array, ("segment", "rows"), pairs)

    def like(rows, dtype):
        return jax.ShapeDtypeStruct((rows, columns, channels), dtype)

    def wide(rows):
        return pltpu.VMEM((rows, columns, 3 * channels), BF16)

    def wide_out(rows):
        return jax.ShapeDtypeStruct((rows, columns, 3 * channels), BF16)

    work = 2 * columns * 9 * channels * channels
    x_other = swap(x, False, other)
    x_core = swap(x, False, core)
    g_other = swap(g, False, other)
    g_core = swap(g, False, core)
    xo, mid = call(
        early_kernel,
        [wide_out(own), like(own - 2, F32)],
        [],
        (x, main, second),
        work * (own - 2),
    )
    pre1, pre2, hid, skip_here = call(
        functools.partial(front_kernel, segments, strips),
        [like(own + 2, F32), like(own + 4, F32), like(own, BF16), like(own + 4, BF16)],
        [wide(3 * own), wide(own + 6)],
        (xo, mid, x_core, x_other, main, second),
        work * (2 * own + 8),
    )
    skip_here, g_core, g_other = lax.optimization_barrier((skip_here, g_core, g_other))
    skip_there = swap(skip_here, True, same)
    out, gw, back, edge_core, edge_other = call(
        functools.partial(middle_kernel, segments, strips),
        [like(own, BF16), wide_out(own + 2), like(own, BF16), like(2, BF16), like(2, BF16)],
        [wide(own + 4)],
        (skip_here, skip_there, pre1, g, g_core, g_other, second),
        work * (2 * own + 2),
    )
    back_own = swap(back, True, same)
    back_other = swap(edge_other, True, other)
    back_core = swap(edge_core, True, core)
    taps = (3, 3, channels, channels)
    halves = (3, 3, channels // 2, channels)
    terms = [jax.ShapeDtypeStruct(halves, F32), jax.ShapeDtypeStruct(halves, BF16)]
    kept2, sent2, ew = call(
        functools.partial(second_kernel, segments, strips),
        terms + [wide_out(own + 4)],
        [],
        (g, g_core, g_other, back_own, back_core, back_other, pre2, hid, skip_there, gw),
        work * own,
    )
    kept1, sent1, hw = call(
        functools.partial(main_kernel, segments, strips),
        terms + [wide_out(own + 2)],
        [],
        (x, pre1, ew, gw, second),
        work * (2 * own + 2),
    )
    input_grad, output = call(input_kernel, [like(own, BF16)] * 2, [], (hw, main, out), work * own)
    factor = 1.0 / math.sqrt(own * strips * columns)

    def jump(array, bit):
        return swap(array, False, lambda r: r ^ (1 << bit))

    def meet(array, turn):
        return swap(array, False, lambda r: r ^ (turn[r % 2] << 1))

    bits = strips.bit_length() - 1
    quarter = (2, 3, 3, channels // 8, channels)
    got2, got1 = jump(sent2, 0), jump(sent1, 0)
    mine, *sends = call(
        pack_kernel,
        [jax.ShapeDtypeStruct(quarter, F32)] + [jax.ShapeDtypeStruct(quarter, BF16)] * 3,
        [],
        (kept1, got1, kept2, got2),
        kept1.size,
    )
    for turn, send in zip(TURNS, sends):
        mine = mine + meet(send, turn).astype(F32)
    for bit in range(3, bits):
        rounded = lax.optimization_barrier(mine.astype(BF16))
        mine = rounded.astype(F32) + jump(rounded, bit).astype(F32)
    mine = lax.optimization_barrier(mine.astype(BF16))
    gots = [meet(mine, turn) for turn in TURNS]
    (mine,) = call(
        unpack_kernel,
        [jax.ShapeDtypeStruct((2,) + halves, BF16)],
        [],
        (mine, *gots),
        kept1.size,
    )
    theirs = jump(mine, 0)
    first_sum, second_sum = call(
        functools.partial(last_kernel, factor), [jax.ShapeDtypeStruct(taps, F32)] * 2, [], (mine, theirs), kept1.size
    )
    return (output[None], input_grad[None], first_sum[None], second_sum[None])


def solution(mesh):
    field = P("segment", "rows", None, None)
    weight = P("segment", None, None, None, None)
    return jax.shard_map(
        body,
        mesh=mesh,
        in_specs=(field, field, weight, weight),
        out_specs=(field, field, weight, weight),
        check_vma=False,
    )
```

```python
import functools
import math

import jax
import jax.numpy as jnp
from jax import lax
from jax.experimental import pallas as pl
from jax.experimental.pallas import tpu as pltpu
from jax.sharding import PartitionSpec as P

BF16 = jnp.bfloat16
F32 = jnp.float32
TAPS = [(ty, tx) for ty in range(3) for tx in range(3)]


TURNS = ((1, 2), (2, 1), (3, 3))


def silu(values):
    return values * jax.nn.sigmoid(values)


def slope(values):
    gate_value = jax.nn.sigmoid(values)
    return gate_value * (1.0 + values * (1.0 - gate_value))


def place(wide, row, values):
    columns, channels = values.shape
    column = lax.broadcasted_iota(jnp.int32, (columns, channels), 0)
    left = jnp.where(column == 0, 0.0, pltpu.roll(values, 1, 0))
    right = jnp.where(column == columns - 1, 0.0, pltpu.roll(values, columns - 1, 0))
    wide[row, :, 0:channels] = left.astype(BF16)
    wide[row, :, channels : 2 * channels] = values.astype(BF16)
    wide[row, :, 2 * channels : 3 * channels] = right.astype(BF16)


def stacked(wide, start, rows):
    parts = [wide[start + ty : start + ty + rows] for ty in range(3)]
    return jnp.concatenate([part.reshape(rows * part.shape[1], part.shape[2]) for part in parts], axis=1)


def conv(wide, start, rows, kernel):
    lhs = stacked(wide, start, rows)
    out = jnp.dot(lhs, kernel[...].reshape(-1, kernel.shape[-1]), preferred_element_type=F32)
    return out.reshape(rows, -1, out.shape[-1])


def conv_back(wide, start, rows, kernel):
    lhs = stacked(wide, start, rows)
    rhs = jnp.concatenate([kernel[2 - ty, 2 - tx] for ty, tx in TAPS], axis=1)
    out = lax.dot_general(lhs, rhs, (((1,), (1,)), ((), ())), preferred_element_type=F32)
    return out.reshape(rows, -1, out.shape[-1])


def conv_weight(field, wide, start, store):
    rows, columns, channels = field.shape
    lhs = field.reshape(rows * columns, channels)
    for ty in range(3):
        rhs = wide[start + 2 - ty : start + 2 - ty + rows]
        out = lax.dot_general(
            lhs, rhs.reshape(rows * columns, -1), (((0,), (0,)), ((), ())), preferred_element_type=F32
        )
        for tx in range(3):
            store(ty, tx, out[:, (2 - tx) * channels : (3 - tx) * channels])


def here(segments):
    row = lax.axis_index("rows")
    return lax.axis_index("segment") < segments // 2, row, lax.rem(row, 2) == 0


def inside(row, strips, own, offset):
    if offset < 0:
        return row > 0
    if offset >= own:
        return row < strips - 1
    return None


def masked(values, keep):
    return values if keep is None else jnp.where(keep, values, 0.0)


def first_kernel(token):
    token[...] = jnp.zeros_like(token)


def early_kernel(token, x, main, second, xw, mid):
    own = x.shape[0]
    for i in range(own):
        place(xw, i, x[i].astype(F32))
    mid[...] = conv(xw, 0, own - 2, main)


def front_kernel(segments, strips, xo, mid, x_core, x_other, main, second, pre1, pre2, hid, skip, xw, hw):
    encoder, row, even = here(segments)
    own = xo.shape[0]
    core_at = jnp.where(even, 2 * own, 0)
    other_at = jnp.where(even, 0, 2 * own)
    core_in = jnp.where(even, row < strips - 1, row > 0)
    other_in = jnp.where(even, row > 0, row < strips - 1)
    xw[own : 2 * own] = xo[...]
    for i in range(own):
        place(xw, core_at + i, masked(x_core[i].astype(F32), core_in))
        place(xw, other_at + i, masked(x_other[i].astype(F32), other_in))

    @pl.when(encoder)
    def _():
        above = conv(xw, 0, 4, main)
        below = conv(xw, own + 2, 4, main)
        pre1[0:2] = above[2:4]
        pre1[2:own] = mid[...]
        pre1[own : own + 2] = below[0:2]
        for i in range(own + 6):
            first = above[i] if i < 4 else below[i - own - 2] if i >= own + 2 else mid[i - 4]
            value = masked(silu(first), inside(row, strips, own, i - 3))
            place(hw, i, value)
            if 3 <= i < own + 3:
                hid[i - 3] = value.astype(BF16)
        final = conv(hw, 0, own + 4, second)
        pre2[...] = final
        for i in range(own + 4):
            skip[i] = masked(silu(final[i]), inside(row, strips, own, i - 2)).astype(BF16)

    @pl.when(jnp.logical_not(encoder))
    def _():
        pre1[0:2] = conv(xw, 2, 2, main)
        pre1[2:own] = mid[...]
        pre1[own : own + 2] = conv(xw, own + 2, 2, main)


def middle_kernel(
    segments, strips, skip_here, skip_there, pre1, g, g_core, g_other, second, out, gw, back, edge_core, edge_other, yw
):
    encoder, row, even = here(segments)
    own = g.shape[0]

    @pl.when(encoder)
    def _():
        out[...] = skip_here[2 : own + 2]

    @pl.when(jnp.logical_not(encoder))
    def _():
        for i in range(own + 4):
            place(yw, i, skip_there[i].astype(F32))
        pre = pre1[...] + conv(yw, 0, own + 4 - 2, second)
        for i in range(own + 2):
            if i == 0:
                upstream = jnp.where(even, g_other[1].astype(F32), g_core[own - 1].astype(F32))
            elif i == own + 1:
                upstream = jnp.where(even, g_core[0].astype(F32), g_other[0].astype(F32))
            else:
                upstream = g[i - 1].astype(F32)
                out[i - 1] = silu(pre[i]).astype(BF16)
            value = masked(upstream * slope(pre[i]), inside(row, strips, own, i - 1))
            place(gw, i, value)
        back[...] = conv_back(gw, 0, own, second).astype(BF16)
        edge_core[...] = jnp.where(even, back[own - 2 : own], back[0:2])
        edge_other[...] = jnp.where(even, back[0:2], back[own - 2 : own])


def store(even, kept, sent):
    def put(ty, tx, values):
        half = values.shape[0] // 2
        kept[ty, tx] = jnp.where(even, values[:half], values[half:])
        sent[ty, tx] = jnp.where(even, values[half:], values[:half]).astype(BF16)

    return put


def second_kernel(
    segments, strips, g, g_core, g_other, back, back_core, back_other, pre2, hid, skip_there, gw, kept, sent, ew
):
    encoder, row, even = here(segments)
    own = g.shape[0]

    @pl.when(encoder)
    def _():
        for i in range(own + 4):
            if i < 2:
                upstream = jnp.where(even, g_other[i].astype(F32), g_core[own - 2 + i].astype(F32))
                returned = jnp.where(even, back_other[i].astype(F32), back_core[i].astype(F32))
            elif i >= own + 2:
                k = i - own - 2
                upstream = jnp.where(even, g_core[k].astype(F32), g_other[k].astype(F32))
                returned = jnp.where(even, back_core[k].astype(F32), back_other[k].astype(F32))
            else:
                upstream = g[i - 2].astype(F32)
                returned = back[i - 2].astype(F32)
            value = (upstream + returned) * slope(pre2[i])
            place(ew, i, masked(value, inside(row, strips, own, i - 2)))
        conv_weight(hid[...], ew, 1, store(even, kept, sent))

    @pl.when(jnp.logical_not(encoder))
    def _():
        conv_weight(skip_there[2 : own + 2], gw, 0, store(even, kept, sent))


def main_kernel(segments, strips, x, pre1, ew, gw, second, kept, sent, hw):
    encoder, row, even = here(segments)
    own = x.shape[0]

    @pl.when(encoder)
    def _():
        hidden_back = conv_back(ew, 0, own + 2, second)
        for i in range(own + 2):
            value = hidden_back[i] * slope(pre1[i])
            place(hw, i, masked(value, inside(row, strips, own, i - 1)))

    @pl.when(jnp.logical_not(encoder))
    def _():
        hw[...] = gw[...]

    conv_weight(x[...], hw, 0, store(even, kept, sent))


def input_kernel(hw, main, out, input_grad, output):
    output[...] = out[...]
    input_grad[...] = conv_back(hw, 0, input_grad.shape[0], main).astype(BF16)


def quarters(rows):
    at = lax.axis_index("rows")
    quad = lax.rem(at // 2, 4)
    partners = [jnp.bitwise_xor(quad, jnp.where(lax.rem(at, 2) == 0, *turn)) for turn in TURNS]
    return [pl.ds(pl.multiple_of(partner * rows, rows), rows) for partner in [quad] + partners]


def pack_kernel(kept1, got1, kept2, got2, mine, *sends):
    for k, rows in enumerate(quarters(mine.shape[3])):
        for t, (kept, got) in enumerate(((kept1, got1), (kept2, got2))):
            value = kept[:, :, rows, :] + got[:, :, rows, :].astype(F32)
            if k == 0:
                mine[t] = value
            else:
                sends[k - 1][t] = value.astype(BF16)


def unpack_kernel(mine, *rest):
    out = rest[-1]
    for got, rows in zip((mine,) + rest[:-1], quarters(mine.shape[3])):
        out[:, :, :, rows, :] = got[...]


def last_kernel(factor, mine, theirs, *outs):
    even = lax.rem(lax.axis_index("rows"), 2) == 0
    rows = mine.shape[3]
    own_at = pl.ds(pl.multiple_of(jnp.where(even, 0, rows), rows), rows)
    their_at = pl.ds(pl.multiple_of(jnp.where(even, rows, 0), rows), rows)
    for t, out in enumerate(outs):
        out[:, :, own_at, :] = mine[t].astype(F32) * factor
        out[:, :, their_at, :] = theirs[t].astype(F32) * factor


def call(kernel, outs, scratch, args, flops):
    moved = sum(math.prod(a.shape) * a.dtype.itemsize for a in list(args) + outs)
    return pl.pallas_call(
        kernel,
        out_shape=outs,
        in_specs=[pl.BlockSpec(memory_space=pltpu.VMEM)] * len(args),
        out_specs=[pl.BlockSpec(memory_space=pltpu.VMEM)] * len(outs),
        scratch_shapes=scratch,
        cost_estimate=pl.CostEstimate(flops=flops, bytes_accessed=moved, transcendentals=0),
        compiler_params=pltpu.CompilerParams(vmem_limit_bytes=32 * 1024 * 1024),
    )(*args)


def body(incoming, cotangent, main_weight, second_weight):
    x, g, main, second = incoming[0], cotangent[0], main_weight[0], second_weight[0]
    own, columns, channels = x.shape
    segments, strips = lax.axis_size("segment"), lax.axis_size("rows")
    half = segments // 2
    row = lax.axis_index("rows")
    even = row % 2 == 0
    everyone = [(s, r) for s in range(segments) for r in range(strips)]

    def core(r):
        return r ^ 1

    def other(r):
        neighbour = r - 1 if r % 2 == 0 else r + 1
        return neighbour if 0 <= neighbour < strips else r

    def far(r):
        return other(core(r))

    def same(r):
        return r

    def swap(array, across, to):
        pairs = [
            (s * strips + r, ((s + half) % segments if across else s) * strips + to(r)) for s, r in everyone
        ]
        return lax.ppermute(array, ("segment", "rows"), pairs)

    def like(rows, dtype):
        return jax.ShapeDtypeStruct((rows, columns, channels), dtype)

    def wide(rows):
        return pltpu.VMEM((rows, columns, 3 * channels), BF16)

    def wide_out(rows):
        return jax.ShapeDtypeStruct((rows, columns, 3 * channels), BF16)

    work = 2 * columns * 9 * channels * channels
    (token,) = call(first_kernel, [jax.ShapeDtypeStruct((8, 128), F32)], [], (), 5 * 10**9)
    x_core = swap(x, False, core)
    g_core = swap(g, False, core)
    x_core, token = lax.optimization_barrier((x_core, token))
    x_other = swap(x_core, False, far)
    g_other = swap(jnp.where(even, g_core[own - 2 :], g_core[:2]), False, far)
    xo, mid = call(
        early_kernel,
        [wide_out(own), like(own - 2, F32)],
        [],
        (token, x, main, second),
        work * (own - 2),
    )
    pre1, pre2, hid, skip_here = call(
        functools.partial(front_kernel, segments, strips),
        [like(own + 2, F32), like(own + 4, F32), like(own, BF16), like(own + 4, BF16)],
        [wide(3 * own), wide(own + 6)],
        (xo, mid, x_core, x_other, main, second),
        work * (2 * own + 8),
    )
    skip_here, g_core, g_other = lax.optimization_barrier((skip_here, g_core, g_other))
    skip_there = swap(skip_here, True, same)
    out, gw, back, edge_core, edge_other = call(
        functools.partial(middle_kernel, segments, strips),
        [like(own, BF16), wide_out(own + 2), like(own, BF16), like(2, BF16), like(2, BF16)],
        [wide(own + 4)],
        (skip_here, skip_there, pre1, g, g_core, g_other, second),
        work * (2 * own + 2),
    )
    back_own = swap(back, True, same)
    back_other = swap(edge_other, True, other)
    back_core = swap(edge_core, True, core)
    taps = (3, 3, channels, channels)
    halves = (3, 3, channels // 2, channels)
    terms = [jax.ShapeDtypeStruct(halves, F32), jax.ShapeDtypeStruct(halves, BF16)]
    kept2, sent2, ew = call(
        functools.partial(second_kernel, segments, strips),
        terms + [wide_out(own + 4)],
        [],
        (g, g_core, g_other, back_own, back_core, back_other, pre2, hid, skip_there, gw),
        work * own,
    )
    kept1, sent1, hw = call(
        functools.partial(main_kernel, segments, strips),
        terms + [wide_out(own + 2)],
        [],
        (x, pre1, ew, gw, second),
        work * (2 * own + 2),
    )
    input_grad, output = call(input_kernel, [like(own, BF16)] * 2, [], (hw, main, out), work * own)
    factor = 1.0 / math.sqrt(own * strips * columns)

    def jump(array, bit):
        return swap(array, False, lambda r: r ^ (1 << bit))

    def meet(array, turn):
        return swap(array, False, lambda r: r ^ (turn[r % 2] << 1))

    bits = strips.bit_length() - 1
    quarter = (2, 3, 3, channels // 8, channels)
    got2, got1 = jump(sent2, 0), jump(sent1, 0)
    mine, *sends = call(
        pack_kernel,
        [jax.ShapeDtypeStruct(quarter, F32)] + [jax.ShapeDtypeStruct(quarter, BF16)] * 3,
        [],
        (kept1, got1, kept2, got2),
        kept1.size,
    )
    for turn, send in zip(TURNS, sends):
        mine = mine + meet(send, turn).astype(F32)
    for bit in range(3, bits):
        rounded = lax.optimization_barrier(mine.astype(BF16))
        mine = rounded.astype(F32) + jump(rounded, bit).astype(F32)
    mine = lax.optimization_barrier(mine.astype(BF16))
    gots = [meet(mine, turn) for turn in TURNS]
    (mine,) = call(
        unpack_kernel,
        [jax.ShapeDtypeStruct((2,) + halves, BF16)],
        [],
        (mine, *gots),
        kept1.size,
    )
    theirs = jump(mine, 0)
    first_sum, second_sum = call(
        functools.partial(last_kernel, factor), [jax.ShapeDtypeStruct(taps, F32)] * 2, [], (mine, theirs), kept1.size
    )
    return (output[None], input_grad[None], first_sum[None], second_sum[None])


def solution(mesh):
    field = P("segment", "rows", None, None)
    weight = P("segment", None, None, None, None)
    return jax.shard_map(
        body,
        mesh=mesh,
        in_specs=(field, field, weight, weight),
        out_specs=(field, field, weight, weight),
        check_vma=False,
    )
```

```python
import functools
import math

import jax
import jax.numpy as jnp
from jax import lax
from jax.experimental import pallas as pl
from jax.experimental.pallas import tpu as pltpu
from jax.sharding import PartitionSpec as P

BF16 = jnp.bfloat16
F32 = jnp.float32
TAPS = [(ty, tx) for ty in range(3) for tx in range(3)]


TURNS = ((1, 2), (2, 1), (3, 3))


def silu(values):
    return values * jax.nn.sigmoid(values)


def slope(values):
    gate_value = jax.nn.sigmoid(values)
    return gate_value * (1.0 + values * (1.0 - gate_value))


def place(wide, row, values):
    columns, channels = values.shape
    column = lax.broadcasted_iota(jnp.int32, (columns, channels), 0)
    left = jnp.where(column == 0, 0.0, pltpu.roll(values, 1, 0))
    right = jnp.where(column == columns - 1, 0.0, pltpu.roll(values, columns - 1, 0))
    wide[row, :, 0:channels] = left.astype(BF16)
    wide[row, :, channels : 2 * channels] = values.astype(BF16)
    wide[row, :, 2 * channels : 3 * channels] = right.astype(BF16)


def stacked(wide, start, rows):
    parts = [wide[start + ty : start + ty + rows] for ty in range(3)]
    return jnp.concatenate([part.reshape(rows * part.shape[1], part.shape[2]) for part in parts], axis=1)


def conv(wide, start, rows, kernel):
    lhs = stacked(wide, start, rows)
    out = jnp.dot(lhs, kernel[...].reshape(-1, kernel.shape[-1]), preferred_element_type=F32)
    return out.reshape(rows, -1, out.shape[-1])


def conv_back(wide, start, rows, kernel):
    lhs = stacked(wide, start, rows)
    rhs = jnp.concatenate([kernel[2 - ty, 2 - tx] for ty, tx in TAPS], axis=1)
    out = lax.dot_general(lhs, rhs, (((1,), (1,)), ((), ())), preferred_element_type=F32)
    return out.reshape(rows, -1, out.shape[-1])


def conv_weight(field, wide, start, store):
    rows, columns, channels = field.shape
    lhs = field.reshape(rows * columns, channels)
    for ty in range(3):
        rhs = wide[start + 2 - ty : start + 2 - ty + rows]
        out = lax.dot_general(
            lhs, rhs.reshape(rows * columns, -1), (((0,), (0,)), ((), ())), preferred_element_type=F32
        )
        for tx in range(3):
            store(ty, tx, out[:, (2 - tx) * channels : (3 - tx) * channels])


def here(segments):
    row = lax.axis_index("rows")
    return lax.axis_index("segment") < segments // 2, row, lax.rem(row, 2) == 0


def inside(row, strips, own, offset):
    if offset < 0:
        return row > 0
    if offset >= own:
        return row < strips - 1
    return None


def masked(values, keep):
    return values if keep is None else jnp.where(keep, values, 0.0)


def first_kernel(token):
    token[...] = jnp.zeros_like(token)


def near_kernel(segments, token, x, x_core, main, second, xa, first, ha, pre, skip):
    encoder, _, even = here(segments)
    own = x.shape[0]
    for i in range(own):
        place(xa, jnp.where(even, 0, own) + i, x[i].astype(F32))
        place(xa, jnp.where(even, own, 0) + i, x_core[i].astype(F32))
    first[...] = conv(xa, 0, 2 * own - 2, main)

    @pl.when(encoder)
    def _():
        for i in range(2 * own - 2):
            place(ha, i, silu(first[i]))
        pre[...] = conv(ha, 0, 2 * own - 4, second)
        for i in range(2 * own - 4):
            skip[i] = silu(pre[i]).astype(BF16)


def far_kernel(segments, strips, xa, ha, x_far, main, second, first, pre, hid, skip, xb, hb):
    encoder, row, even = here(segments)
    own = x_far.shape[0]
    near = ha.shape[0]
    columns, channels = x_far.shape[1:]
    far_in = jnp.where(even, row > 0, row < strips - 1)
    for i in range(own):
        place(xb, jnp.where(even, 0, 2) + i, masked(x_far[i].astype(F32), far_in))
    for i in range(2):
        xb[jnp.where(even, own, 0) + i] = xa[jnp.where(even, 0, 2 * own - 2) + i]
    first[...] = conv(xb, 0, own, main)

    @pl.when(encoder)
    def _():
        for i in range(own):
            keep = far_in
            if i == 0:
                keep = jnp.logical_or(far_in, jnp.logical_not(even))
            elif i == own - 1:
                keep = jnp.logical_or(far_in, even)
            place(hb, jnp.where(even, 0, 2) + i, masked(silu(first[i]), keep))
        for i in range(2):
            hb[jnp.where(even, own, 0) + i] = ha[jnp.where(even, 0, near - 2) + i]
        pre[...] = conv(hb, 0, own, second)
        for i in range(own):
            keep = jnp.logical_or(far_in, jnp.logical_not(even) if i < 2 else even)
            skip[i] = masked(silu(pre[i]), keep).astype(BF16)
        for i in range(own):
            middle = slice(channels, 2 * channels)
            at_even = hb[own - 1, :, middle] if i == 0 else ha[i - 1, :, middle]
            at_odd = hb[2, :, middle] if i == own - 1 else ha[own - 1 + i, :, middle]
            hid[i] = jnp.where(even, at_even, at_odd)


def joined(even, near, far, i):
    half = near.shape[0]
    if i < half:
        return jnp.where(even, far[i], near[i])
    return jnp.where(even, near[i - half], far[i - half])


def joined_first(even, near, far, i):
    own = far.shape[0]
    t = own - 1 + i
    at_even = near[t - own - 1] if t > own else far[t - 1]
    at_odd = near[t - 1] if t < 2 * own - 1 else far[t - 2 * own + 1]
    return jnp.where(even, at_even, at_odd)


def middle_kernel(
    segments, strips, near_here, far_here, near, far, near_first, far_first, g, g_core, g_other, second, out, gw, back, edge_core, edge_other, yw
):
    encoder, row, even = here(segments)
    own = g.shape[0]

    @pl.when(encoder)
    def _():
        for i in range(own):
            out[i] = joined(even, near_here, far_here, i + 2)

    @pl.when(jnp.logical_not(encoder))
    def _():
        half = near.shape[0]
        for i in range(half):
            place(yw, jnp.where(even, half, 0) + i, near[i].astype(F32))
            place(yw, jnp.where(even, 0, half) + i, far[i].astype(F32))
        skip_pre = conv(yw, 0, own + 2, second)
        for i in range(own + 2):
            pre = skip_pre[i] + joined_first(even, near_first, far_first, i)
            if i == 0:
                upstream = jnp.where(even, g_other[1].astype(F32), g_core[own - 1].astype(F32))
            elif i == own + 1:
                upstream = jnp.where(even, g_core[0].astype(F32), g_other[0].astype(F32))
            else:
                upstream = g[i - 1].astype(F32)
                out[i - 1] = silu(pre).astype(BF16)
            value = masked(upstream * slope(pre), inside(row, strips, own, i - 1))
            place(gw, i, value)
        back[...] = conv_back(gw, 0, own, second).astype(BF16)
        edge_core[...] = jnp.where(even, back[own - 2 : own], back[0:2])
        edge_other[...] = jnp.where(even, back[0:2], back[own - 2 : own])


def store(even, kept, sent):
    def put(ty, tx, values):
        half = values.shape[0] // 2
        kept[ty, tx] = jnp.where(even, values[:half], values[half:])
        sent[ty, tx] = jnp.where(even, values[half:], values[:half]).astype(BF16)

    return put


def second_kernel(
    segments, strips, g, g_core, g_other, back, back_core, back_other, near_pre, far_pre, hid, near, far, gw, kept, sent, ew
):
    encoder, row, even = here(segments)
    own = g.shape[0]

    @pl.when(encoder)
    def _():
        for i in range(own + 4):
            if i < 2:
                upstream = jnp.where(even, g_other[i].astype(F32), g_core[own - 2 + i].astype(F32))
                returned = jnp.where(even, back_other[i].astype(F32), back_core[i].astype(F32))
            elif i >= own + 2:
                k = i - own - 2
                upstream = jnp.where(even, g_core[k].astype(F32), g_other[k].astype(F32))
                returned = jnp.where(even, back_core[k].astype(F32), back_other[k].astype(F32))
            else:
                upstream = g[i - 2].astype(F32)
                returned = back[i - 2].astype(F32)
            value = (upstream + returned) * slope(joined(even, near_pre, far_pre, i))
            place(ew, i, masked(value, inside(row, strips, own, i - 2)))
        conv_weight(hid[...], ew, 1, store(even, kept, sent))

    @pl.when(jnp.logical_not(encoder))
    def _():
        skip = jnp.stack([joined(even, near, far, i + 2) for i in range(own)])
        conv_weight(skip, gw, 0, store(even, kept, sent))


def main_kernel(segments, strips, x, near_first, far_first, ew, gw, second, kept, sent, hw):
    encoder, row, even = here(segments)
    own = x.shape[0]

    @pl.when(encoder)
    def _():
        hidden_back = conv_back(ew, 0, own + 2, second)
        for i in range(own + 2):
            value = hidden_back[i] * slope(joined_first(even, near_first, far_first, i))
            place(hw, i, masked(value, inside(row, strips, own, i - 1)))

    @pl.when(jnp.logical_not(encoder))
    def _():
        hw[...] = gw[...]

    conv_weight(x[...], hw, 0, store(even, kept, sent))


def input_kernel(hw, main, out, input_grad, output):
    output[...] = out[...]
    input_grad[...] = conv_back(hw, 0, input_grad.shape[0], main).astype(BF16)


def quarters(rows):
    at = lax.axis_index("rows")
    quad = lax.rem(at // 2, 4)
    partners = [jnp.bitwise_xor(quad, jnp.where(lax.rem(at, 2) == 0, *turn)) for turn in TURNS]
    return [pl.ds(pl.multiple_of(partner * rows, rows), rows) for partner in [quad] + partners]


def pack_kernel(kept1, got1, kept2, got2, mine, *sends):
    for k, rows in enumerate(quarters(mine.shape[3])):
        for t, (kept, got) in enumerate(((kept1, got1), (kept2, got2))):
            value = kept[:, :, rows, :] + got[:, :, rows, :].astype(F32)
            if k == 0:
                mine[t] = value
            else:
                sends[k - 1][t] = value.astype(BF16)


def unpack_kernel(mine, *rest):
    out = rest[-1]
    for got, rows in zip((mine,) + rest[:-1], quarters(mine.shape[3])):
        out[:, :, :, rows, :] = got[...]


def last_kernel(factor, mine, theirs, *outs):
    even = lax.rem(lax.axis_index("rows"), 2) == 0
    rows = mine.shape[3]
    own_at = pl.ds(pl.multiple_of(jnp.where(even, 0, rows), rows), rows)
    their_at = pl.ds(pl.multiple_of(jnp.where(even, rows, 0), rows), rows)
    for t, out in enumerate(outs):
        out[:, :, own_at, :] = mine[t].astype(F32) * factor
        out[:, :, their_at, :] = theirs[t].astype(F32) * factor


def call(kernel, outs, scratch, args, flops):
    moved = sum(math.prod(a.shape) * a.dtype.itemsize for a in list(args) + outs)
    return pl.pallas_call(
        kernel,
        out_shape=outs,
        in_specs=[pl.BlockSpec(memory_space=pltpu.VMEM)] * len(args),
        out_specs=[pl.BlockSpec(memory_space=pltpu.VMEM)] * len(outs),
        scratch_shapes=scratch,
        cost_estimate=pl.CostEstimate(flops=flops, bytes_accessed=moved, transcendentals=0),
        compiler_params=pltpu.CompilerParams(vmem_limit_bytes=32 * 1024 * 1024),
    )(*args)


def body(incoming, cotangent, main_weight, second_weight):
    x, g, main, second = incoming[0], cotangent[0], main_weight[0], second_weight[0]
    own, columns, channels = x.shape
    segments, strips = lax.axis_size("segment"), lax.axis_size("rows")
    half = segments // 2
    row = lax.axis_index("rows")
    even = row % 2 == 0
    everyone = [(s, r) for s in range(segments) for r in range(strips)]

    def core(r):
        return r ^ 1

    def other(r):
        neighbour = r - 1 if r % 2 == 0 else r + 1
        return neighbour if 0 <= neighbour < strips else r

    def far(r):
        return other(core(r))

    def same(r):
        return r

    def swap(array, across, to):
        pairs = [
            (s * strips + r, ((s + half) % segments if across else s) * strips + to(r)) for s, r in everyone
        ]
        return lax.ppermute(array, ("segment", "rows"), pairs)

    def like(rows, dtype):
        return jax.ShapeDtypeStruct((rows, columns, channels), dtype)

    def wide(rows):
        return pltpu.VMEM((rows, columns, 3 * channels), BF16)

    def wide_out(rows):
        return jax.ShapeDtypeStruct((rows, columns, 3 * channels), BF16)

    work = 2 * columns * 9 * channels * channels
    (token,) = call(first_kernel, [jax.ShapeDtypeStruct((8, 128), F32)], [], (), 5 * 10**9)
    x_core = swap(x, False, core)
    g_core = swap(g, False, core)
    x_core, token = lax.optimization_barrier((x_core, token))
    x_far = swap(x_core, False, far)
    xa, near_first, ha, near_pre, near_here = call(
        functools.partial(near_kernel, segments),
        [wide_out(2 * own), like(2 * own - 2, F32), wide_out(2 * own - 2), like(2 * own - 4, F32), like(2 * own - 4, BF16)],
        [],
        (token, x, x_core, main, second),
        work * (4 * own - 6),
    )
    near_here, edge = lax.optimization_barrier((near_here, jnp.where(even, g_core[own - 2 :], g_core[:2])))
    near_there = swap(near_here, True, same)
    g_other = swap(edge, False, far)
    far_first, far_pre, hid, far_here = call(
        functools.partial(far_kernel, segments, strips),
        [like(own, F32), like(own, F32), like(own, BF16), like(own, BF16)],
        [wide(own + 2), wide(own + 2)],
        (xa, ha, x_far, main, second),
        work * 2 * own,
    )
    far_there = swap(far_here, True, same)
    out, gw, back, edge_core, edge_other = call(
        functools.partial(middle_kernel, segments, strips),
        [like(own, BF16), wide_out(own + 2), like(own, BF16), like(2, BF16), like(2, BF16)],
        [wide(own + 4)],
        (near_here, far_here, near_there, far_there, near_first, far_first, g, g_core, g_other, second),
        work * (2 * own + 2),
    )
    back_own = swap(back, True, same)
    back_other = swap(edge_other, True, other)
    back_core = swap(edge_core, True, core)
    taps = (3, 3, channels, channels)
    halves = (3, 3, channels // 2, channels)
    terms = [jax.ShapeDtypeStruct(halves, F32), jax.ShapeDtypeStruct(halves, BF16)]
    kept2, sent2, ew = call(
        functools.partial(second_kernel, segments, strips),
        terms + [wide_out(own + 4)],
        [],
        (g, g_core, g_other, back_own, back_core, back_other, near_pre, far_pre, hid, near_there, far_there, gw),
        work * own,
    )
    kept1, sent1, hw = call(
        functools.partial(main_kernel, segments, strips),
        terms + [wide_out(own + 2)],
        [],
        (x, near_first, far_first, ew, gw, second),
        work * (2 * own + 2),
    )
    input_grad, output = call(input_kernel, [like(own, BF16)] * 2, [], (hw, main, out), work * own)
    factor = 1.0 / math.sqrt(own * strips * columns)

    def jump(array, bit):
        return swap(array, False, lambda r: r ^ (1 << bit))

    def meet(array, turn):
        return swap(array, False, lambda r: r ^ (turn[r % 2] << 1))

    bits = strips.bit_length() - 1
    quarter = (2, 3, 3, channels // 8, channels)
    got2, got1 = jump(sent2, 0), jump(sent1, 0)
    mine, *sends = call(
        pack_kernel,
        [jax.ShapeDtypeStruct(quarter, F32)] + [jax.ShapeDtypeStruct(quarter, BF16)] * 3,
        [],
        (kept1, got1, kept2, got2),
        kept1.size,
    )
    for turn, send in zip(TURNS, sends):
        mine = mine + meet(send, turn).astype(F32)
    for bit in range(3, bits):
        rounded = lax.optimization_barrier(mine.astype(BF16))
        mine = rounded.astype(F32) + jump(rounded, bit).astype(F32)
    mine = lax.optimization_barrier(mine.astype(BF16))
    gots = [meet(mine, turn) for turn in TURNS]
    (mine,) = call(
        unpack_kernel,
        [jax.ShapeDtypeStruct((2,) + halves, BF16)],
        [],
        (mine, *gots),
        kept1.size,
    )
    theirs = jump(mine, 0)
    first_sum, second_sum = call(
        functools.partial(last_kernel, factor), [jax.ShapeDtypeStruct(taps, F32)] * 2, [], (mine, theirs), kept1.size
    )
    return (output[None], input_grad[None], first_sum[None], second_sum[None])


def solution(mesh):
    field = P("segment", "rows", None, None)
    weight = P("segment", None, None, None, None)
    return jax.shard_map(
        body,
        mesh=mesh,
        in_specs=(field, field, weight, weight),
        out_specs=(field, field, weight, weight),
        check_vma=False,
    )
```

```python
import functools
import math

import jax
import jax.numpy as jnp
from jax import lax
from jax.experimental import pallas as pl
from jax.experimental.pallas import tpu as pltpu
from jax.sharding import PartitionSpec as P

BF16 = jnp.bfloat16
F32 = jnp.float32
TAPS = [(ty, tx) for ty in range(3) for tx in range(3)]


TURNS = ((3, 3), (1, 2), (2, 1))


def silu(values):
    return values * jax.nn.sigmoid(values)


def slope(values):
    gate_value = jax.nn.sigmoid(values)
    return gate_value * (1.0 + values * (1.0 - gate_value))


def place(wide, row, values):
    columns, channels = values.shape
    column = lax.broadcasted_iota(jnp.int32, (columns, channels), 0)
    left = jnp.where(column == 0, 0.0, pltpu.roll(values, 1, 0))
    right = jnp.where(column == columns - 1, 0.0, pltpu.roll(values, columns - 1, 0))
    wide[row, :, 0:channels] = left.astype(BF16)
    wide[row, :, channels : 2 * channels] = values.astype(BF16)
    wide[row, :, 2 * channels : 3 * channels] = right.astype(BF16)


def stacked(wide, start, rows):
    parts = [wide[start + ty : start + ty + rows] for ty in range(3)]
    return jnp.concatenate([part.reshape(rows * part.shape[1], part.shape[2]) for part in parts], axis=1)


def conv(wide, start, rows, kernel):
    lhs = stacked(wide, start, rows)
    out = jnp.dot(lhs, kernel[...].reshape(-1, kernel.shape[-1]), preferred_element_type=F32)
    return out.reshape(rows, -1, out.shape[-1])


def conv_back(wide, start, rows, kernel):
    lhs = stacked(wide, start, rows)
    rhs = jnp.concatenate([kernel[2 - ty, 2 - tx] for ty, tx in TAPS], axis=1)
    out = lax.dot_general(lhs, rhs, (((1,), (1,)), ((), ())), preferred_element_type=F32)
    return out.reshape(rows, -1, out.shape[-1])


def conv_weight(field, wide, start, store):
    rows, columns, channels = field.shape
    lhs = field.reshape(rows * columns, channels)
    for ty in range(3):
        rhs = wide[start + 2 - ty : start + 2 - ty + rows]
        out = lax.dot_general(
            lhs, rhs.reshape(rows * columns, -1), (((0,), (0,)), ((), ())), preferred_element_type=F32
        )
        for tx in range(3):
            store(ty, tx, out[:, (2 - tx) * channels : (3 - tx) * channels])


def here(segments):
    row = lax.axis_index("rows")
    return lax.axis_index("segment") < segments // 2, row, lax.rem(row, 2) == 0


def inside(row, strips, own, offset):
    if offset < 0:
        return row > 0
    if offset >= own:
        return row < strips - 1
    return None


def masked(values, keep):
    return values if keep is None else jnp.where(keep, values, 0.0)


def first_kernel(token):
    token[...] = jnp.zeros_like(token)


def near_kernel(segments, token, x, x_core, main, second, xa, first, ha, pre, skip):
    encoder, _, even = here(segments)
    own = x.shape[0]
    for i in range(own):
        place(xa, jnp.where(even, 0, own) + i, x[i].astype(F32))
        place(xa, jnp.where(even, own, 0) + i, x_core[i].astype(F32))
    first[...] = conv(xa, 0, 2 * own - 2, main)

    @pl.when(encoder)
    def _():
        for i in range(2 * own - 2):
            place(ha, i, silu(first[i]))
        pre[...] = conv(ha, 0, 2 * own - 4, second)
        for i in range(2 * own - 4):
            skip[i] = silu(pre[i]).astype(BF16)


def far_kernel(segments, strips, xa, ha, from_far, main, second, first, pre, hid, skip, xb, hb):
    encoder, row, even = here(segments)
    own = first.shape[0]
    near = ha.shape[0]
    channels = from_far.shape[2]
    far_in = jnp.where(even, row > 0, row < strips - 1)
    for i in range(own):
        place(xb, jnp.where(even, 0, 2) + i, masked(from_far[i].astype(F32), far_in))
    for i in range(2):
        xb[jnp.where(even, own, 0) + i] = xa[jnp.where(even, 0, 2 * own - 2) + i]
    first[...] = conv(xb, 0, own, main)

    @pl.when(encoder)
    def _():
        for i in range(own):
            keep = far_in
            if i == 0:
                keep = jnp.logical_or(far_in, jnp.logical_not(even))
            elif i == own - 1:
                keep = jnp.logical_or(far_in, even)
            place(hb, jnp.where(even, 0, 2) + i, masked(silu(first[i]), keep))
        for i in range(2):
            hb[jnp.where(even, own, 0) + i] = ha[jnp.where(even, 0, near - 2) + i]
        pre[...] = conv(hb, 0, own, second)
        for i in range(own):
            keep = jnp.logical_or(far_in, jnp.logical_not(even) if i < 2 else even)
            skip[i] = masked(silu(pre[i]), keep).astype(BF16)
        for i in range(own):
            middle = slice(channels, 2 * channels)
            at_even = hb[own - 1, :, middle] if i == 0 else ha[i - 1, :, middle]
            at_odd = hb[2, :, middle] if i == own - 1 else ha[own - 1 + i, :, middle]
            hid[i] = jnp.where(even, at_even, at_odd)


def joined(even, near, far, i):
    half = near.shape[0]
    if i < half:
        return jnp.where(even, far[i], near[i])
    return jnp.where(even, near[i - half], far[i - half])


def joined_first(even, near, far, i):
    own = far.shape[0]
    t = own - 1 + i
    at_even = near[t - own - 1] if t > own else far[t - 1]
    at_odd = near[t - 1] if t < 2 * own - 1 else far[t - 2 * own + 1]
    return jnp.where(even, at_even, at_odd)


def middle_kernel(
    segments, strips, near_here, far_here, near, far, near_first, far_first, g, g_core, from_far, second, out, gw, back, edge_core, edge_other, yw
):
    encoder, row, even = here(segments)
    own = g.shape[0]

    @pl.when(encoder)
    def _():
        for i in range(own):
            out[i] = joined(even, near_here, far_here, i + 2)

    @pl.when(jnp.logical_not(encoder))
    def _():
        half = near.shape[0]
        for i in range(half):
            place(yw, jnp.where(even, half, 0) + i, near[i].astype(F32))
            place(yw, jnp.where(even, 0, half) + i, far[i].astype(F32))
        skip_pre = conv(yw, 0, own + 2, second)
        for i in range(own + 2):
            pre = skip_pre[i] + joined_first(even, near_first, far_first, i)
            if i == 0:
                upstream = jnp.where(even, from_far[own + 1].astype(F32), g_core[own - 1].astype(F32))
            elif i == own + 1:
                upstream = jnp.where(even, g_core[0].astype(F32), from_far[own].astype(F32))
            else:
                upstream = g[i - 1].astype(F32)
                out[i - 1] = silu(pre).astype(BF16)
            value = masked(upstream * slope(pre), inside(row, strips, own, i - 1))
            place(gw, i, value)
        back[...] = conv_back(gw, 0, own, second).astype(BF16)
        edge_core[...] = jnp.where(even, back[own - 2 : own], back[0:2])
        edge_other[...] = jnp.where(even, back[0:2], back[own - 2 : own])


def store(even, kept, sent):
    def put(ty, tx, values):
        half = values.shape[0] // 2
        kept[ty, tx] = jnp.where(even, values[:half], values[half:])
        sent[ty, tx] = jnp.where(even, values[half:], values[:half]).astype(BF16)

    return put


def second_kernel(
    segments, strips, g, g_core, from_far, back, back_core, back_other, near_pre, far_pre, hid, near, far, gw, kept, sent, ew
):
    encoder, row, even = here(segments)
    own = g.shape[0]

    @pl.when(encoder)
    def _():
        for i in range(own + 4):
            if i < 2:
                upstream = jnp.where(even, from_far[own + i].astype(F32), g_core[own - 2 + i].astype(F32))
                returned = jnp.where(even, back_other[i].astype(F32), back_core[i].astype(F32))
            elif i >= own + 2:
                k = i - own - 2
                upstream = jnp.where(even, g_core[k].astype(F32), from_far[own + k].astype(F32))
                returned = jnp.where(even, back_core[k].astype(F32), back_other[k].astype(F32))
            else:
                upstream = g[i - 2].astype(F32)
                returned = back[i - 2].astype(F32)
            value = (upstream + returned) * slope(joined(even, near_pre, far_pre, i))
            place(ew, i, masked(value, inside(row, strips, own, i - 2)))
        conv_weight(hid[...], ew, 1, store(even, kept, sent))

    @pl.when(jnp.logical_not(encoder))
    def _():
        skip = jnp.stack([joined(even, near, far, i + 2) for i in range(own)])
        conv_weight(skip, gw, 0, store(even, kept, sent))


def main_kernel(segments, strips, x, near_first, far_first, ew, gw, second, kept, sent, hw):
    encoder, row, even = here(segments)
    own = x.shape[0]

    @pl.when(encoder)
    def _():
        hidden_back = conv_back(ew, 0, own + 2, second)
        for i in range(own + 2):
            value = hidden_back[i] * slope(joined_first(even, near_first, far_first, i))
            place(hw, i, masked(value, inside(row, strips, own, i - 1)))

    @pl.when(jnp.logical_not(encoder))
    def _():
        hw[...] = gw[...]

    conv_weight(x[...], hw, 0, store(even, kept, sent))


def input_kernel(hw, main, out, input_grad, output):
    output[...] = out[...]
    input_grad[...] = conv_back(hw, 0, input_grad.shape[0], main).astype(BF16)


def quarters(rows):
    at = lax.axis_index("rows")
    quad = lax.rem(at // 2, 4)
    partners = [jnp.bitwise_xor(quad, jnp.where(lax.rem(at, 2) == 0, *turn)) for turn in TURNS]
    return [pl.ds(pl.multiple_of(partner * rows, rows), rows) for partner in [quad] + partners]


def pack_kernel(kept1, got1, kept2, got2, mine, *sends):
    for k, rows in enumerate(quarters(mine.shape[3])):
        for t, (kept, got) in enumerate(((kept1, got1), (kept2, got2))):
            value = kept[:, :, rows, :] + got[:, :, rows, :].astype(F32)
            if k == 0:
                mine[t] = value
            else:
                sends[k - 1][t] = value.astype(BF16)


def unpack_kernel(mine, *rest):
    out = rest[-1]
    for got, rows in zip((mine,) + rest[:-1], quarters(mine.shape[3])):
        out[:, :, :, rows, :] = got[...]


def last_kernel(factor, mine, theirs, *outs):
    even = lax.rem(lax.axis_index("rows"), 2) == 0
    rows = mine.shape[3]
    own_at = pl.ds(pl.multiple_of(jnp.where(even, 0, rows), rows), rows)
    their_at = pl.ds(pl.multiple_of(jnp.where(even, rows, 0), rows), rows)
    for t, out in enumerate(outs):
        out[:, :, own_at, :] = mine[t].astype(F32) * factor
        out[:, :, their_at, :] = theirs[t].astype(F32) * factor


def call(kernel, outs, scratch, args, flops):
    moved = sum(math.prod(a.shape) * a.dtype.itemsize for a in list(args) + outs)
    return pl.pallas_call(
        kernel,
        out_shape=outs,
        in_specs=[pl.BlockSpec(memory_space=pltpu.VMEM)] * len(args),
        out_specs=[pl.BlockSpec(memory_space=pltpu.VMEM)] * len(outs),
        scratch_shapes=scratch,
        cost_estimate=pl.CostEstimate(flops=flops, bytes_accessed=moved, transcendentals=0),
        compiler_params=pltpu.CompilerParams(vmem_limit_bytes=32 * 1024 * 1024),
    )(*args)


def body(incoming, cotangent, main_weight, second_weight):
    x, g, main, second = incoming[0], cotangent[0], main_weight[0], second_weight[0]
    own, columns, channels = x.shape
    segments, strips = lax.axis_size("segment"), lax.axis_size("rows")
    half = segments // 2
    row = lax.axis_index("rows")
    even = row % 2 == 0
    everyone = [(s, r) for s in range(segments) for r in range(strips)]

    def core(r):
        return r ^ 1

    def other(r):
        neighbour = r - 1 if r % 2 == 0 else r + 1
        return neighbour if 0 <= neighbour < strips else r

    def far(r):
        return other(core(r))

    def same(r):
        return r

    def swap(array, across, to):
        pairs = [
            (s * strips + r, ((s + half) % segments if across else s) * strips + to(r)) for s, r in everyone
        ]
        return lax.ppermute(array, ("segment", "rows"), pairs)

    def like(rows, dtype):
        return jax.ShapeDtypeStruct((rows, columns, channels), dtype)

    def wide(rows):
        return pltpu.VMEM((rows, columns, 3 * channels), BF16)

    def wide_out(rows):
        return jax.ShapeDtypeStruct((rows, columns, 3 * channels), BF16)

    work = 2 * columns * 9 * channels * channels
    (token,) = call(first_kernel, [jax.ShapeDtypeStruct((8, 128), F32)], [], (), 5 * 10**9)
    x_core = swap(x, False, core)
    g_core = swap(g, False, core)
    x_core, token = lax.optimization_barrier((x_core, token))
    edge = jnp.where(even, g_core[own - 2 :], g_core[:2])
    from_far = swap(jnp.concatenate([x_core, edge]), False, far)
    xa, near_first, ha, near_pre, near_here = call(
        functools.partial(near_kernel, segments),
        [wide_out(2 * own), like(2 * own - 2, F32), wide_out(2 * own - 2), like(2 * own - 4, F32), like(2 * own - 4, BF16)],
        [],
        (token, x, x_core, main, second),
        work * (4 * own - 6),
    )
    near_there = swap(near_here, True, same)
    far_first, far_pre, hid, far_here = call(
        functools.partial(far_kernel, segments, strips),
        [like(own, F32), like(own, F32), like(own, BF16), like(own, BF16)],
        [wide(own + 2), wide(own + 2)],
        (xa, ha, from_far, main, second),
        work * 2 * own,
    )
    far_there = swap(far_here, True, same)
    out, gw, back, edge_core, edge_other = call(
        functools.partial(middle_kernel, segments, strips),
        [like(own, BF16), wide_out(own + 2), like(own, BF16), like(2, BF16), like(2, BF16)],
        [wide(own + 4)],
        (near_here, far_here, near_there, far_there, near_first, far_first, g, g_core, from_far, second),
        work * (2 * own + 2),
    )
    back_own = swap(back, True, same)
    back_other = swap(edge_other, True, other)
    back_core = swap(edge_core, True, core)
    taps = (3, 3, channels, channels)
    halves = (3, 3, channels // 2, channels)
    terms = [jax.ShapeDtypeStruct(halves, F32), jax.ShapeDtypeStruct(halves, BF16)]
    kept2, sent2, ew = call(
        functools.partial(second_kernel, segments, strips),
        terms + [wide_out(own + 4)],
        [],
        (g, g_core, from_far, back_own, back_core, back_other, near_pre, far_pre, hid, near_there, far_there, gw),
        work * own,
    )
    kept1, sent1, hw = call(
        functools.partial(main_kernel, segments, strips),
        terms + [wide_out(own + 2)],
        [],
        (x, near_first, far_first, ew, gw, second),
        work * (2 * own + 2),
    )
    input_grad, output = call(input_kernel, [like(own, BF16)] * 2, [], (hw, main, out), work * own)
    factor = 1.0 / math.sqrt(own * strips * columns)

    def jump(array, bit):
        return swap(array, False, lambda r: r ^ (1 << bit))

    def meet(array, turn):
        return swap(array, False, lambda r: r ^ (turn[r % 2] << 1))

    bits = strips.bit_length() - 1
    quarter = (2, 3, 3, channels // 8, channels)
    got2, got1 = jump(sent2, 0), jump(sent1, 0)
    mine, *sends = call(
        pack_kernel,
        [jax.ShapeDtypeStruct(quarter, F32)] + [jax.ShapeDtypeStruct(quarter, BF16)] * 3,
        [],
        (kept1, got1, kept2, got2),
        kept1.size,
    )
    for turn, send in zip(TURNS, sends):
        mine = mine + meet(send, turn).astype(F32)
    for bit in range(3, bits):
        rounded = lax.optimization_barrier(mine.astype(BF16))
        mine = rounded.astype(F32) + jump(rounded, bit).astype(F32)
    mine = lax.optimization_barrier(mine.astype(BF16))
    gots = [meet(mine, turn) for turn in TURNS]
    (mine,) = call(
        unpack_kernel,
        [jax.ShapeDtypeStruct((2,) + halves, BF16)],
        [],
        (mine, *gots),
        kept1.size,
    )
    theirs = jump(mine, 0)
    first_sum, second_sum = call(
        functools.partial(last_kernel, factor), [jax.ShapeDtypeStruct(taps, F32)] * 2, [], (mine, theirs), kept1.size
    )
    return (output[None], input_grad[None], first_sum[None], second_sum[None])


def solution(mesh):
    field = P("segment", "rows", None, None)
    weight = P("segment", None, None, None, None)
    return jax.shard_map(
        body,
        mesh=mesh,
        in_specs=(field, field, weight, weight),
        out_specs=(field, field, weight, weight),
        check_vma=False,
    )
```

```python
import functools
import math

import jax
import jax.numpy as jnp
from jax import lax
from jax.experimental import pallas as pl
from jax.experimental.pallas import tpu as pltpu
from jax.sharding import PartitionSpec as P

BF16 = jnp.bfloat16
F32 = jnp.float32
TAPS = [(ty, tx) for ty in range(3) for tx in range(3)]


TURNS = (3, 1, 2)


def silu(values):
    return values * jax.nn.sigmoid(values)


def slope(values):
    gate_value = jax.nn.sigmoid(values)
    return gate_value * (1.0 + values * (1.0 - gate_value))


def place(wide, row, values):
    columns, channels = values.shape
    column = lax.broadcasted_iota(jnp.int32, (columns, channels), 0)
    left = jnp.where(column == 0, 0.0, pltpu.roll(values, 1, 0))
    right = jnp.where(column == columns - 1, 0.0, pltpu.roll(values, columns - 1, 0))
    wide[row, :, 0:channels] = left.astype(BF16)
    wide[row, :, channels : 2 * channels] = values.astype(BF16)
    wide[row, :, 2 * channels : 3 * channels] = right.astype(BF16)


def stacked(wide, start, rows):
    parts = [wide[start + ty : start + ty + rows] for ty in range(3)]
    return jnp.concatenate([part.reshape(rows * part.shape[1], part.shape[2]) for part in parts], axis=1)


def conv(wide, start, rows, kernel):
    lhs = stacked(wide, start, rows)
    out = jnp.dot(lhs, kernel[...].reshape(-1, kernel.shape[-1]), preferred_element_type=F32)
    return out.reshape(rows, -1, out.shape[-1])


def conv_back(wide, start, rows, kernel):
    lhs = stacked(wide, start, rows)
    rhs = jnp.concatenate([kernel[2 - ty, 2 - tx] for ty, tx in TAPS], axis=1)
    out = lax.dot_general(lhs, rhs, (((1,), (1,)), ((), ())), preferred_element_type=F32)
    return out.reshape(rows, -1, out.shape[-1])


def conv_weight(field, wide, start, store):
    rows, columns, channels = field.shape
    lhs = field.reshape(rows * columns, channels)
    for ty in range(3):
        rhs = wide[start + 2 - ty : start + 2 - ty + rows]
        out = lax.dot_general(
            lhs, rhs.reshape(rows * columns, -1), (((0,), (0,)), ((), ())), preferred_element_type=F32
        )
        for tx in range(3):
            store(ty, tx, out[:, (2 - tx) * channels : (3 - tx) * channels])


def here(segments):
    row = lax.axis_index("rows")
    return lax.axis_index("segment") < segments // 2, row, lax.rem(row, 2) == 0


def inside(row, strips, own, offset):
    if offset < 0:
        return row > 0
    if offset >= own:
        return row < strips - 1
    return None


def masked(values, keep):
    return values if keep is None else jnp.where(keep, values, 0.0)


def first_kernel(token):
    token[...] = jnp.zeros_like(token)


def near_kernel(segments, token, x, x_core, main, second, xa, first, ha, pre, skip):
    encoder, _, even = here(segments)
    own = x.shape[0]
    for i in range(own):
        place(xa, jnp.where(even, 0, own) + i, x[i].astype(F32))
        place(xa, jnp.where(even, own, 0) + i, x_core[i].astype(F32))
    first[...] = conv(xa, 0, 2 * own - 2, main)

    @pl.when(encoder)
    def _():
        for i in range(2 * own - 2):
            place(ha, i, silu(first[i]))
        pre[...] = conv(ha, 0, 2 * own - 4, second)
        for i in range(2 * own - 4):
            skip[i] = silu(pre[i]).astype(BF16)


def far_kernel(segments, strips, xa, ha, x_far, main, second, first, pre, hid, skip, xb, hb):
    encoder, row, even = here(segments)
    own = x_far.shape[0]
    near = ha.shape[0]
    columns, channels = x_far.shape[1:]
    far_in = jnp.where(even, row > 0, row < strips - 1)
    for i in range(own):
        place(xb, jnp.where(even, 0, 2) + i, masked(x_far[i].astype(F32), far_in))
    for i in range(2):
        xb[jnp.where(even, own, 0) + i] = xa[jnp.where(even, 0, 2 * own - 2) + i]
    first[...] = conv(xb, 0, own, main)

    @pl.when(encoder)
    def _():
        for i in range(own):
            keep = far_in
            if i == 0:
                keep = jnp.logical_or(far_in, jnp.logical_not(even))
            elif i == own - 1:
                keep = jnp.logical_or(far_in, even)
            place(hb, jnp.where(even, 0, 2) + i, masked(silu(first[i]), keep))
        for i in range(2):
            hb[jnp.where(even, own, 0) + i] = ha[jnp.where(even, 0, near - 2) + i]
        pre[...] = conv(hb, 0, own, second)
        for i in range(own):
            keep = jnp.logical_or(far_in, jnp.logical_not(even) if i < 2 else even)
            skip[i] = masked(silu(pre[i]), keep).astype(BF16)
        for i in range(own):
            middle = slice(channels, 2 * channels)
            at_even = hb[own - 1, :, middle] if i == 0 else ha[i - 1, :, middle]
            at_odd = hb[2, :, middle] if i == own - 1 else ha[own - 1 + i, :, middle]
            hid[i] = jnp.where(even, at_even, at_odd)


def joined(even, near, far, i):
    half = near.shape[0]
    if i < half:
        return jnp.where(even, far[i], near[i])
    return jnp.where(even, near[i - half], far[i - half])


def joined_first(even, near, far, i):
    own = far.shape[0]
    t = own - 1 + i
    at_even = near[t - own - 1] if t > own else far[t - 1]
    at_odd = near[t - 1] if t < 2 * own - 1 else far[t - 2 * own + 1]
    return jnp.where(even, at_even, at_odd)


def middle_kernel(
    segments, strips, near_here, far_here, near, far, near_first, far_first, g, g_core, g_other, second, out, gw, back, edge_core, edge_other, yw
):
    encoder, row, even = here(segments)
    own = g.shape[0]

    @pl.when(encoder)
    def _():
        for i in range(own):
            out[i] = joined(even, near_here, far_here, i + 2)

    @pl.when(jnp.logical_not(encoder))
    def _():
        half = near.shape[0]
        for i in range(half):
            place(yw, jnp.where(even, half, 0) + i, near[i].astype(F32))
            place(yw, jnp.where(even, 0, half) + i, far[i].astype(F32))
        skip_pre = conv(yw, 0, own + 2, second)
        for i in range(own + 2):
            pre = skip_pre[i] + joined_first(even, near_first, far_first, i)
            if i == 0:
                upstream = jnp.where(even, g_other[1].astype(F32), g_core[own - 1].astype(F32))
            elif i == own + 1:
                upstream = jnp.where(even, g_core[0].astype(F32), g_other[0].astype(F32))
            else:
                upstream = g[i - 1].astype(F32)
                out[i - 1] = silu(pre).astype(BF16)
            value = masked(upstream * slope(pre), inside(row, strips, own, i - 1))
            place(gw, i, value)
        back[...] = conv_back(gw, 0, own, second).astype(BF16)
        edge_core[...] = jnp.where(even, back[own - 2 : own], back[0:2])
        edge_other[...] = jnp.where(even, back[0:2], back[own - 2 : own])


def store(kept, sent):
    def put(ty, tx, values):
        kept[ty, tx] = values
        sent[ty, tx] = values.astype(BF16)

    return put


def second_kernel(
    segments, strips, g, g_core, g_other, back, back_core, back_other, near_pre, far_pre, hid, near, far, gw, kept, sent, ew
):
    encoder, row, even = here(segments)
    own = g.shape[0]

    @pl.when(encoder)
    def _():
        for i in range(own + 4):
            if i < 2:
                upstream = jnp.where(even, g_other[i].astype(F32), g_core[own - 2 + i].astype(F32))
                returned = jnp.where(even, back_other[i].astype(F32), back_core[i].astype(F32))
            elif i >= own + 2:
                k = i - own - 2
                upstream = jnp.where(even, g_core[k].astype(F32), g_other[k].astype(F32))
                returned = jnp.where(even, back_core[k].astype(F32), back_other[k].astype(F32))
            else:
                upstream = g[i - 2].astype(F32)
                returned = back[i - 2].astype(F32)
            value = (upstream + returned) * slope(joined(even, near_pre, far_pre, i))
            place(ew, i, masked(value, inside(row, strips, own, i - 2)))
        conv_weight(hid[...], ew, 1, store(kept, sent))

    @pl.when(jnp.logical_not(encoder))
    def _():
        skip = jnp.stack([joined(even, near, far, i + 2) for i in range(own)])
        conv_weight(skip, gw, 0, store(kept, sent))


def main_kernel(segments, strips, x, near_first, far_first, ew, gw, second, kept, sent, hw):
    encoder, row, even = here(segments)
    own = x.shape[0]

    @pl.when(encoder)
    def _():
        hidden_back = conv_back(ew, 0, own + 2, second)
        for i in range(own + 2):
            value = hidden_back[i] * slope(joined_first(even, near_first, far_first, i))
            place(hw, i, masked(value, inside(row, strips, own, i - 1)))

    @pl.when(jnp.logical_not(encoder))
    def _():
        hw[...] = gw[...]

    conv_weight(x[...], hw, 0, store(kept, sent))


def input_kernel(hw, main, out, input_grad, output):
    output[...] = out[...]
    input_grad[...] = conv_back(hw, 0, input_grad.shape[0], main).astype(BF16)


def quarters(rows):
    quad = lax.rem(lax.axis_index("rows") // 2, 4)
    return [pl.ds(pl.multiple_of(jnp.bitwise_xor(quad, k) * rows, rows), rows) for k in (0,) + TURNS]


def pack_kernel(kept1, got1, kept2, got2, mine, *sends):
    for k, rows in enumerate(quarters(mine.shape[3])):
        for t, (kept, got) in enumerate(((kept1, got1), (kept2, got2))):
            value = kept[:, :, rows, :] + got[:, :, rows, :].astype(F32)
            if k == 0:
                mine[t] = value
            else:
                sends[k - 1][t] = value.astype(BF16)


def unpack_kernel(mine, *rest):
    out = rest[-1]
    for got, rows in zip((mine,) + rest[:-1], quarters(mine.shape[3])):
        out[:, :, :, rows, :] = got[...]


def last_kernel(factor, mine, theirs, *outs):
    even = lax.rem(lax.axis_index("rows"), 2) == 0

    def write(sums):
        for t, out in enumerate(outs):
            out[...] = sums[t].astype(F32) * factor

    pl.when(even)(lambda: write(theirs))
    pl.when(jnp.logical_not(even))(lambda: write(mine))


def call(kernel, outs, scratch, args, flops):
    moved = sum(math.prod(a.shape) * a.dtype.itemsize for a in list(args) + outs)
    return pl.pallas_call(
        kernel,
        out_shape=outs,
        in_specs=[pl.BlockSpec(memory_space=pltpu.VMEM)] * len(args),
        out_specs=[pl.BlockSpec(memory_space=pltpu.VMEM)] * len(outs),
        scratch_shapes=scratch,
        cost_estimate=pl.CostEstimate(flops=flops, bytes_accessed=moved, transcendentals=0),
        compiler_params=pltpu.CompilerParams(vmem_limit_bytes=32 * 1024 * 1024),
    )(*args)


def body(incoming, cotangent, main_weight, second_weight):
    x, g, main, second = incoming[0], cotangent[0], main_weight[0], second_weight[0]
    own, columns, channels = x.shape
    segments, strips = lax.axis_size("segment"), lax.axis_size("rows")
    half = segments // 2
    row = lax.axis_index("rows")
    even = row % 2 == 0
    everyone = [(s, r) for s in range(segments) for r in range(strips)]

    def core(r):
        return r ^ 1

    def other(r):
        neighbour = r - 1 if r % 2 == 0 else r + 1
        return neighbour if 0 <= neighbour < strips else r

    def far(r):
        return other(core(r))

    def same(r):
        return r

    def swap(array, across, to):
        pairs = [
            (s * strips + r, ((s + half) % segments if across else s) * strips + to(r)) for s, r in everyone
        ]
        return lax.ppermute(array, ("segment", "rows"), pairs)

    def like(rows, dtype):
        return jax.ShapeDtypeStruct((rows, columns, channels), dtype)

    def wide(rows):
        return pltpu.VMEM((rows, columns, 3 * channels), BF16)

    def wide_out(rows):
        return jax.ShapeDtypeStruct((rows, columns, 3 * channels), BF16)

    work = 2 * columns * 9 * channels * channels
    (token,) = call(first_kernel, [jax.ShapeDtypeStruct((8, 128), F32)], [], (), 5 * 10**9)
    x_core = swap(x, False, core)
    g_core = swap(g, False, core)
    x_core, token = lax.optimization_barrier((x_core, token))
    x_far = swap(x_core, False, far)
    xa, near_first, ha, near_pre, near_here = call(
        functools.partial(near_kernel, segments),
        [wide_out(2 * own), like(2 * own - 2, F32), wide_out(2 * own - 2), like(2 * own - 4, F32), like(2 * own - 4, BF16)],
        [],
        (token, x, x_core, main, second),
        work * (4 * own - 6),
    )
    near_here, edge = lax.optimization_barrier((near_here, jnp.where(even, g_core[own - 2 :], g_core[:2])))
    near_there = swap(near_here, True, same)
    g_other = swap(edge, False, far)
    far_first, far_pre, hid, far_here = call(
        functools.partial(far_kernel, segments, strips),
        [like(own, F32), like(own, F32), like(own, BF16), like(own, BF16)],
        [wide(own + 2), wide(own + 2)],
        (xa, ha, x_far, main, second),
        work * 2 * own,
    )
    far_here, g_other = lax.optimization_barrier((far_here, g_other))
    far_there = swap(far_here, True, same)
    out, gw, back, edge_core, edge_other = call(
        functools.partial(middle_kernel, segments, strips),
        [like(own, BF16), wide_out(own + 2), like(own, BF16), like(2, BF16), like(2, BF16)],
        [wide(own + 4)],
        (near_here, far_here, near_there, far_there, near_first, far_first, g, g_core, g_other, second),
        work * (2 * own + 2),
    )
    back_own = swap(back, True, same)
    back_other = swap(edge_other, True, other)
    back_core = swap(edge_core, True, core)
    taps = (3, 3, channels, channels)
    terms = [jax.ShapeDtypeStruct(taps, F32), jax.ShapeDtypeStruct(taps, BF16)]
    kept2, sent2, ew = call(
        functools.partial(second_kernel, segments, strips),
        terms + [wide_out(own + 4)],
        [],
        (g, g_core, g_other, back_own, back_core, back_other, near_pre, far_pre, hid, near_there, far_there, gw),
        work * own,
    )
    kept1, sent1, hw = call(
        functools.partial(main_kernel, segments, strips),
        terms + [wide_out(own + 2)],
        [],
        (x, near_first, far_first, ew, gw, second),
        work * (2 * own + 2),
    )
    input_grad, output = call(input_kernel, [like(own, BF16)] * 2, [], (hw, main, out), work * own)
    factor = 1.0 / math.sqrt(own * strips * columns)

    def hand(array):
        return swap(array, False, core)

    def meet(array, chips):
        return swap(array, False, lambda r: r ^ (chips << 1) if r % 2 else r)

    bits = strips.bit_length() - 1
    quarter = (2, 3, 3, channels // 4, channels)
    got2, got1 = hand(sent2), hand(sent1)
    mine, *sends = call(
        pack_kernel,
        [jax.ShapeDtypeStruct(quarter, F32)] + [jax.ShapeDtypeStruct(quarter, BF16)] * 3,
        [],
        (kept1, got1, kept2, got2),
        kept1.size,
    )
    for turn, send in zip(TURNS, sends):
        mine = mine + meet(send, turn).astype(F32)
    for bit in range(3, bits):
        rounded = lax.optimization_barrier(mine.astype(BF16))
        mine = rounded.astype(F32) + meet(rounded, 1 << (bit - 1)).astype(F32)
    mine = lax.optimization_barrier(mine.astype(BF16))
    gots = [meet(mine, turn) for turn in TURNS]
    (mine,) = call(
        unpack_kernel,
        [jax.ShapeDtypeStruct((2,) + taps, BF16)],
        [],
        (mine, *gots),
        kept1.size,
    )
    theirs = hand(mine)
    first_sum, second_sum = call(
        functools.partial(last_kernel, factor), [jax.ShapeDtypeStruct(taps, F32)] * 2, [], (mine, theirs), kept1.size
    )
    return (output[None], input_grad[None], first_sum[None], second_sum[None])


def solution(mesh):
    field = P("segment", "rows", None, None)
    weight = P("segment", None, None, None, None)
    return jax.shard_map(
        body,
        mesh=mesh,
        in_specs=(field, field, weight, weight),
        out_specs=(field, field, weight, weight),
        check_vma=False,
    )
```

```python
import functools
import math

import jax
import jax.numpy as jnp
from jax import lax
from jax.experimental import pallas as pl
from jax.experimental.pallas import tpu as pltpu
from jax.sharding import PartitionSpec as P

BF16 = jnp.bfloat16
F32 = jnp.float32
TAPS = [(ty, tx) for ty in range(3) for tx in range(3)]


TURNS = ((3, 3), (1, 2), (2, 1))


def silu(values):
    return values * jax.nn.sigmoid(values)


def slope(values):
    gate_value = jax.nn.sigmoid(values)
    return gate_value * (1.0 + values * (1.0 - gate_value))


def place(wide, row, values):
    columns, channels = values.shape
    column = lax.broadcasted_iota(jnp.int32, (columns, channels), 0)
    left = jnp.where(column == 0, 0.0, pltpu.roll(values, 1, 0))
    right = jnp.where(column == columns - 1, 0.0, pltpu.roll(values, columns - 1, 0))
    wide[row, :, 0:channels] = left.astype(BF16)
    wide[row, :, channels : 2 * channels] = values.astype(BF16)
    wide[row, :, 2 * channels : 3 * channels] = right.astype(BF16)


def stacked(wide, start, rows):
    parts = [wide[start + ty : start + ty + rows] for ty in range(3)]
    return jnp.concatenate([part.reshape(rows * part.shape[1], part.shape[2]) for part in parts], axis=1)


def conv(wide, start, rows, kernel):
    lhs = stacked(wide, start, rows)
    out = jnp.dot(lhs, kernel[...].reshape(-1, kernel.shape[-1]), preferred_element_type=F32)
    return out.reshape(rows, -1, out.shape[-1])


def conv_back(wide, start, rows, kernel):
    lhs = stacked(wide, start, rows)
    rhs = jnp.concatenate([kernel[2 - ty, 2 - tx] for ty, tx in TAPS], axis=1)
    out = lax.dot_general(lhs, rhs, (((1,), (1,)), ((), ())), preferred_element_type=F32)
    return out.reshape(rows, -1, out.shape[-1])


def conv_weight(field, wide, start, store):
    rows, columns, channels = field.shape
    lhs = field.reshape(rows * columns, channels)
    for ty in range(3):
        rhs = wide[start + 2 - ty : start + 2 - ty + rows]
        out = lax.dot_general(
            lhs, rhs.reshape(rows * columns, -1), (((0,), (0,)), ((), ())), preferred_element_type=F32
        )
        for tx in range(3):
            store(ty, tx, out[:, (2 - tx) * channels : (3 - tx) * channels])


def here(segments):
    row = lax.axis_index("rows")
    return lax.axis_index("segment") < segments // 2, row, lax.rem(row, 2) == 0


def inside(row, strips, own, offset):
    if offset < 0:
        return row > 0
    if offset >= own:
        return row < strips - 1
    return None


def masked(values, keep):
    return values if keep is None else jnp.where(keep, values, 0.0)


def first_kernel(token):
    token[...] = jnp.zeros_like(token)


def near_kernel(segments, token, x, x_core, main, second, xa, first, ha, pre, skip):
    encoder, _, even = here(segments)
    own = x.shape[0]
    for i in range(own):
        place(xa, jnp.where(even, 0, own) + i, x[i].astype(F32))
        place(xa, jnp.where(even, own, 0) + i, x_core[i].astype(F32))
    first[...] = conv(xa, 0, 2 * own - 2, main)

    @pl.when(encoder)
    def _():
        for i in range(2 * own - 2):
            place(ha, i, silu(first[i]))
        pre[...] = conv(ha, 0, 2 * own - 4, second)
        for i in range(2 * own - 4):
            skip[i] = silu(pre[i]).astype(BF16)


def far_kernel(segments, strips, xa, ha, x_far, main, second, first, pre, hid, skip, xb, hb):
    encoder, row, even = here(segments)
    own = x_far.shape[0]
    near = ha.shape[0]
    columns, channels = x_far.shape[1:]
    far_in = jnp.where(even, row > 0, row < strips - 1)
    for i in range(own):
        place(xb, jnp.where(even, 0, 2) + i, masked(x_far[i].astype(F32), far_in))
    for i in range(2):
        xb[jnp.where(even, own, 0) + i] = xa[jnp.where(even, 0, 2 * own - 2) + i]
    first[...] = conv(xb, 0, own, main)

    @pl.when(encoder)
    def _():
        for i in range(own):
            keep = far_in
            if i == 0:
                keep = jnp.logical_or(far_in, jnp.logical_not(even))
            elif i == own - 1:
                keep = jnp.logical_or(far_in, even)
            place(hb, jnp.where(even, 0, 2) + i, masked(silu(first[i]), keep))
        for i in range(2):
            hb[jnp.where(even, own, 0) + i] = ha[jnp.where(even, 0, near - 2) + i]
        pre[...] = conv(hb, 0, own, second)
        for i in range(own):
            keep = jnp.logical_or(far_in, jnp.logical_not(even) if i < 2 else even)
            skip[i] = masked(silu(pre[i]), keep).astype(BF16)
        for i in range(own):
            middle = slice(channels, 2 * channels)
            at_even = hb[own - 1, :, middle] if i == 0 else ha[i - 1, :, middle]
            at_odd = hb[2, :, middle] if i == own - 1 else ha[own - 1 + i, :, middle]
            hid[i] = jnp.where(even, at_even, at_odd)


def joined(even, near, far, i):
    half = near.shape[0]
    if i < half:
        return jnp.where(even, far[i], near[i])
    return jnp.where(even, near[i - half], far[i - half])


def joined_first(even, near, far, i):
    own = far.shape[0]
    t = own - 1 + i
    at_even = near[t - own - 1] if t > own else far[t - 1]
    at_odd = near[t - 1] if t < 2 * own - 1 else far[t - 2 * own + 1]
    return jnp.where(even, at_even, at_odd)


def middle_kernel(
    segments, strips, near_here, far_here, near, far, near_first, far_first, g, g_core, g_other, second, out, gw, back, edge_other, yw
):
    encoder, row, even = here(segments)
    own = g.shape[0]

    @pl.when(encoder)
    def _():
        for i in range(own):
            out[i] = joined(even, near_here, far_here, i + 2)

    @pl.when(jnp.logical_not(encoder))
    def _():
        half = near.shape[0]
        for i in range(half):
            place(yw, jnp.where(even, half, 0) + i, near[i].astype(F32))
            place(yw, jnp.where(even, 0, half) + i, far[i].astype(F32))
        skip_pre = conv(yw, 0, own + 2, second)
        for i in range(own + 2):
            pre = skip_pre[i] + joined_first(even, near_first, far_first, i)
            if i == 0:
                upstream = jnp.where(even, g_other[1].astype(F32), g_core[own - 1].astype(F32))
            elif i == own + 1:
                upstream = jnp.where(even, g_core[0].astype(F32), g_other[0].astype(F32))
            else:
                upstream = g[i - 1].astype(F32)
                out[i - 1] = silu(pre).astype(BF16)
            value = masked(upstream * slope(pre), inside(row, strips, own, i - 1))
            place(gw, i, value)
        back[...] = conv_back(gw, 0, own, second).astype(BF16)
        edge_other[...] = jnp.where(even, back[0:2], back[own - 2 : own])


def store(even, kept, sent):
    def put(ty, tx, values):
        half = values.shape[0] // 2
        kept[ty, tx] = jnp.where(even, values[:half], values[half:])
        sent[ty, tx] = jnp.where(even, values[half:], values[:half]).astype(BF16)

    return put


def edge_kernel(segments, strips, g_other, back_other, far_pre, edge_grad):
    encoder, row, even = here(segments)
    far_in = jnp.where(even, row > 0, row < strips - 1)

    @pl.when(encoder)
    def _():
        for i in range(2):
            value = g_other[i].astype(F32) + back_other[i].astype(F32)
            value = value * slope(jnp.where(even, far_pre[i], far_pre[2 + i]))
            edge_grad[i] = masked(value, far_in).astype(BF16)


def second_kernel(
    segments, g, g_core, edge_grad, back, back_core, near_pre, far_pre, hid, near, far, gw, kept, sent, ew
):
    encoder, row, even = here(segments)
    own = g.shape[0]

    @pl.when(encoder)
    def _():
        for i in range(2):
            place(ew, jnp.where(even, 0, own + 2) + i, edge_grad[i].astype(F32))
        for i in range(own):
            value = g[i].astype(F32) + back[i].astype(F32)
            place(ew, 2 + i, value * slope(joined(even, near_pre, far_pre, i + 2)))
        for i in range(2):
            upstream = jnp.where(even, g_core[i].astype(F32), g_core[own - 2 + i].astype(F32))
            returned = jnp.where(even, back_core[i].astype(F32), back_core[own - 2 + i].astype(F32))
            value = (upstream + returned) * slope(jnp.where(even, near_pre[2 + i], near_pre[i]))
            place(ew, jnp.where(even, own + 2, 0) + i, value)
        conv_weight(hid[...], ew, 1, store(even, kept, sent))

    @pl.when(jnp.logical_not(encoder))
    def _():
        skip = jnp.stack([joined(even, near, far, i + 2) for i in range(own)])
        conv_weight(skip, gw, 0, store(even, kept, sent))


def main_kernel(segments, strips, x, near_first, far_first, ew, gw, second, kept, sent, hw):
    encoder, row, even = here(segments)
    own = x.shape[0]

    @pl.when(encoder)
    def _():
        hidden_back = conv_back(ew, 0, own + 2, second)
        for i in range(own + 2):
            value = hidden_back[i] * slope(joined_first(even, near_first, far_first, i))
            place(hw, i, masked(value, inside(row, strips, own, i - 1)))

    @pl.when(jnp.logical_not(encoder))
    def _():
        hw[...] = gw[...]

    conv_weight(x[...], hw, 0, store(even, kept, sent))


def input_kernel(hw, main, out, input_grad, output):
    output[...] = out[...]
    input_grad[...] = conv_back(hw, 0, input_grad.shape[0], main).astype(BF16)


def quarters(rows):
    at = lax.axis_index("rows")
    quad = lax.rem(at // 2, 4)
    partners = [jnp.bitwise_xor(quad, jnp.where(lax.rem(at, 2) == 0, *turn)) for turn in TURNS]
    return [pl.ds(pl.multiple_of(partner * rows, rows), rows) for partner in [quad] + partners]


def pack_kernel(kept1, got1, kept2, got2, mine, *sends):
    for k, rows in enumerate(quarters(mine.shape[3])):
        for t, (kept, got) in enumerate(((kept1, got1), (kept2, got2))):
            value = kept[:, :, rows, :] + got[:, :, rows, :].astype(F32)
            if k == 0:
                mine[t] = value
            else:
                sends[k - 1][t] = value.astype(BF16)


def unpack_kernel(mine, *rest):
    out = rest[-1]
    for got, rows in zip((mine,) + rest[:-1], quarters(mine.shape[3])):
        out[:, :, :, rows, :] = got[...]


def last_kernel(factor, mine, theirs, *outs):
    even = lax.rem(lax.axis_index("rows"), 2) == 0
    rows = mine.shape[3]
    own_at = pl.ds(pl.multiple_of(jnp.where(even, 0, rows), rows), rows)
    their_at = pl.ds(pl.multiple_of(jnp.where(even, rows, 0), rows), rows)
    for t, out in enumerate(outs):
        out[:, :, own_at, :] = mine[t].astype(F32) * factor
        out[:, :, their_at, :] = theirs[t].astype(F32) * factor


def call(kernel, outs, scratch, args, flops):
    moved = sum(math.prod(a.shape) * a.dtype.itemsize for a in list(args) + outs)
    return pl.pallas_call(
        kernel,
        out_shape=outs,
        in_specs=[pl.BlockSpec(memory_space=pltpu.VMEM)] * len(args),
        out_specs=[pl.BlockSpec(memory_space=pltpu.VMEM)] * len(outs),
        scratch_shapes=scratch,
        cost_estimate=pl.CostEstimate(flops=flops, bytes_accessed=moved, transcendentals=0),
        compiler_params=pltpu.CompilerParams(vmem_limit_bytes=32 * 1024 * 1024),
    )(*args)


def body(incoming, cotangent, main_weight, second_weight):
    x, g, main, second = incoming[0], cotangent[0], main_weight[0], second_weight[0]
    own, columns, channels = x.shape
    segments, strips = lax.axis_size("segment"), lax.axis_size("rows")
    half = segments // 2
    row = lax.axis_index("rows")
    even = row % 2 == 0
    everyone = [(s, r) for s in range(segments) for r in range(strips)]

    def core(r):
        return r ^ 1

    def other(r):
        neighbour = r - 1 if r % 2 == 0 else r + 1
        return neighbour if 0 <= neighbour < strips else r

    def far(r):
        return other(core(r))

    def same(r):
        return r

    def swap(array, across, to):
        pairs = [
            (s * strips + r, ((s + half) % segments if across else s) * strips + to(r)) for s, r in everyone
        ]
        return lax.ppermute(array, ("segment", "rows"), pairs)

    def like(rows, dtype):
        return jax.ShapeDtypeStruct((rows, columns, channels), dtype)

    def wide(rows):
        return pltpu.VMEM((rows, columns, 3 * channels), BF16)

    def wide_out(rows):
        return jax.ShapeDtypeStruct((rows, columns, 3 * channels), BF16)

    work = 2 * columns * 9 * channels * channels
    (token,) = call(first_kernel, [jax.ShapeDtypeStruct((8, 128), F32)], [], (), 5 * 10**9)
    x_core = swap(x, False, core)
    g_core = swap(g, False, core)
    x_core, token = lax.optimization_barrier((x_core, token))
    x_far = swap(x_core, False, far)
    xa, near_first, ha, near_pre, near_here = call(
        functools.partial(near_kernel, segments),
        [wide_out(2 * own), like(2 * own - 2, F32), wide_out(2 * own - 2), like(2 * own - 4, F32), like(2 * own - 4, BF16)],
        [],
        (token, x, x_core, main, second),
        work * (4 * own - 6),
    )
    near_here, edge = lax.optimization_barrier((near_here, jnp.where(even, g_core[own - 2 :], g_core[:2])))
    near_there = swap(near_here, True, same)
    g_other = swap(edge, False, far)
    far_first, far_pre, hid, far_here = call(
        functools.partial(far_kernel, segments, strips),
        [like(own, F32), like(own, F32), like(own, BF16), like(own, BF16)],
        [wide(own + 2), wide(own + 2)],
        (xa, ha, x_far, main, second),
        work * 2 * own,
    )
    far_there = swap(far_here, True, same)
    out, gw, back, edge_other = call(
        functools.partial(middle_kernel, segments, strips),
        [like(own, BF16), wide_out(own + 2), like(own, BF16), like(2, BF16)],
        [wide(own + 4)],
        (near_here, far_here, near_there, far_there, near_first, far_first, g, g_core, g_other, second),
        work * (2 * own + 2),
    )
    back_own = swap(back, True, same)
    back_other = swap(edge_other, True, other)
    back_core = swap(back_own, False, core)
    (edge_grad,) = call(
        functools.partial(edge_kernel, segments, strips), [like(2, BF16)], [], (g_other, back_other, far_pre), 2 * 10**9
    )
    taps = (3, 3, channels, channels)
    halves = (3, 3, channels // 2, channels)
    terms = [jax.ShapeDtypeStruct(halves, F32), jax.ShapeDtypeStruct(halves, BF16)]
    kept2, sent2, ew = call(
        functools.partial(second_kernel, segments),
        terms + [wide_out(own + 4)],
        [],
        (g, g_core, edge_grad, back_own, back_core, near_pre, far_pre, hid, near_there, far_there, gw),
        work * own,
    )
    kept1, sent1, hw = call(
        functools.partial(main_kernel, segments, strips),
        terms + [wide_out(own + 2)],
        [],
        (x, near_first, far_first, ew, gw, second),
        work * (2 * own + 2),
    )
    input_grad, output = call(input_kernel, [like(own, BF16)] * 2, [], (hw, main, out), work * own)
    factor = 1.0 / math.sqrt(own * strips * columns)

    def jump(array, bit):
        return swap(array, False, lambda r: r ^ (1 << bit))

    def meet(array, turn):
        return swap(array, False, lambda r: r ^ (turn[r % 2] << 1))

    bits = strips.bit_length() - 1
    quarter = (2, 3, 3, channels // 8, channels)
    got2, got1 = jump(sent2, 0), jump(sent1, 0)
    mine, *sends = call(
        pack_kernel,
        [jax.ShapeDtypeStruct(quarter, F32)] + [jax.ShapeDtypeStruct(quarter, BF16)] * 3,
        [],
        (kept1, got1, kept2, got2),
        kept1.size,
    )
    for turn, send in zip(TURNS, sends):
        mine = mine + meet(send, turn).astype(F32)
    for bit in range(3, bits):
        rounded = lax.optimization_barrier(mine.astype(BF16))
        mine = rounded.astype(F32) + jump(rounded, bit).astype(F32)
    mine = lax.optimization_barrier(mine.astype(BF16))
    gots = [meet(mine, turn) for turn in TURNS]
    (mine,) = call(
        unpack_kernel,
        [jax.ShapeDtypeStruct((2,) + halves, BF16)],
        [],
        (mine, *gots),
        kept1.size,
    )
    theirs = jump(mine, 0)
    first_sum, second_sum = call(
        functools.partial(last_kernel, factor), [jax.ShapeDtypeStruct(taps, F32)] * 2, [], (mine, theirs), kept1.size
    )
    return (output[None], input_grad[None], first_sum[None], second_sum[None])


def solution(mesh):
    field = P("segment", "rows", None, None)
    weight = P("segment", None, None, None, None)
    return jax.shard_map(
        body,
        mesh=mesh,
        in_specs=(field, field, weight, weight),
        out_specs=(field, field, weight, weight),
        check_vma=False,
    )
```

```python
import functools
import math

import jax
import jax.numpy as jnp
from jax import lax
from jax.experimental import pallas as pl
from jax.experimental.pallas import tpu as pltpu
from jax.sharding import PartitionSpec as P

BF16 = jnp.bfloat16
F32 = jnp.float32
TAPS = [(ty, tx) for ty in range(3) for tx in range(3)]


TURNS = ((3, 3), (1, 2), (2, 1))


def silu(values):
    return values * jax.nn.sigmoid(values)


def slope(values):
    gate_value = jax.nn.sigmoid(values)
    return gate_value * (1.0 + values * (1.0 - gate_value))


def place(wide, row, values):
    columns, channels = values.shape
    column = lax.broadcasted_iota(jnp.int32, (columns, channels), 0)
    left = jnp.where(column == 0, 0.0, pltpu.roll(values, 1, 0))
    right = jnp.where(column == columns - 1, 0.0, pltpu.roll(values, columns - 1, 0))
    wide[row, :, 0:channels] = left.astype(BF16)
    wide[row, :, channels : 2 * channels] = values.astype(BF16)
    wide[row, :, 2 * channels : 3 * channels] = right.astype(BF16)


def stacked(wide, start, rows):
    parts = [wide[start + ty : start + ty + rows] for ty in range(3)]
    return jnp.concatenate([part.reshape(rows * part.shape[1], part.shape[2]) for part in parts], axis=1)


def conv(wide, start, rows, kernel):
    lhs = stacked(wide, start, rows)
    out = jnp.dot(lhs, kernel[...].reshape(-1, kernel.shape[-1]), preferred_element_type=F32)
    return out.reshape(rows, -1, out.shape[-1])


def conv_back(wide, start, rows, kernel):
    lhs = stacked(wide, start, rows)
    rhs = jnp.concatenate([kernel[2 - ty, 2 - tx] for ty, tx in TAPS], axis=1)
    out = lax.dot_general(lhs, rhs, (((1,), (1,)), ((), ())), preferred_element_type=F32)
    return out.reshape(rows, -1, out.shape[-1])


def conv_weight(field, wide, start, store):
    rows, columns, channels = field.shape
    lhs = field.reshape(rows * columns, channels)
    for ty in range(3):
        rhs = wide[start + 2 - ty : start + 2 - ty + rows]
        out = lax.dot_general(
            lhs, rhs.reshape(rows * columns, -1), (((0,), (0,)), ((), ())), preferred_element_type=F32
        )
        for tx in range(3):
            store(ty, tx, out[:, (2 - tx) * channels : (3 - tx) * channels])


def here(segments):
    row = lax.axis_index("rows")
    return lax.axis_index("segment") < segments // 2, row, lax.rem(row, 2) == 0


def inside(row, strips, own, offset):
    if offset < 0:
        return row > 0
    if offset >= own:
        return row < strips - 1
    return None


def masked(values, keep):
    return values if keep is None else jnp.where(keep, values, 0.0)


def first_kernel(token):
    token[...] = jnp.zeros_like(token)


def near_kernel(segments, token, x, x_core, main, second, xa, first, ha, pre, skip):
    encoder, _, even = here(segments)
    own = x.shape[0]
    for i in range(own):
        place(xa, jnp.where(even, 0, own) + i, x[i].astype(F32))
        place(xa, jnp.where(even, own, 0) + i, x_core[i].astype(F32))
    first[...] = conv(xa, 0, 2 * own - 2, main)

    @pl.when(encoder)
    def _():
        for i in range(2 * own - 2):
            place(ha, i, silu(first[i]))
        pre[...] = conv(ha, 0, 2 * own - 4, second)
        for i in range(2 * own - 4):
            skip[i] = silu(pre[i]).astype(BF16)


def far_kernel(segments, strips, xa, ha, x_far, main, second, first, pre, hid, skip, xb, hb):
    encoder, row, even = here(segments)
    own = x_far.shape[0]
    near = ha.shape[0]
    columns, channels = x_far.shape[1:]
    far_in = jnp.where(even, row > 0, row < strips - 1)
    for i in range(own):
        place(xb, jnp.where(even, 0, 2) + i, masked(x_far[i].astype(F32), far_in))
    for i in range(2):
        xb[jnp.where(even, own, 0) + i] = xa[jnp.where(even, 0, 2 * own - 2) + i]
    first[...] = conv(xb, 0, own, main)

    @pl.when(encoder)
    def _():
        for i in range(own):
            keep = far_in
            if i == 0:
                keep = jnp.logical_or(far_in, jnp.logical_not(even))
            elif i == own - 1:
                keep = jnp.logical_or(far_in, even)
            place(hb, jnp.where(even, 0, 2) + i, masked(silu(first[i]), keep))
        for i in range(2):
            hb[jnp.where(even, own, 0) + i] = ha[jnp.where(even, 0, near - 2) + i]
        pre[...] = conv(hb, 0, own, second)
        for i in range(own):
            keep = jnp.logical_or(far_in, jnp.logical_not(even) if i < 2 else even)
            skip[i] = masked(silu(pre[i]), keep).astype(BF16)
        for i in range(own):
            middle = slice(channels, 2 * channels)
            at_even = hb[own - 1, :, middle] if i == 0 else ha[i - 1, :, middle]
            at_odd = hb[2, :, middle] if i == own - 1 else ha[own - 1 + i, :, middle]
            hid[i] = jnp.where(even, at_even, at_odd)


def rows_kernel(g, g_core, g_other, out):
    even = lax.rem(lax.axis_index("rows"), 2) == 0
    own = g.shape[0]
    out[2 : own + 2] = g[...]
    out[0:2] = jnp.where(even, g_other[...], g_core[own - 2 :])
    out[own + 2 : own + 4] = jnp.where(even, g_core[:2], g_other[...])


def joined(even, near, far, i):
    half = near.shape[0]
    if i < half:
        return jnp.where(even, far[i], near[i])
    return jnp.where(even, near[i - half], far[i - half])


def joined_first(even, near, far, i):
    own = far.shape[0]
    t = own - 1 + i
    at_even = near[t - own - 1] if t > own else far[t - 1]
    at_odd = near[t - 1] if t < 2 * own - 1 else far[t - 2 * own + 1]
    return jnp.where(even, at_even, at_odd)


def middle_kernel(
    segments, strips, near_here, far_here, near, far, near_first, far_first, g, second, out, gw, back, edge_other, yw
):
    encoder, row, even = here(segments)
    own = out.shape[0]

    @pl.when(encoder)
    def _():
        for i in range(own):
            out[i] = joined(even, near_here, far_here, i + 2)

    @pl.when(jnp.logical_not(encoder))
    def _():
        half = near.shape[0]
        for i in range(half):
            place(yw, jnp.where(even, half, 0) + i, near[i].astype(F32))
            place(yw, jnp.where(even, 0, half) + i, far[i].astype(F32))
        skip_pre = conv(yw, 0, own + 2, second)
        for i in range(own + 2):
            pre = skip_pre[i] + joined_first(even, near_first, far_first, i)
            if 1 <= i <= own:
                out[i - 1] = silu(pre).astype(BF16)
            value = masked(g[i + 1].astype(F32) * slope(pre), inside(row, strips, own, i - 1))
            place(gw, i, value)
        back[...] = conv_back(gw, 0, own, second).astype(BF16)
        edge_other[...] = jnp.where(even, back[0:2], back[own - 2 : own])


def store(even, kept, sent):
    def put(ty, tx, values):
        half = values.shape[0] // 2
        kept[ty, tx] = jnp.where(even, values[:half], values[half:])
        sent[ty, tx] = jnp.where(even, values[half:], values[:half]).astype(BF16)

    return put


def edge_kernel(segments, strips, g, back_other, far_pre, edge_grad):
    encoder, row, even = here(segments)
    far_in = jnp.where(even, row > 0, row < strips - 1)

    @pl.when(encoder)
    def _():
        for i in range(2):
            value = g[jnp.where(even, 0, g.shape[0] - 2) + i].astype(F32) + back_other[i].astype(F32)
            value = value * slope(jnp.where(even, far_pre[i], far_pre[2 + i]))
            edge_grad[i] = masked(value, far_in).astype(BF16)


def second_kernel(
    segments, g, edge_grad, back, back_core, near_pre, far_pre, hid, near, far, gw, kept, sent, ew
):
    encoder, row, even = here(segments)
    own = back.shape[0]

    @pl.when(encoder)
    def _():
        for i in range(2):
            place(ew, jnp.where(even, 0, own + 2) + i, edge_grad[i].astype(F32))
        for i in range(own):
            value = g[i + 2].astype(F32) + back[i].astype(F32)
            place(ew, 2 + i, value * slope(joined(even, near_pre, far_pre, i + 2)))
        for i in range(2):
            upstream = g[jnp.where(even, own + 2, 0) + i].astype(F32)
            returned = jnp.where(even, back_core[i].astype(F32), back_core[own - 2 + i].astype(F32))
            value = (upstream + returned) * slope(jnp.where(even, near_pre[2 + i], near_pre[i]))
            place(ew, jnp.where(even, own + 2, 0) + i, value)
        conv_weight(hid[...], ew, 1, store(even, kept, sent))

    @pl.when(jnp.logical_not(encoder))
    def _():
        skip = jnp.stack([joined(even, near, far, i + 2) for i in range(own)])
        conv_weight(skip, gw, 0, store(even, kept, sent))


def main_kernel(segments, strips, x, near_first, far_first, ew, gw, second, kept, sent, hw):
    encoder, row, even = here(segments)
    own = x.shape[0]

    @pl.when(encoder)
    def _():
        hidden_back = conv_back(ew, 0, own + 2, second)
        for i in range(own + 2):
            value = hidden_back[i] * slope(joined_first(even, near_first, far_first, i))
            place(hw, i, masked(value, inside(row, strips, own, i - 1)))

    @pl.when(jnp.logical_not(encoder))
    def _():
        hw[...] = gw[...]

    conv_weight(x[...], hw, 0, store(even, kept, sent))


def input_kernel(hw, main, out, input_grad, output):
    output[...] = out[...]
    input_grad[...] = conv_back(hw, 0, input_grad.shape[0], main).astype(BF16)


def quarters(rows):
    at = lax.axis_index("rows")
    quad = lax.rem(at // 2, 4)
    partners = [jnp.bitwise_xor(quad, jnp.where(lax.rem(at, 2) == 0, *turn)) for turn in TURNS]
    return [pl.ds(pl.multiple_of(partner * rows, rows), rows) for partner in [quad] + partners]


def sum_kernel(kept, got, out):
    out[...] = kept[...] + got[...].astype(F32)


def pack_kernel(kept1, got1, total2, mine, *sends):
    for k, rows in enumerate(quarters(mine.shape[3])):
        values = (kept1[:, :, rows, :] + got1[:, :, rows, :].astype(F32), total2[:, :, rows, :])
        for t, value in enumerate(values):
            if k == 0:
                mine[t] = value
            else:
                sends[k - 1][t] = value.astype(BF16)


def unpack_kernel(mine, *rest):
    out = rest[-1]
    for got, rows in zip((mine,) + rest[:-1], quarters(mine.shape[3])):
        out[:, :, :, rows, :] = got[...]


def last_kernel(factor, mine, theirs, *outs):
    even = lax.rem(lax.axis_index("rows"), 2) == 0
    rows = mine.shape[3]
    own_at = pl.ds(pl.multiple_of(jnp.where(even, 0, rows), rows), rows)
    their_at = pl.ds(pl.multiple_of(jnp.where(even, rows, 0), rows), rows)
    for t, out in enumerate(outs):
        out[:, :, own_at, :] = mine[t].astype(F32) * factor
        out[:, :, their_at, :] = theirs[t].astype(F32) * factor


def call(kernel, outs, scratch, args, flops):
    moved = sum(math.prod(a.shape) * a.dtype.itemsize for a in list(args) + outs)
    return pl.pallas_call(
        kernel,
        out_shape=outs,
        in_specs=[pl.BlockSpec(memory_space=pltpu.VMEM)] * len(args),
        out_specs=[pl.BlockSpec(memory_space=pltpu.VMEM)] * len(outs),
        scratch_shapes=scratch,
        cost_estimate=pl.CostEstimate(flops=flops, bytes_accessed=moved, transcendentals=0),
        compiler_params=pltpu.CompilerParams(vmem_limit_bytes=32 * 1024 * 1024),
    )(*args)


def body(incoming, cotangent, main_weight, second_weight):
    x, g, main, second = incoming[0], cotangent[0], main_weight[0], second_weight[0]
    own, columns, channels = x.shape
    segments, strips = lax.axis_size("segment"), lax.axis_size("rows")
    half = segments // 2
    row = lax.axis_index("rows")
    even = row % 2 == 0
    everyone = [(s, r) for s in range(segments) for r in range(strips)]

    def core(r):
        return r ^ 1

    def other(r):
        neighbour = r - 1 if r % 2 == 0 else r + 1
        return neighbour if 0 <= neighbour < strips else r

    def far(r):
        return other(core(r))

    def same(r):
        return r

    def swap(array, across, to):
        pairs = [
            (s * strips + r, ((s + half) % segments if across else s) * strips + to(r)) for s, r in everyone
        ]
        return lax.ppermute(array, ("segment", "rows"), pairs)

    def like(rows, dtype):
        return jax.ShapeDtypeStruct((rows, columns, channels), dtype)

    def wide(rows):
        return pltpu.VMEM((rows, columns, 3 * channels), BF16)

    def wide_out(rows):
        return jax.ShapeDtypeStruct((rows, columns, 3 * channels), BF16)

    work = 2 * columns * 9 * channels * channels
    (token,) = call(first_kernel, [jax.ShapeDtypeStruct((8, 128), F32)], [], (), 5 * 10**9)
    x_core = swap(x, False, core)
    g_core = swap(g, False, core)
    x_core, token = lax.optimization_barrier((x_core, token))
    x_far = swap(x_core, False, far)
    xa, near_first, ha, near_pre, near_here = call(
        functools.partial(near_kernel, segments),
        [wide_out(2 * own), like(2 * own - 2, F32), wide_out(2 * own - 2), like(2 * own - 4, F32), like(2 * own - 4, BF16)],
        [],
        (token, x, x_core, main, second),
        work * (4 * own - 6),
    )
    near_here, edge = lax.optimization_barrier((near_here, jnp.where(even, g_core[own - 2 :], g_core[:2])))
    near_there = swap(near_here, True, same)
    g_other = swap(edge, False, far)
    (g_rows,) = call(rows_kernel, [like(own + 4, BF16)], [], (g, g_core, g_other), 2 * 10**9)
    far_first, far_pre, hid, far_here = call(
        functools.partial(far_kernel, segments, strips),
        [like(own, F32), like(own, F32), like(own, BF16), like(own, BF16)],
        [wide(own + 2), wide(own + 2)],
        (xa, ha, x_far, main, second),
        work * 2 * own,
    )
    far_there = swap(far_here, True, same)
    out, gw, back, edge_other = call(
        functools.partial(middle_kernel, segments, strips),
        [like(own, BF16), wide_out(own + 2), like(own, BF16), like(2, BF16)],
        [wide(own + 4)],
        (near_here, far_here, near_there, far_there, near_first, far_first, g_rows, second),
        work * (2 * own + 2),
    )
    back_own = swap(back, True, same)
    back_other = swap(edge_other, True, other)
    back_core = swap(back_own, False, core)
    (edge_grad,) = call(
        functools.partial(edge_kernel, segments, strips), [like(2, BF16)], [], (g_rows, back_other, far_pre), 2 * 10**9
    )
    taps = (3, 3, channels, channels)
    halves = (3, 3, channels // 2, channels)
    terms = [jax.ShapeDtypeStruct(halves, F32), jax.ShapeDtypeStruct(halves, BF16)]
    kept2, sent2, ew = call(
        functools.partial(second_kernel, segments),
        terms + [wide_out(own + 4)],
        [],
        (g_rows, edge_grad, back_own, back_core, near_pre, far_pre, hid, near_there, far_there, gw),
        work * own,
    )
    kept1, sent1, hw = call(
        functools.partial(main_kernel, segments, strips),
        terms + [wide_out(own + 2)],
        [],
        (x, near_first, far_first, ew, gw, second),
        work * (2 * own + 2),
    )
    input_grad, output = call(input_kernel, [like(own, BF16)] * 2, [], (hw, main, out), work * own)
    factor = 1.0 / math.sqrt(own * strips * columns)

    def jump(array, bit):
        return swap(array, False, lambda r: r ^ (1 << bit))

    def meet(array, turn):
        return swap(array, False, lambda r: r ^ (turn[r % 2] << 1))

    bits = strips.bit_length() - 1
    quarter = (2, 3, 3, channels // 8, channels)
    (total2,) = call(sum_kernel, [jax.ShapeDtypeStruct(halves, F32)], [], (kept2, jump(sent2, 0)), 3 * 10**9)
    got1 = jump(sent1, 0)
    mine, *sends = call(
        pack_kernel,
        [jax.ShapeDtypeStruct(quarter, F32)] + [jax.ShapeDtypeStruct(quarter, BF16)] * 3,
        [],
        (kept1, got1, total2),
        kept1.size,
    )
    for turn, send in zip(TURNS, sends):
        mine = mine + meet(send, turn).astype(F32)
    for bit in range(3, bits):
        rounded = lax.optimization_barrier(mine.astype(BF16))
        mine = rounded.astype(F32) + jump(rounded, bit).astype(F32)
    mine = lax.optimization_barrier(mine.astype(BF16))
    gots = [meet(mine, turn) for turn in TURNS]
    (mine,) = call(
        unpack_kernel,
        [jax.ShapeDtypeStruct((2,) + halves, BF16)],
        [],
        (mine, *gots),
        kept1.size,
    )
    theirs = jump(mine, 0)
    first_sum, second_sum = call(
        functools.partial(last_kernel, factor), [jax.ShapeDtypeStruct(taps, F32)] * 2, [], (mine, theirs), kept1.size
    )
    return (output[None], input_grad[None], first_sum[None], second_sum[None])


def solution(mesh):
    field = P("segment", "rows", None, None)
    weight = P("segment", None, None, None, None)
    return jax.shard_map(
        body,
        mesh=mesh,
        in_specs=(field, field, weight, weight),
        out_specs=(field, field, weight, weight),
        check_vma=False,
    )
```

```python
import functools
import math

import jax
import jax.numpy as jnp
from jax import lax
from jax.experimental import pallas as pl
from jax.experimental.pallas import tpu as pltpu
from jax.sharding import PartitionSpec as P

BF16 = jnp.bfloat16
F32 = jnp.float32
TAPS = [(ty, tx) for ty in range(3) for tx in range(3)]


TURNS = ((3, 3), (1, 2), (2, 1))


def silu(values):
    return values * jax.nn.sigmoid(values)


def slope(values):
    gate_value = jax.nn.sigmoid(values)
    return gate_value * (1.0 + values * (1.0 - gate_value))


def place(wide, row, values):
    columns, channels = values.shape
    column = lax.broadcasted_iota(jnp.int32, (columns, channels), 0)
    left = jnp.where(column == 0, 0.0, pltpu.roll(values, 1, 0))
    right = jnp.where(column == columns - 1, 0.0, pltpu.roll(values, columns - 1, 0))
    wide[row, :, 0:channels] = left.astype(BF16)
    wide[row, :, channels : 2 * channels] = values.astype(BF16)
    wide[row, :, 2 * channels : 3 * channels] = right.astype(BF16)


def stacked(wide, start, rows):
    parts = [wide[start + ty : start + ty + rows] for ty in range(3)]
    return jnp.concatenate([part.reshape(rows * part.shape[1], part.shape[2]) for part in parts], axis=1)


def conv(wide, start, rows, kernel):
    lhs = stacked(wide, start, rows)
    out = jnp.dot(lhs, kernel[...].reshape(-1, kernel.shape[-1]), preferred_element_type=F32)
    return out.reshape(rows, -1, out.shape[-1])


def conv_back(wide, start, rows, kernel):
    lhs = stacked(wide, start, rows)
    rhs = jnp.concatenate([kernel[2 - ty, 2 - tx] for ty, tx in TAPS], axis=1)
    out = lax.dot_general(lhs, rhs, (((1,), (1,)), ((), ())), preferred_element_type=F32)
    return out.reshape(rows, -1, out.shape[-1])


def conv_weight(field, wide, start, store):
    rows, columns, channels = field.shape
    lhs = field.reshape(rows * columns, channels)
    for ty in range(3):
        rhs = wide[start + 2 - ty : start + 2 - ty + rows]
        out = lax.dot_general(
            lhs, rhs.reshape(rows * columns, -1), (((0,), (0,)), ((), ())), preferred_element_type=F32
        )
        for tx in range(3):
            store(ty, tx, out[:, (2 - tx) * channels : (3 - tx) * channels])


def here(segments):
    row = lax.axis_index("rows")
    return lax.axis_index("segment") < segments // 2, row, lax.rem(row, 2) == 0


def inside(row, strips, own, offset):
    if offset < 0:
        return row > 0
    if offset >= own:
        return row < strips - 1
    return None


def masked(values, keep):
    return values if keep is None else jnp.where(keep, values, 0.0)


def first_kernel(token):
    token[...] = jnp.zeros_like(token)


def near_kernel(segments, token, x, x_core, main, second, xa, first, ha, pre, skip, skip_own):
    encoder, _, even = here(segments)
    own = x.shape[0]
    for i in range(own):
        place(xa, jnp.where(even, 0, own) + i, x[i].astype(F32))
        place(xa, jnp.where(even, own, 0) + i, x_core[i].astype(F32))
    first[...] = conv(xa, 0, 2 * own - 2, main)

    @pl.when(encoder)
    def _():
        for i in range(2 * own - 2):
            place(ha, i, silu(first[i]))
        pre[...] = conv(ha, 0, 2 * own - 4, second)
        for i in range(2 * own - 4):
            skip[i] = silu(pre[i]).astype(BF16)
        skip_own[...] = jnp.where(even, skip[0:2], skip[own - 2 : own])


def far_kernel(segments, strips, xa, ha, x_far, main, second, first, pre, hid, skip, xb, hb):
    encoder, row, even = here(segments)
    own = x_far.shape[0]
    near = ha.shape[0]
    columns, channels = x_far.shape[1:]
    far_in = jnp.where(even, row > 0, row < strips - 1)
    for i in range(own):
        place(xb, jnp.where(even, 0, 2) + i, masked(x_far[i].astype(F32), far_in))
    for i in range(2):
        xb[jnp.where(even, own, 0) + i] = xa[jnp.where(even, 0, 2 * own - 2) + i]
    first[...] = conv(xb, 0, own, main)

    @pl.when(encoder)
    def _():
        for i in range(own):
            keep = far_in
            if i == 0:
                keep = jnp.logical_or(far_in, jnp.logical_not(even))
            elif i == own - 1:
                keep = jnp.logical_or(far_in, even)
            place(hb, jnp.where(even, 0, 2) + i, masked(silu(first[i]), keep))
        for i in range(2):
            hb[jnp.where(even, own, 0) + i] = ha[jnp.where(even, 0, near - 2) + i]
        pre[...] = conv(hb, 0, own, second)
        for i in range(own):
            keep = jnp.logical_or(far_in, jnp.logical_not(even) if i < 2 else even)
            skip[i] = masked(silu(pre[i]), keep).astype(BF16)
        for i in range(own):
            middle = slice(channels, 2 * channels)
            at_even = hb[own - 1, :, middle] if i == 0 else ha[i - 1, :, middle]
            at_odd = hb[2, :, middle] if i == own - 1 else ha[own - 1 + i, :, middle]
            hid[i] = jnp.where(even, at_even, at_odd)


def rows_kernel(g, g_core, g_other, out):
    even = lax.rem(lax.axis_index("rows"), 2) == 0
    own = g.shape[0]
    out[2 : own + 2] = g[...]
    out[0:2] = jnp.where(even, g_other[...], g_core[own - 2 :])
    out[own + 2 : own + 4] = jnp.where(even, g_core[:2], g_other[...])


def joined(even, near, far, i):
    half = near.shape[0]
    if i < half:
        return jnp.where(even, far[i], near[i])
    return jnp.where(even, near[i - half], far[i - half])


def joined_first(even, near, far, i):
    own = far.shape[0]
    t = own - 1 + i
    at_even = near[t - own - 1] if t > own else far[t - 1]
    at_odd = near[t - 1] if t < 2 * own - 1 else far[t - 2 * own + 1]
    return jnp.where(even, at_even, at_odd)


def middle_kernel(
    segments, strips, near_here, far_here, near_own, near_core, far, near_first, far_first, g, second, out, gw, back, edge_other, yw
):
    encoder, row, even = here(segments)
    own = out.shape[0]

    @pl.when(encoder)
    def _():
        for i in range(own):
            out[i] = joined(even, near_here, far_here, i + 2)

    @pl.when(jnp.logical_not(encoder))
    def _():
        for i in range(2):
            place(yw, jnp.where(even, own, own - 2) + i, near_own[i].astype(F32))
            place(yw, jnp.where(even, own + 2, 0) + i, near_core[i].astype(F32))
        for i in range(own):
            place(yw, jnp.where(even, 0, own) + i, far[i].astype(F32))
        skip_pre = conv(yw, 0, own + 2, second)
        for i in range(own + 2):
            pre = skip_pre[i] + joined_first(even, near_first, far_first, i)
            if 1 <= i <= own:
                out[i - 1] = silu(pre).astype(BF16)
            value = masked(g[i + 1].astype(F32) * slope(pre), inside(row, strips, own, i - 1))
            place(gw, i, value)
        back[...] = conv_back(gw, 0, own, second).astype(BF16)
        edge_other[...] = jnp.where(even, back[0:2], back[own - 2 : own])


def store(even, kept, sent):
    def put(ty, tx, values):
        half = values.shape[0] // 2
        kept[ty, tx] = jnp.where(even, values[:half], values[half:])
        sent[ty, tx] = jnp.where(even, values[half:], values[:half]).astype(BF16)

    return put


def edge_kernel(segments, strips, g, back_other, far_pre, edge_grad):
    encoder, row, even = here(segments)
    far_in = jnp.where(even, row > 0, row < strips - 1)

    @pl.when(encoder)
    def _():
        for i in range(2):
            value = g[jnp.where(even, 0, g.shape[0] - 2) + i].astype(F32) + back_other[i].astype(F32)
            value = value * slope(jnp.where(even, far_pre[i], far_pre[2 + i]))
            edge_grad[i] = masked(value, far_in).astype(BF16)


def second_kernel(
    segments, g, edge_grad, back, back_core, near_pre, far_pre, hid, near_own, far, gw, kept, sent, ew
):
    encoder, row, even = here(segments)
    own = back.shape[0]

    @pl.when(encoder)
    def _():
        for i in range(2):
            place(ew, jnp.where(even, 0, own + 2) + i, edge_grad[i].astype(F32))
        for i in range(own):
            value = g[i + 2].astype(F32) + back[i].astype(F32)
            place(ew, 2 + i, value * slope(joined(even, near_pre, far_pre, i + 2)))
        for i in range(2):
            upstream = g[jnp.where(even, own + 2, 0) + i].astype(F32)
            returned = jnp.where(even, back_core[i].astype(F32), back_core[own - 2 + i].astype(F32))
            value = (upstream + returned) * slope(jnp.where(even, near_pre[2 + i], near_pre[i]))
            place(ew, jnp.where(even, own + 2, 0) + i, value)
        conv_weight(hid[...], ew, 1, store(even, kept, sent))

    @pl.when(jnp.logical_not(encoder))
    def _():
        half = own // 2
        rows = [jnp.where(even, far[own - half + i], near_own[i]) for i in range(half)]
        rows += [jnp.where(even, near_own[i], far[i]) for i in range(half)]
        skip = jnp.stack(rows)
        conv_weight(skip, gw, 0, store(even, kept, sent))


def main_kernel(segments, strips, x, near_first, far_first, ew, gw, second, kept, sent, hw):
    encoder, row, even = here(segments)
    own = x.shape[0]

    @pl.when(encoder)
    def _():
        hidden_back = conv_back(ew, 0, own + 2, second)
        for i in range(own + 2):
            value = hidden_back[i] * slope(joined_first(even, near_first, far_first, i))
            place(hw, i, masked(value, inside(row, strips, own, i - 1)))

    @pl.when(jnp.logical_not(encoder))
    def _():
        hw[...] = gw[...]

    conv_weight(x[...], hw, 0, store(even, kept, sent))


def input_kernel(hw, main, out, input_grad, output):
    output[...] = out[...]
    input_grad[...] = conv_back(hw, 0, input_grad.shape[0], main).astype(BF16)


def quarters(rows):
    at = lax.axis_index("rows")
    quad = lax.rem(at // 2, 4)
    partners = [jnp.bitwise_xor(quad, jnp.where(lax.rem(at, 2) == 0, *turn)) for turn in TURNS]
    return [pl.ds(pl.multiple_of(partner * rows, rows), rows) for partner in [quad] + partners]


def sum_kernel(kept, got, out):
    out[...] = kept[...] + got[...].astype(F32)


def pack_kernel(kept1, got1, total2, mine, *sends):
    for k, rows in enumerate(quarters(mine.shape[3])):
        values = (kept1[:, :, rows, :] + got1[:, :, rows, :].astype(F32), total2[:, :, rows, :])
        for t, value in enumerate(values):
            if k == 0:
                mine[t] = value
            else:
                sends[k - 1][t] = value.astype(BF16)


def unpack_kernel(mine, *rest):
    out = rest[-1]
    for got, rows in zip((mine,) + rest[:-1], quarters(mine.shape[3])):
        out[:, :, :, rows, :] = got[...]


def last_kernel(factor, mine, theirs, *outs):
    even = lax.rem(lax.axis_index("rows"), 2) == 0
    rows = mine.shape[3]
    own_at = pl.ds(pl.multiple_of(jnp.where(even, 0, rows), rows), rows)
    their_at = pl.ds(pl.multiple_of(jnp.where(even, rows, 0), rows), rows)
    for t, out in enumerate(outs):
        out[:, :, own_at, :] = mine[t].astype(F32) * factor
        out[:, :, their_at, :] = theirs[t].astype(F32) * factor


def call(kernel, outs, scratch, args, flops):
    moved = sum(math.prod(a.shape) * a.dtype.itemsize for a in list(args) + outs)
    return pl.pallas_call(
        kernel,
        out_shape=outs,
        in_specs=[pl.BlockSpec(memory_space=pltpu.VMEM)] * len(args),
        out_specs=[pl.BlockSpec(memory_space=pltpu.VMEM)] * len(outs),
        scratch_shapes=scratch,
        cost_estimate=pl.CostEstimate(flops=flops, bytes_accessed=moved, transcendentals=0),
        compiler_params=pltpu.CompilerParams(vmem_limit_bytes=32 * 1024 * 1024),
    )(*args)


def body(incoming, cotangent, main_weight, second_weight):
    x, g, main, second = incoming[0], cotangent[0], main_weight[0], second_weight[0]
    own, columns, channels = x.shape
    segments, strips = lax.axis_size("segment"), lax.axis_size("rows")
    half = segments // 2
    row = lax.axis_index("rows")
    even = row % 2 == 0
    everyone = [(s, r) for s in range(segments) for r in range(strips)]

    def core(r):
        return r ^ 1

    def other(r):
        neighbour = r - 1 if r % 2 == 0 else r + 1
        return neighbour if 0 <= neighbour < strips else r

    def far(r):
        return other(core(r))

    def same(r):
        return r

    def swap(array, across, to):
        pairs = [
            (s * strips + r, ((s + half) % segments if across else s) * strips + to(r)) for s, r in everyone
        ]
        return lax.ppermute(array, ("segment", "rows"), pairs)

    def like(rows, dtype):
        return jax.ShapeDtypeStruct((rows, columns, channels), dtype)

    def wide(rows):
        return pltpu.VMEM((rows, columns, 3 * channels), BF16)

    def wide_out(rows):
        return jax.ShapeDtypeStruct((rows, columns, 3 * channels), BF16)

    work = 2 * columns * 9 * channels * channels
    (token,) = call(first_kernel, [jax.ShapeDtypeStruct((8, 128), F32)], [], (), 5 * 10**9)
    x_core = swap(x, False, core)
    g_core = swap(g, False, core)
    x_core, token = lax.optimization_barrier((x_core, token))
    x_far = swap(x_core, False, far)
    xa, near_first, ha, near_pre, near_here, near_sent = call(
        functools.partial(near_kernel, segments),
        [wide_out(2 * own), like(2 * own - 2, F32), wide_out(2 * own - 2), like(2 * own - 4, F32), like(2 * own - 4, BF16), like(2, BF16)],
        [],
        (token, x, x_core, main, second),
        work * (4 * own - 6),
    )
    near_sent, edge = lax.optimization_barrier((near_sent, jnp.where(even, g_core[own - 2 :], g_core[:2])))
    near_own = swap(near_sent, True, same)
    g_other = swap(edge, False, far)
    (g_rows,) = call(rows_kernel, [like(own + 4, BF16)], [], (g, g_core, g_other), 2 * 10**9)
    far_first, far_pre, hid, far_here = call(
        functools.partial(far_kernel, segments, strips),
        [like(own, F32), like(own, F32), like(own, BF16), like(own, BF16)],
        [wide(own + 2), wide(own + 2)],
        (xa, ha, x_far, main, second),
        work * 2 * own,
    )
    far_there = swap(far_here, True, same)
    near_own, hid = lax.optimization_barrier((near_own, hid))
    near_core = swap(near_own, False, core)
    out, gw, back, edge_other = call(
        functools.partial(middle_kernel, segments, strips),
        [like(own, BF16), wide_out(own + 2), like(own, BF16), like(2, BF16)],
        [wide(own + 4)],
        (near_here, far_here, near_own, near_core, far_there, near_first, far_first, g_rows, second),
        work * (2 * own + 2),
    )
    back_own = swap(back, True, same)
    back_other = swap(edge_other, True, other)
    back_core = swap(back_own, False, core)
    (edge_grad,) = call(
        functools.partial(edge_kernel, segments, strips), [like(2, BF16)], [], (g_rows, back_other, far_pre), 2 * 10**9
    )
    taps = (3, 3, channels, channels)
    halves = (3, 3, channels // 2, channels)
    terms = [jax.ShapeDtypeStruct(halves, F32), jax.ShapeDtypeStruct(halves, BF16)]
    kept2, sent2, ew = call(
        functools.partial(second_kernel, segments),
        terms + [wide_out(own + 4)],
        [],
        (g_rows, edge_grad, back_own, back_core, near_pre, far_pre, hid, near_own, far_there, gw),
        work * own,
    )
    kept1, sent1, hw = call(
        functools.partial(main_kernel, segments, strips),
        terms + [wide_out(own + 2)],
        [],
        (x, near_first, far_first, ew, gw, second),
        work * (2 * own + 2),
    )
    input_grad, output = call(input_kernel, [like(own, BF16)] * 2, [], (hw, main, out), work * own)
    factor = 1.0 / math.sqrt(own * strips * columns)

    def jump(array, bit):
        return swap(array, False, lambda r: r ^ (1 << bit))

    def meet(array, turn):
        return swap(array, False, lambda r: r ^ (turn[r % 2] << 1))

    bits = strips.bit_length() - 1
    quarter = (2, 3, 3, channels // 8, channels)
    (total2,) = call(sum_kernel, [jax.ShapeDtypeStruct(halves, F32)], [], (kept2, jump(sent2, 0)), 3 * 10**9)
    got1 = jump(sent1, 0)
    mine, *sends = call(
        pack_kernel,
        [jax.ShapeDtypeStruct(quarter, F32)] + [jax.ShapeDtypeStruct(quarter, BF16)] * 3,
        [],
        (kept1, got1, total2),
        kept1.size,
    )
    for turn, send in zip(TURNS, sends):
        mine = mine + meet(send, turn).astype(F32)
    for bit in range(3, bits):
        rounded = lax.optimization_barrier(mine.astype(BF16))
        mine = rounded.astype(F32) + jump(rounded, bit).astype(F32)
    mine = lax.optimization_barrier(mine.astype(BF16))
    gots = [meet(mine, turn) for turn in TURNS]
    (mine,) = call(
        unpack_kernel,
        [jax.ShapeDtypeStruct((2,) + halves, BF16)],
        [],
        (mine, *gots),
        kept1.size,
    )
    theirs = jump(mine, 0)
    first_sum, second_sum = call(
        functools.partial(last_kernel, factor), [jax.ShapeDtypeStruct(taps, F32)] * 2, [], (mine, theirs), kept1.size
    )
    return (output[None], input_grad[None], first_sum[None], second_sum[None])


def solution(mesh):
    field = P("segment", "rows", None, None)
    weight = P("segment", None, None, None, None)
    return jax.shard_map(
        body,
        mesh=mesh,
        in_specs=(field, field, weight, weight),
        out_specs=(field, field, weight, weight),
        check_vma=False,
    )
```

```python
import functools
import math

import jax
import jax.numpy as jnp
from jax import lax
from jax.experimental import pallas as pl
from jax.experimental.pallas import tpu as pltpu
from jax.sharding import PartitionSpec as P

BF16 = jnp.bfloat16
F32 = jnp.float32
TAPS = [(ty, tx) for ty in range(3) for tx in range(3)]


TURNS = ((3, 3), (1, 2), (2, 1))


def silu(values):
    return values * jax.nn.sigmoid(values)


def slope(values):
    gate_value = jax.nn.sigmoid(values)
    return gate_value * (1.0 + values * (1.0 - gate_value))


def place(wide, row, values):
    columns, channels = values.shape
    column = lax.broadcasted_iota(jnp.int32, (columns, channels), 0)
    left = jnp.where(column == 0, 0.0, pltpu.roll(values, 1, 0))
    right = jnp.where(column == columns - 1, 0.0, pltpu.roll(values, columns - 1, 0))
    wide[row, :, 0:channels] = left.astype(BF16)
    wide[row, :, channels : 2 * channels] = values.astype(BF16)
    wide[row, :, 2 * channels : 3 * channels] = right.astype(BF16)


def stacked(wide, start, rows):
    parts = [wide[start + ty : start + ty + rows] for ty in range(3)]
    return jnp.concatenate([part.reshape(rows * part.shape[1], part.shape[2]) for part in parts], axis=1)


def conv(wide, start, rows, kernel):
    lhs = stacked(wide, start, rows)
    out = jnp.dot(lhs, kernel[...].reshape(-1, kernel.shape[-1]), preferred_element_type=F32)
    return out.reshape(rows, -1, out.shape[-1])


def conv_back(wide, start, rows, kernel):
    lhs = stacked(wide, start, rows)
    rhs = jnp.concatenate([kernel[2 - ty, 2 - tx] for ty, tx in TAPS], axis=1)
    out = lax.dot_general(lhs, rhs, (((1,), (1,)), ((), ())), preferred_element_type=F32)
    return out.reshape(rows, -1, out.shape[-1])


def conv_weight(field, wide, start, store):
    rows, columns, channels = field.shape
    lhs = field.reshape(rows * columns, channels)
    for ty in range(3):
        rhs = wide[start + 2 - ty : start + 2 - ty + rows]
        out = lax.dot_general(
            lhs, rhs.reshape(rows * columns, -1), (((0,), (0,)), ((), ())), preferred_element_type=F32
        )
        for tx in range(3):
            store(ty, tx, out[:, (2 - tx) * channels : (3 - tx) * channels])


def here(segments):
    row = lax.axis_index("rows")
    return lax.axis_index("segment") < segments // 2, row, lax.rem(row, 2) == 0


def inside(row, strips, own, offset):
    if offset < 0:
        return row > 0
    if offset >= own:
        return row < strips - 1
    return None


def masked(values, keep):
    return values if keep is None else jnp.where(keep, values, 0.0)


def first_kernel(token):
    token[...] = jnp.zeros_like(token)


def near_kernel(segments, token, x, x_core, main, second, xa, first, ha, pre, skip, skip_own):
    encoder, _, even = here(segments)
    own = x.shape[0]
    for i in range(own):
        place(xa, jnp.where(even, 0, own) + i, x[i].astype(F32))
        place(xa, jnp.where(even, own, 0) + i, x_core[i].astype(F32))
    first[...] = conv(xa, 0, 2 * own - 2, main)

    @pl.when(encoder)
    def _():
        for i in range(2 * own - 2):
            place(ha, i, silu(first[i]))
        pre[...] = conv(ha, 0, 2 * own - 4, second)
        for i in range(2 * own - 4):
            skip[i] = silu(pre[i]).astype(BF16)
        skip_own[...] = jnp.where(even, skip[0:2], skip[own - 2 : own])


def far_kernel(segments, strips, xa, ha, x_far, main, second, first, pre, hid, skip, xb, hb):
    encoder, row, even = here(segments)
    own = x_far.shape[0]
    near = ha.shape[0]
    columns, channels = x_far.shape[1:]
    far_in = jnp.where(even, row > 0, row < strips - 1)
    for i in range(own):
        place(xb, jnp.where(even, 0, 2) + i, masked(x_far[i].astype(F32), far_in))
    for i in range(2):
        xb[jnp.where(even, own, 0) + i] = xa[jnp.where(even, 0, 2 * own - 2) + i]
    first[...] = conv(xb, 0, own, main)

    @pl.when(encoder)
    def _():
        for i in range(own):
            keep = far_in
            if i == 0:
                keep = jnp.logical_or(far_in, jnp.logical_not(even))
            elif i == own - 1:
                keep = jnp.logical_or(far_in, even)
            place(hb, jnp.where(even, 0, 2) + i, masked(silu(first[i]), keep))
        for i in range(2):
            hb[jnp.where(even, own, 0) + i] = ha[jnp.where(even, 0, near - 2) + i]
        pre[...] = conv(hb, 0, own, second)
        for i in range(own):
            keep = jnp.logical_or(far_in, jnp.logical_not(even) if i < 2 else even)
            skip[i] = masked(silu(pre[i]), keep).astype(BF16)
        for i in range(own):
            middle = slice(channels, 2 * channels)
            at_even = hb[own - 1, :, middle] if i == 0 else ha[i - 1, :, middle]
            at_odd = hb[2, :, middle] if i == own - 1 else ha[own - 1 + i, :, middle]
            hid[i] = jnp.where(even, at_even, at_odd)


def rows_kernel(g, g_core, g_other, out):
    even = lax.rem(lax.axis_index("rows"), 2) == 0
    own = g.shape[0]
    out[2 : own + 2] = g[...]
    out[0:2] = jnp.where(even, g_other[...], g_core[own - 2 :])
    out[own + 2 : own + 4] = jnp.where(even, g_core[:2], g_other[...])


def joined(even, near, far, i):
    half = near.shape[0]
    if i < half:
        return jnp.where(even, far[i], near[i])
    return jnp.where(even, near[i - half], far[i - half])


def joined_first(even, near, far, i):
    own = far.shape[0]
    t = own - 1 + i
    at_even = near[t - own - 1] if t > own else far[t - 1]
    at_odd = near[t - 1] if t < 2 * own - 1 else far[t - 2 * own + 1]
    return jnp.where(even, at_even, at_odd)


def middle_kernel(
    segments, strips, near_here, far_here, near_own, near_core, far, near_first, far_first, g, second, out, gw, back, edge_other, yw
):
    encoder, row, even = here(segments)
    own = out.shape[0]

    @pl.when(encoder)
    def _():
        for i in range(own):
            out[i] = joined(even, near_here, far_here, i + 2)

    @pl.when(jnp.logical_not(encoder))
    def _():
        for i in range(2):
            place(yw, jnp.where(even, own, own - 2) + i, near_own[i].astype(F32))
            place(yw, jnp.where(even, own + 2, 0) + i, near_core[i].astype(F32))
        for i in range(own):
            place(yw, jnp.where(even, 0, own) + i, far[i].astype(F32))
        skip_pre = conv(yw, 0, own + 2, second)
        for i in range(own + 2):
            pre = skip_pre[i] + joined_first(even, near_first, far_first, i)
            if 1 <= i <= own:
                out[i - 1] = silu(pre).astype(BF16)
            value = masked(g[i + 1].astype(F32) * slope(pre), inside(row, strips, own, i - 1))
            place(gw, i, value)
        back[...] = conv_back(gw, 0, own, second).astype(BF16)
        edge_other[...] = jnp.where(even, back[0:2], back[own - 2 : own])


def store(even, kept, sent):
    def put(ty, tx, values):
        half = values.shape[0] // 2
        kept[ty, tx] = jnp.where(even, values[:half], values[half:])
        sent[ty, tx] = jnp.where(even, values[half:], values[:half]).astype(BF16)

    return put


def edge_kernel(segments, strips, g, back_other, far_pre, edge_grad):
    encoder, row, even = here(segments)
    far_in = jnp.where(even, row > 0, row < strips - 1)

    @pl.when(encoder)
    def _():
        for i in range(2):
            value = g[jnp.where(even, 0, g.shape[0] - 2) + i].astype(F32) + back_other[i].astype(F32)
            value = value * slope(jnp.where(even, far_pre[i], far_pre[2 + i]))
            edge_grad[i] = masked(value, far_in).astype(BF16)


def second_kernel(
    segments, g, edge_grad, back, back_core, near_pre, far_pre, hid, near_own, far, gw, kept, sent, ew
):
    encoder, row, even = here(segments)
    own = back.shape[0]

    @pl.when(encoder)
    def _():
        for i in range(2):
            place(ew, jnp.where(even, 0, own + 2) + i, edge_grad[i].astype(F32))
        for i in range(own):
            value = g[i + 2].astype(F32) + back[i].astype(F32)
            place(ew, 2 + i, value * slope(joined(even, near_pre, far_pre, i + 2)))
        for i in range(2):
            upstream = g[jnp.where(even, own + 2, 0) + i].astype(F32)
            returned = jnp.where(even, back_core[i].astype(F32), back_core[own - 2 + i].astype(F32))
            value = (upstream + returned) * slope(jnp.where(even, near_pre[2 + i], near_pre[i]))
            place(ew, jnp.where(even, own + 2, 0) + i, value)
        conv_weight(hid[...], ew, 1, store(even, kept, sent))

    @pl.when(jnp.logical_not(encoder))
    def _():
        half = own // 2
        rows = [jnp.where(even, far[own - half + i], near_own[i]) for i in range(half)]
        rows += [jnp.where(even, near_own[i], far[i]) for i in range(half)]
        skip = jnp.stack(rows)
        conv_weight(skip, gw, 0, store(even, kept, sent))


def main_kernel(segments, strips, x, near_first, far_first, ew, gw, second, kept, sent, hw):
    encoder, row, even = here(segments)
    own = x.shape[0]

    @pl.when(encoder)
    def _():
        hidden_back = conv_back(ew, 0, own + 2, second)
        for i in range(own + 2):
            value = hidden_back[i] * slope(joined_first(even, near_first, far_first, i))
            place(hw, i, masked(value, inside(row, strips, own, i - 1)))

    @pl.when(jnp.logical_not(encoder))
    def _():
        hw[...] = gw[...]

    conv_weight(x[...], hw, 0, store(even, kept, sent))


def input_kernel(hw, main, out, input_grad, output):
    output[...] = out[...]
    input_grad[...] = conv_back(hw, 0, input_grad.shape[0], main).astype(BF16)


def quarters(rows):
    at = lax.axis_index("rows")
    quad = lax.rem(at // 2, 4)
    partners = [jnp.bitwise_xor(quad, jnp.where(lax.rem(at, 2) == 0, *turn)) for turn in TURNS]
    return [pl.ds(pl.multiple_of(partner * rows, rows), rows) for partner in [quad] + partners]


def sum_kernel(kept, got, out):
    out[...] = kept[...] + got[...].astype(F32)


def pack_kernel(kept1, got1, total2, mine, *sends):
    for k, rows in enumerate(quarters(mine.shape[3])):
        values = (kept1[:, :, rows, :] + got1[:, :, rows, :].astype(F32), total2[:, :, rows, :])
        for t, value in enumerate(values):
            if k == 0:
                mine[t] = value
            else:
                sends[k - 1][t] = value.astype(BF16)


def unpack_kernel(mine, *rest):
    out = rest[-1]
    for got, rows in zip((mine,) + rest[:-1], quarters(mine.shape[3])):
        out[:, :, :, rows, :] = got[...]


def last_kernel(factor, mine, theirs, *outs):
    even = lax.rem(lax.axis_index("rows"), 2) == 0
    rows = mine.shape[3]
    own_at = pl.ds(pl.multiple_of(jnp.where(even, 0, rows), rows), rows)
    their_at = pl.ds(pl.multiple_of(jnp.where(even, rows, 0), rows), rows)
    for t, out in enumerate(outs):
        out[:, :, own_at, :] = mine[t].astype(F32) * factor
        out[:, :, their_at, :] = theirs[t].astype(F32) * factor


def call(kernel, outs, scratch, args, flops):
    moved = sum(math.prod(a.shape) * a.dtype.itemsize for a in list(args) + outs)
    return pl.pallas_call(
        kernel,
        out_shape=outs,
        in_specs=[pl.BlockSpec(memory_space=pltpu.VMEM)] * len(args),
        out_specs=[pl.BlockSpec(memory_space=pltpu.VMEM)] * len(outs),
        scratch_shapes=scratch,
        cost_estimate=pl.CostEstimate(flops=flops, bytes_accessed=moved, transcendentals=0),
        compiler_params=pltpu.CompilerParams(vmem_limit_bytes=32 * 1024 * 1024),
    )(*args)


def body(incoming, cotangent, main_weight, second_weight):
    x, g, main, second = incoming[0], cotangent[0], main_weight[0], second_weight[0]
    own, columns, channels = x.shape
    segments, strips = lax.axis_size("segment"), lax.axis_size("rows")
    half = segments // 2
    row = lax.axis_index("rows")
    even = row % 2 == 0
    everyone = [(s, r) for s in range(segments) for r in range(strips)]

    def core(r):
        return r ^ 1

    def other(r):
        neighbour = r - 1 if r % 2 == 0 else r + 1
        return neighbour if 0 <= neighbour < strips else r

    def far(r):
        return other(core(r))

    def same(r):
        return r

    def swap(array, across, to):
        pairs = [
            (s * strips + r, ((s + half) % segments if across else s) * strips + to(r)) for s, r in everyone
        ]
        return lax.ppermute(array, ("segment", "rows"), pairs)

    def like(rows, dtype):
        return jax.ShapeDtypeStruct((rows, columns, channels), dtype)

    def wide(rows):
        return pltpu.VMEM((rows, columns, 3 * channels), BF16)

    def wide_out(rows):
        return jax.ShapeDtypeStruct((rows, columns, 3 * channels), BF16)

    work = 2 * columns * 9 * channels * channels
    (token,) = call(first_kernel, [jax.ShapeDtypeStruct((8, 128), F32)], [], (), 5 * 10**9)
    x_core = swap(x, False, core)
    g_core = swap(g, False, core)
    x_core, token = lax.optimization_barrier((x_core, token))
    x_far = swap(x_core, False, far)
    xa, near_first, ha, near_pre, near_here, near_sent = call(
        functools.partial(near_kernel, segments),
        [wide_out(2 * own), like(2 * own - 2, F32), wide_out(2 * own - 2), like(2 * own - 4, F32), like(2 * own - 4, BF16), like(2, BF16)],
        [],
        (token, x, x_core, main, second),
        work * (4 * own - 6),
    )
    near_sent, edge = lax.optimization_barrier((near_sent, jnp.where(even, g_core[own - 2 :], g_core[:2])))
    near_own = swap(near_sent, True, same)
    g_other = swap(edge, False, far)
    (g_rows,) = call(rows_kernel, [like(own + 4, BF16)], [], (g, g_core, g_other), 2 * 10**9)
    far_first, far_pre, hid, far_here = call(
        functools.partial(far_kernel, segments, strips),
        [like(own, F32), like(own, F32), like(own, BF16), like(own, BF16)],
        [wide(own + 2), wide(own + 2)],
        (xa, ha, x_far, main, second),
        work * 2 * own,
    )
    far_there = swap(far_here, True, same)
    near_own, g_rows = lax.optimization_barrier((near_own, g_rows))
    near_core = swap(near_own, False, core)
    out, gw, back, edge_other = call(
        functools.partial(middle_kernel, segments, strips),
        [like(own, BF16), wide_out(own + 2), like(own, BF16), like(2, BF16)],
        [wide(own + 4)],
        (near_here, far_here, near_own, near_core, far_there, near_first, far_first, g_rows, second),
        work * (2 * own + 2),
    )
    back_own = swap(back, True, same)
    back_other = swap(edge_other, True, other)
    back_core = swap(back_own, False, core)
    (edge_grad,) = call(
        functools.partial(edge_kernel, segments, strips), [like(2, BF16)], [], (g_rows, back_other, far_pre), 2 * 10**9
    )
    taps = (3, 3, channels, channels)
    halves = (3, 3, channels // 2, channels)
    terms = [jax.ShapeDtypeStruct(halves, F32), jax.ShapeDtypeStruct(halves, BF16)]
    kept2, sent2, ew = call(
        functools.partial(second_kernel, segments),
        terms + [wide_out(own + 4)],
        [],
        (g_rows, edge_grad, back_own, back_core, near_pre, far_pre, hid, near_own, far_there, gw),
        work * own,
    )
    kept1, sent1, hw = call(
        functools.partial(main_kernel, segments, strips),
        terms + [wide_out(own + 2)],
        [],
        (x, near_first, far_first, ew, gw, second),
        work * (2 * own + 2),
    )
    input_grad, output = call(input_kernel, [like(own, BF16)] * 2, [], (hw, main, out), work * own)
    factor = 1.0 / math.sqrt(own * strips * columns)

    def jump(array, bit):
        return swap(array, False, lambda r: r ^ (1 << bit))

    def meet(array, turn):
        return swap(array, False, lambda r: r ^ (turn[r % 2] << 1))

    bits = strips.bit_length() - 1
    quarter = (2, 3, 3, channels // 8, channels)
    (total2,) = call(sum_kernel, [jax.ShapeDtypeStruct(halves, F32)], [], (kept2, jump(sent2, 0)), 3 * 10**9)
    got1 = jump(sent1, 0)
    mine, *sends = call(
        pack_kernel,
        [jax.ShapeDtypeStruct(quarter, F32)] + [jax.ShapeDtypeStruct(quarter, BF16)] * 3,
        [],
        (kept1, got1, total2),
        kept1.size,
    )
    for turn, send in zip(TURNS, sends):
        mine = mine + meet(send, turn).astype(F32)
    for bit in range(3, bits):
        rounded = lax.optimization_barrier(mine.astype(BF16))
        mine = rounded.astype(F32) + jump(rounded, bit).astype(F32)
    mine = lax.optimization_barrier(mine.astype(BF16))
    gots = [meet(mine, turn) for turn in TURNS]
    (mine,) = call(
        unpack_kernel,
        [jax.ShapeDtypeStruct((2,) + halves, BF16)],
        [],
        (mine, *gots),
        kept1.size,
    )
    theirs = jump(mine, 0)
    first_sum, second_sum = call(
        functools.partial(last_kernel, factor), [jax.ShapeDtypeStruct(taps, F32)] * 2, [], (mine, theirs), kept1.size
    )
    return (output[None], input_grad[None], first_sum[None], second_sum[None])


def solution(mesh):
    field = P("segment", "rows", None, None)
    weight = P("segment", None, None, None, None)
    return jax.shard_map(
        body,
        mesh=mesh,
        in_specs=(field, field, weight, weight),
        out_specs=(field, field, weight, weight),
        check_vma=False,
    )
```

```python
import functools
import math

import jax
import jax.numpy as jnp
from jax import lax
from jax.experimental import pallas as pl
from jax.experimental.pallas import tpu as pltpu
from jax.sharding import PartitionSpec as P

BF16 = jnp.bfloat16
F32 = jnp.float32
TAPS = [(ty, tx) for ty in range(3) for tx in range(3)]


TURNS = ((3, 3), (1, 2), (2, 1))


def silu(values):
    return values * jax.nn.sigmoid(values)


def slope(values):
    gate_value = jax.nn.sigmoid(values)
    return gate_value * (1.0 + values * (1.0 - gate_value))


def place(wide, row, values):
    columns, channels = values.shape
    column = lax.broadcasted_iota(jnp.int32, (columns, channels), 0)
    left = jnp.where(column == 0, 0.0, pltpu.roll(values, 1, 0))
    right = jnp.where(column == columns - 1, 0.0, pltpu.roll(values, columns - 1, 0))
    wide[row, :, 0:channels] = left.astype(BF16)
    wide[row, :, channels : 2 * channels] = values.astype(BF16)
    wide[row, :, 2 * channels : 3 * channels] = right.astype(BF16)


def stacked(wide, start, rows):
    parts = [wide[start + ty : start + ty + rows] for ty in range(3)]
    return jnp.concatenate([part.reshape(rows * part.shape[1], part.shape[2]) for part in parts], axis=1)


def conv(wide, start, rows, kernel):
    lhs = stacked(wide, start, rows)
    out = jnp.dot(lhs, kernel[...].reshape(-1, kernel.shape[-1]), preferred_element_type=F32)
    return out.reshape(rows, -1, out.shape[-1])


def conv_back(wide, start, rows, kernel):
    lhs = stacked(wide, start, rows)
    rhs = jnp.concatenate([kernel[2 - ty, 2 - tx] for ty, tx in TAPS], axis=1)
    out = lax.dot_general(lhs, rhs, (((1,), (1,)), ((), ())), preferred_element_type=F32)
    return out.reshape(rows, -1, out.shape[-1])


def conv_weight(field, wide, start, store):
    rows, columns, channels = field.shape
    lhs = field.reshape(rows * columns, channels)
    for ty in range(3):
        rhs = wide[start + 2 - ty : start + 2 - ty + rows]
        out = lax.dot_general(
            lhs, rhs.reshape(rows * columns, -1), (((0,), (0,)), ((), ())), preferred_element_type=F32
        )
        for tx in range(3):
            store(ty, tx, out[:, (2 - tx) * channels : (3 - tx) * channels])


def here(segments):
    row = lax.axis_index("rows")
    return lax.axis_index("segment") < segments // 2, row, lax.rem(row, 2) == 0


def inside(row, strips, own, offset):
    if offset < 0:
        return row > 0
    if offset >= own:
        return row < strips - 1
    return None


def masked(values, keep):
    return values if keep is None else jnp.where(keep, values, 0.0)


def first_kernel(token):
    token[...] = jnp.zeros_like(token)


def near_kernel(segments, token, x, x_core, main, second, xa, first, ha, pre, skip):
    encoder, _, even = here(segments)
    own = x.shape[0]
    for i in range(own):
        place(xa, jnp.where(even, 0, own) + i, x[i].astype(F32))
        place(xa, jnp.where(even, own, 0) + i, x_core[i].astype(F32))
    first[...] = conv(xa, 0, 2 * own - 2, main)

    @pl.when(encoder)
    def _():
        for i in range(2 * own - 2):
            place(ha, i, silu(first[i]))
        pre[...] = conv(ha, 0, 2 * own - 4, second)
        for i in range(2 * own - 4):
            skip[i] = silu(pre[i]).astype(BF16)


def far_kernel(segments, strips, xa, ha, x_far, main, second, first, pre, hid, skip, xb, hb):
    encoder, row, even = here(segments)
    own = x_far.shape[0]
    near = ha.shape[0]
    columns, channels = x_far.shape[1:]
    far_in = jnp.where(even, row > 0, row < strips - 1)
    for i in range(own):
        place(xb, jnp.where(even, 0, 2) + i, masked(x_far[i].astype(F32), far_in))
    for i in range(2):
        xb[jnp.where(even, own, 0) + i] = xa[jnp.where(even, 0, 2 * own - 2) + i]
    first[...] = conv(xb, 0, own, main)

    @pl.when(encoder)
    def _():
        for i in range(own):
            keep = far_in
            if i == 0:
                keep = jnp.logical_or(far_in, jnp.logical_not(even))
            elif i == own - 1:
                keep = jnp.logical_or(far_in, even)
            place(hb, jnp.where(even, 0, 2) + i, masked(silu(first[i]), keep))
        for i in range(2):
            hb[jnp.where(even, own, 0) + i] = ha[jnp.where(even, 0, near - 2) + i]
        pre[...] = conv(hb, 0, own, second)
        for i in range(own):
            keep = jnp.logical_or(far_in, jnp.logical_not(even) if i < 2 else even)
            skip[i] = masked(silu(pre[i]), keep).astype(BF16)
        for i in range(own):
            middle = slice(channels, 2 * channels)
            at_even = hb[own - 1, :, middle] if i == 0 else ha[i - 1, :, middle]
            at_odd = hb[2, :, middle] if i == own - 1 else ha[own - 1 + i, :, middle]
            hid[i] = jnp.where(even, at_even, at_odd)


def rows_kernel(g, g_core, g_other, out):
    even = lax.rem(lax.axis_index("rows"), 2) == 0
    own = g.shape[0]
    out[2 : own + 2] = g[...]
    out[0:2] = jnp.where(even, g_other[...], g_core[own - 2 :])
    out[own + 2 : own + 4] = jnp.where(even, g_core[:2], g_other[...])


def joined(even, near, far, i):
    half = near.shape[0]
    if i < half:
        return jnp.where(even, far[i], near[i])
    return jnp.where(even, near[i - half], far[i - half])


def joined_first(even, near, far, i):
    own = far.shape[0]
    t = own - 1 + i
    at_even = near[t - own - 1] if t > own else far[t - 1]
    at_odd = near[t - 1] if t < 2 * own - 1 else far[t - 2 * own + 1]
    return jnp.where(even, at_even, at_odd)


def part_conv(yw, rows, upper, kernel):
    own = rows.shape[0]
    zeros = jnp.zeros(yw.shape[1:], yw.dtype)
    for i in range(2):
        yw[jnp.where(upper, 0, own) + i] = zeros
    for i in range(own):
        place(yw, jnp.where(upper, 2, 0) + i, rows[i].astype(F32))
    return conv(yw, 0, own, kernel)


def part_row(part, upper, i):
    own = part.shape[0]
    zeros = jnp.zeros(part.shape[1:], part.dtype)
    return jnp.where(upper, part[i - 2] if i >= 2 else zeros, part[i] if i < own else zeros)


def base_kernel(segments, near, near_first, far_first, second, base, yw):
    encoder, _, even = here(segments)

    @pl.when(jnp.logical_not(encoder))
    def _():
        part = part_conv(yw, near, even, second)
        for i in range(base.shape[0]):
            base[i] = joined_first(even, near_first, far_first, i) + part_row(part, even, i)


def middle_kernel(
    segments, strips, near_here, far_here, far, base, g, second, out, gw, back, edge_other, yw
):
    encoder, row, even = here(segments)
    own = out.shape[0]

    @pl.when(encoder)
    def _():
        for i in range(own):
            out[i] = joined(even, near_here, far_here, i + 2)

    @pl.when(jnp.logical_not(encoder))
    def _():
        part = part_conv(yw, far, jnp.logical_not(even), second)
        for i in range(own + 2):
            pre = base[i] + part_row(part, jnp.logical_not(even), i)
            if 1 <= i <= own:
                out[i - 1] = silu(pre).astype(BF16)
            value = masked(g[i + 1].astype(F32) * slope(pre), inside(row, strips, own, i - 1))
            place(gw, i, value)
        back[...] = conv_back(gw, 0, own, second).astype(BF16)
        edge_other[...] = jnp.where(even, back[0:2], back[own - 2 : own])


def store(even, kept, sent):
    def put(ty, tx, values):
        half = values.shape[0] // 2
        kept[ty, tx] = jnp.where(even, values[:half], values[half:])
        sent[ty, tx] = jnp.where(even, values[half:], values[:half]).astype(BF16)

    return put


def edge_kernel(segments, strips, g, back_other, far_pre, edge_grad):
    encoder, row, even = here(segments)
    far_in = jnp.where(even, row > 0, row < strips - 1)

    @pl.when(encoder)
    def _():
        for i in range(2):
            value = g[jnp.where(even, 0, g.shape[0] - 2) + i].astype(F32) + back_other[i].astype(F32)
            value = value * slope(jnp.where(even, far_pre[i], far_pre[2 + i]))
            edge_grad[i] = masked(value, far_in).astype(BF16)


def second_kernel(
    segments, g, edge_grad, back, back_core, near_pre, far_pre, hid, near, far, gw, kept, sent, ew
):
    encoder, row, even = here(segments)
    own = back.shape[0]

    @pl.when(encoder)
    def _():
        for i in range(2):
            place(ew, jnp.where(even, 0, own + 2) + i, edge_grad[i].astype(F32))
        for i in range(own):
            value = g[i + 2].astype(F32) + back[i].astype(F32)
            place(ew, 2 + i, value * slope(joined(even, near_pre, far_pre, i + 2)))
        for i in range(2):
            upstream = g[jnp.where(even, own + 2, 0) + i].astype(F32)
            returned = jnp.where(even, back_core[i].astype(F32), back_core[own - 2 + i].astype(F32))
            value = (upstream + returned) * slope(jnp.where(even, near_pre[2 + i], near_pre[i]))
            place(ew, jnp.where(even, own + 2, 0) + i, value)
        conv_weight(hid[...], ew, 1, store(even, kept, sent))

    @pl.when(jnp.logical_not(encoder))
    def _():
        skip = jnp.stack([joined(even, near, far, i + 2) for i in range(own)])
        conv_weight(skip, gw, 0, store(even, kept, sent))


def main_kernel(segments, strips, x, near_first, far_first, ew, gw, second, kept, sent, hw):
    encoder, row, even = here(segments)
    own = x.shape[0]

    @pl.when(encoder)
    def _():
        hidden_back = conv_back(ew, 0, own + 2, second)
        for i in range(own + 2):
            value = hidden_back[i] * slope(joined_first(even, near_first, far_first, i))
            place(hw, i, masked(value, inside(row, strips, own, i - 1)))

    @pl.when(jnp.logical_not(encoder))
    def _():
        hw[...] = gw[...]

    conv_weight(x[...], hw, 0, store(even, kept, sent))


def input_kernel(hw, main, out, input_grad, output):
    output[...] = out[...]
    input_grad[...] = conv_back(hw, 0, input_grad.shape[0], main).astype(BF16)


def quarters(rows):
    at = lax.axis_index("rows")
    quad = lax.rem(at // 2, 4)
    partners = [jnp.bitwise_xor(quad, jnp.where(lax.rem(at, 2) == 0, *turn)) for turn in TURNS]
    return [pl.ds(pl.multiple_of(partner * rows, rows), rows) for partner in [quad] + partners]


def sum_kernel(kept, got, out):
    out[...] = kept[...] + got[...].astype(F32)


def pack_kernel(kept1, got1, total2, mine, *sends):
    for k, rows in enumerate(quarters(mine.shape[3])):
        values = (kept1[:, :, rows, :] + got1[:, :, rows, :].astype(F32), total2[:, :, rows, :])
        for t, value in enumerate(values):
            if k == 0:
                mine[t] = value
            else:
                sends[k - 1][t] = value.astype(BF16)


def unpack_kernel(mine, *rest):
    out = rest[-1]
    for got, rows in zip((mine,) + rest[-2::-1], quarters(mine.shape[3])):
        out[:, :, :, rows, :] = got[...]


def last_kernel(factor, mine, theirs, *outs):
    even = lax.rem(lax.axis_index("rows"), 2) == 0
    rows = mine.shape[3]
    own_at = pl.ds(pl.multiple_of(jnp.where(even, 0, rows), rows), rows)
    their_at = pl.ds(pl.multiple_of(jnp.where(even, rows, 0), rows), rows)
    for t, out in enumerate(outs):
        out[:, :, own_at, :] = mine[t].astype(F32) * factor
        out[:, :, their_at, :] = theirs[t].astype(F32) * factor


def call(kernel, outs, scratch, args, flops):
    moved = sum(math.prod(a.shape) * a.dtype.itemsize for a in list(args) + outs)
    return pl.pallas_call(
        kernel,
        out_shape=outs,
        in_specs=[pl.BlockSpec(memory_space=pltpu.VMEM)] * len(args),
        out_specs=[pl.BlockSpec(memory_space=pltpu.VMEM)] * len(outs),
        scratch_shapes=scratch,
        cost_estimate=pl.CostEstimate(flops=flops, bytes_accessed=moved, transcendentals=0),
        compiler_params=pltpu.CompilerParams(vmem_limit_bytes=32 * 1024 * 1024),
    )(*args)


def body(incoming, cotangent, main_weight, second_weight):
    x, g, main, second = incoming[0], cotangent[0], main_weight[0], second_weight[0]
    own, columns, channels = x.shape
    segments, strips = lax.axis_size("segment"), lax.axis_size("rows")
    half = segments // 2
    row = lax.axis_index("rows")
    even = row % 2 == 0
    everyone = [(s, r) for s in range(segments) for r in range(strips)]

    def core(r):
        return r ^ 1

    def other(r):
        neighbour = r - 1 if r % 2 == 0 else r + 1
        return neighbour if 0 <= neighbour < strips else r

    def far(r):
        return other(core(r))

    def same(r):
        return r

    def swap(array, across, to):
        pairs = [
            (s * strips + r, ((s + half) % segments if across else s) * strips + to(r)) for s, r in everyone
        ]
        return lax.ppermute(array, ("segment", "rows"), pairs)

    def like(rows, dtype):
        return jax.ShapeDtypeStruct((rows, columns, channels), dtype)

    def wide(rows):
        return pltpu.VMEM((rows, columns, 3 * channels), BF16)

    def wide_out(rows):
        return jax.ShapeDtypeStruct((rows, columns, 3 * channels), BF16)

    work = 2 * columns * 9 * channels * channels
    (token,) = call(first_kernel, [jax.ShapeDtypeStruct((8, 128), F32)], [], (), 5 * 10**9)
    x_core = swap(x, False, core)
    g_core = swap(g, False, core)
    x_core, token = lax.optimization_barrier((x_core, token))
    x_far = swap(x_core, False, far)
    xa, near_first, ha, near_pre, near_here = call(
        functools.partial(near_kernel, segments),
        [wide_out(2 * own), like(2 * own - 2, F32), wide_out(2 * own - 2), like(2 * own - 4, F32), like(2 * own - 4, BF16)],
        [],
        (token, x, x_core, main, second),
        work * (4 * own - 6),
    )
    near_here, edge = lax.optimization_barrier((near_here, jnp.where(even, g_core[own - 2 :], g_core[:2])))
    near_there = swap(near_here, True, same)
    g_other = swap(edge, False, far)
    (g_rows,) = call(rows_kernel, [like(own + 4, BF16)], [], (g, g_core, g_other), 2 * 10**9)
    far_first, far_pre, hid, far_here = call(
        functools.partial(far_kernel, segments, strips),
        [like(own, F32), like(own, F32), like(own, BF16), like(own, BF16)],
        [wide(own + 2), wide(own + 2)],
        (xa, ha, x_far, main, second),
        work * 2 * own,
    )
    far_there = swap(far_here, True, same)
    (base,) = call(
        functools.partial(base_kernel, segments),
        [like(own + 2, F32)],
        [wide(own + 2)],
        (near_there, near_first, far_first, second),
        work * own,
    )
    out, gw, back, edge_other = call(
        functools.partial(middle_kernel, segments, strips),
        [like(own, BF16), wide_out(own + 2), like(own, BF16), like(2, BF16)],
        [wide(own + 2)],
        (near_here, far_here, far_there, base, g_rows, second),
        work * (2 * own + 2),
    )
    back_own = swap(back, True, same)
    back_other = swap(edge_other, True, other)
    back_core = swap(back_own, False, core)
    (edge_grad,) = call(
        functools.partial(edge_kernel, segments, strips), [like(2, BF16)], [], (g_rows, back_other, far_pre), 2 * 10**9
    )
    taps = (3, 3, channels, channels)
    halves = (3, 3, channels // 2, channels)
    terms = [jax.ShapeDtypeStruct(halves, F32), jax.ShapeDtypeStruct(halves, BF16)]
    kept2, sent2, ew = call(
        functools.partial(second_kernel, segments),
        terms + [wide_out(own + 4)],
        [],
        (g_rows, edge_grad, back_own, back_core, near_pre, far_pre, hid, near_there, far_there, gw),
        work * own,
    )
    kept1, sent1, hw = call(
        functools.partial(main_kernel, segments, strips),
        terms + [wide_out(own + 2)],
        [],
        (x, near_first, far_first, ew, gw, second),
        work * (2 * own + 2),
    )
    input_grad, output = call(input_kernel, [like(own, BF16)] * 2, [], (hw, main, out), work * own)
    factor = 1.0 / math.sqrt(own * strips * columns)

    def jump(array, bit):
        return swap(array, False, lambda r: r ^ (1 << bit))

    def meet(array, turn):
        return swap(array, False, lambda r: r ^ (turn[r % 2] << 1))

    bits = strips.bit_length() - 1
    quarter = (2, 3, 3, channels // 8, channels)
    (total2,) = call(sum_kernel, [jax.ShapeDtypeStruct(halves, F32)], [], (kept2, jump(sent2, 0)), 3 * 10**9)
    got1 = jump(sent1, 0)
    mine, *sends = call(
        pack_kernel,
        [jax.ShapeDtypeStruct(quarter, F32)] + [jax.ShapeDtypeStruct(quarter, BF16)] * 3,
        [],
        (kept1, got1, total2),
        kept1.size,
    )
    for turn, send in zip(TURNS, sends):
        mine = mine + meet(send, turn).astype(F32)
    for bit in range(3, bits):
        rounded = lax.optimization_barrier(mine.astype(BF16))
        mine = rounded.astype(F32) + jump(rounded, bit).astype(F32)
    mine = lax.optimization_barrier(mine.astype(BF16))
    gots = [meet(mine, turn) for turn in TURNS]
    (mine,) = call(
        unpack_kernel,
        [jax.ShapeDtypeStruct((2,) + halves, BF16)],
        [],
        (mine, *reversed(gots)),
        kept1.size,
    )
    theirs = jump(mine, 0)
    first_sum, second_sum = call(
        functools.partial(last_kernel, factor), [jax.ShapeDtypeStruct(taps, F32)] * 2, [], (mine, theirs), kept1.size
    )
    return (output[None], input_grad[None], first_sum[None], second_sum[None])


def solution(mesh):
    field = P("segment", "rows", None, None)
    weight = P("segment", None, None, None, None)
    return jax.shard_map(
        body,
        mesh=mesh,
        in_specs=(field, field, weight, weight),
        out_specs=(field, field, weight, weight),
        check_vma=False,
    )
```

```python
import functools
import math

import jax
import jax.numpy as jnp
from jax import lax
from jax.experimental import pallas as pl
from jax.experimental.pallas import tpu as pltpu
from jax.sharding import PartitionSpec as P

BF16 = jnp.bfloat16
F32 = jnp.float32
TAPS = [(ty, tx) for ty in range(3) for tx in range(3)]


TURNS = ((3, 3), (1, 2), (2, 1))


def silu(values):
    return values * jax.nn.sigmoid(values)


def slope(values):
    gate_value = jax.nn.sigmoid(values)
    return gate_value * (1.0 + values * (1.0 - gate_value))


def place(wide, row, values):
    columns, channels = values.shape
    column = lax.broadcasted_iota(jnp.int32, (columns, channels), 0)
    left = jnp.where(column == 0, 0.0, pltpu.roll(values, 1, 0))
    right = jnp.where(column == columns - 1, 0.0, pltpu.roll(values, columns - 1, 0))
    wide[row, :, 0:channels] = left.astype(BF16)
    wide[row, :, channels : 2 * channels] = values.astype(BF16)
    wide[row, :, 2 * channels : 3 * channels] = right.astype(BF16)


def stacked(wide, start, rows):
    parts = [wide[start + ty : start + ty + rows] for ty in range(3)]
    return jnp.concatenate([part.reshape(rows * part.shape[1], part.shape[2]) for part in parts], axis=1)


def conv(wide, start, rows, kernel):
    lhs = stacked(wide, start, rows)
    out = jnp.dot(lhs, kernel[...].reshape(-1, kernel.shape[-1]), preferred_element_type=F32)
    return out.reshape(rows, -1, out.shape[-1])


def conv_back(wide, start, rows, kernel):
    lhs = stacked(wide, start, rows)
    rhs = jnp.concatenate([kernel[2 - ty, 2 - tx] for ty, tx in TAPS], axis=1)
    out = lax.dot_general(lhs, rhs, (((1,), (1,)), ((), ())), preferred_element_type=F32)
    return out.reshape(rows, -1, out.shape[-1])


def conv_weight(field, wide, start, store):
    rows, columns, channels = field.shape
    lhs = field.reshape(rows * columns, channels)
    for ty in range(3):
        rhs = wide[start + 2 - ty : start + 2 - ty + rows]
        out = lax.dot_general(
            lhs, rhs.reshape(rows * columns, -1), (((0,), (0,)), ((), ())), preferred_element_type=F32
        )
        for tx in range(3):
            store(ty, tx, out[:, (2 - tx) * channels : (3 - tx) * channels])


def here(segments):
    row = lax.axis_index("rows")
    return lax.axis_index("segment") < segments // 2, row, lax.rem(row, 2) == 0


def inside(row, strips, own, offset):
    if offset < 0:
        return row > 0
    if offset >= own:
        return row < strips - 1
    return None


def masked(values, keep):
    return values if keep is None else jnp.where(keep, values, 0.0)


def first_kernel(token):
    token[...] = jnp.zeros_like(token)


def near_kernel(segments, token, x, x_core, main, second, xa, first, ha, pre, skip):
    encoder, _, even = here(segments)
    own = x.shape[0]
    for i in range(own):
        place(xa, jnp.where(even, 0, own) + i, x[i].astype(F32))
        place(xa, jnp.where(even, own, 0) + i, x_core[i].astype(F32))
    first[...] = conv(xa, 0, 2 * own - 2, main)

    @pl.when(encoder)
    def _():
        for i in range(2 * own - 2):
            place(ha, i, silu(first[i]))
        pre[...] = conv(ha, 0, 2 * own - 4, second)
        for i in range(2 * own - 4):
            skip[i] = silu(pre[i]).astype(BF16)


def far_kernel(segments, strips, xa, ha, x_far, main, second, first, pre, skip, hb, xb):
    encoder, row, even = here(segments)
    own = x_far.shape[0]
    near = ha.shape[0]
    columns, channels = x_far.shape[1:]
    far_in = jnp.where(even, row > 0, row < strips - 1)
    for i in range(own):
        place(xb, jnp.where(even, 0, 2) + i, masked(x_far[i].astype(F32), far_in))
    for i in range(2):
        xb[jnp.where(even, own, 0) + i] = xa[jnp.where(even, 0, 2 * own - 2) + i]
    first[...] = conv(xb, 0, own, main)

    @pl.when(encoder)
    def _():
        for i in range(own):
            keep = far_in
            if i == 0:
                keep = jnp.logical_or(far_in, jnp.logical_not(even))
            elif i == own - 1:
                keep = jnp.logical_or(far_in, even)
            place(hb, jnp.where(even, 0, 2) + i, masked(silu(first[i]), keep))
        for i in range(2):
            hb[jnp.where(even, own, 0) + i] = ha[jnp.where(even, 0, near - 2) + i]
        pre[...] = conv(hb, 0, own, second)
        for i in range(own):
            keep = jnp.logical_or(far_in, jnp.logical_not(even) if i < 2 else even)
            skip[i] = masked(silu(pre[i]), keep).astype(BF16)


def rows_kernel(g, g_core, g_other, out):
    even = lax.rem(lax.axis_index("rows"), 2) == 0
    own = g.shape[0]
    out[2 : own + 2] = g[...]
    out[0:2] = jnp.where(even, g_other[...], g_core[own - 2 :])
    out[own + 2 : own + 4] = jnp.where(even, g_core[:2], g_other[...])


def joined(even, near, far, i):
    half = near.shape[0]
    if i < half:
        return jnp.where(even, far[i], near[i])
    return jnp.where(even, near[i - half], far[i - half])


def joined_first(even, near, far, i):
    own = far.shape[0]
    t = own - 1 + i
    at_even = near[t - own - 1] if t > own else far[t - 1]
    at_odd = near[t - 1] if t < 2 * own - 1 else far[t - 2 * own + 1]
    return jnp.where(even, at_even, at_odd)


def part_conv(yw, rows, upper, kernel):
    own = rows.shape[0]
    zeros = jnp.zeros(yw.shape[1:], yw.dtype)
    for i in range(2):
        yw[jnp.where(upper, 0, own) + i] = zeros
    for i in range(own):
        place(yw, jnp.where(upper, 2, 0) + i, rows[i].astype(F32))
    return conv(yw, 0, own, kernel)


def part_row(part, upper, i):
    own = part.shape[0]
    zeros = jnp.zeros(part.shape[1:], part.dtype)
    return jnp.where(upper, part[i - 2] if i >= 2 else zeros, part[i] if i < own else zeros)


def base_kernel(segments, near, near_first, far_first, second, base, yw):
    encoder, _, even = here(segments)

    @pl.when(jnp.logical_not(encoder))
    def _():
        part = part_conv(yw, near, even, second)
        for i in range(base.shape[0]):
            base[i] = joined_first(even, near_first, far_first, i) + part_row(part, even, i)


def middle_kernel(
    segments, strips, near_here, far_here, far, base, g, second, out, gw, back, edge_other, yw
):
    encoder, row, even = here(segments)
    own = out.shape[0]

    @pl.when(encoder)
    def _():
        for i in range(own):
            out[i] = joined(even, near_here, far_here, i + 2)

    @pl.when(jnp.logical_not(encoder))
    def _():
        part = part_conv(yw, far, jnp.logical_not(even), second)
        for i in range(own + 2):
            pre = base[i] + part_row(part, jnp.logical_not(even), i)
            if 1 <= i <= own:
                out[i - 1] = silu(pre).astype(BF16)
            value = masked(g[i + 1].astype(F32) * slope(pre), inside(row, strips, own, i - 1))
            place(gw, i, value)
        back[...] = conv_back(gw, 0, own, second).astype(BF16)
        edge_other[...] = jnp.where(even, back[0:2], back[own - 2 : own])


def store(even, kept, sent):
    def put(ty, tx, values):
        half = values.shape[0] // 2
        kept[ty, tx] = jnp.where(even, values[:half], values[half:])
        sent[ty, tx] = jnp.where(even, values[half:], values[:half]).astype(BF16)

    return put


def edge_kernel(segments, strips, g, back_other, far_pre, edge_grad):
    encoder, row, even = here(segments)
    far_in = jnp.where(even, row > 0, row < strips - 1)

    @pl.when(encoder)
    def _():
        for i in range(2):
            value = g[jnp.where(even, 0, g.shape[0] - 2) + i].astype(F32) + back_other[i].astype(F32)
            value = value * slope(jnp.where(even, far_pre[i], far_pre[2 + i]))
            edge_grad[i] = masked(value, far_in).astype(BF16)


def second_kernel(segments, g, back, near_pre, far_pre, ha, hb, near, far, gw, kept, sent, ew):
    encoder, _, even = here(segments)
    own = back.shape[0]

    @pl.when(encoder)
    def _():
        for i in range(own):
            value = g[i + 2].astype(F32) + back[i].astype(F32)
            place(ew, i, value * slope(joined(even, near_pre, far_pre, i + 2)))
        rows = []
        for i in range(own + 2):
            at_even = hb[own - 2 + i] if i < 2 else ha[i - 2]
            at_odd = ha[2 + i] if i < own else hb[i - 2]
            rows.append(jnp.where(even, at_even, at_odd))
        columns, channels = back.shape[1:]
        grad = ew[:, :, channels : 2 * channels].reshape(own * columns, channels)
        for ty in range(3):
            lhs = jnp.concatenate(rows[ty : ty + own], axis=0)
            out = lax.dot_general(lhs, grad, (((0,), (0,)), ((), ())), preferred_element_type=F32)
            for tx in range(3):
                store(even, kept, sent)(ty, tx, out[tx * channels : (tx + 1) * channels])

    @pl.when(jnp.logical_not(encoder))
    def _():
        skip = jnp.stack([joined(even, near, far, i + 2) for i in range(own)])
        conv_weight(skip, gw, 0, store(even, kept, sent))


def main_kernel(
    segments, strips, x, g, edge_grad, back_core, near_pre, near_first, far_first, e_own, gw, second, kept, sent, hw, ew
):
    encoder, row, even = here(segments)
    own = x.shape[0]

    @pl.when(encoder)
    def _():
        ew[2 : own + 2] = e_own[...]
        for i in range(2):
            place(ew, jnp.where(even, 0, own + 2) + i, edge_grad[i].astype(F32))
            upstream = g[jnp.where(even, own + 2, 0) + i].astype(F32)
            returned = jnp.where(even, back_core[i].astype(F32), back_core[own - 2 + i].astype(F32))
            value = (upstream + returned) * slope(jnp.where(even, near_pre[2 + i], near_pre[i]))
            place(ew, jnp.where(even, own + 2, 0) + i, value)
        hidden_back = conv_back(ew, 0, own + 2, second)
        for i in range(own + 2):
            value = hidden_back[i] * slope(joined_first(even, near_first, far_first, i))
            place(hw, i, masked(value, inside(row, strips, own, i - 1)))

    @pl.when(jnp.logical_not(encoder))
    def _():
        hw[...] = gw[...]

    conv_weight(x[...], hw, 0, store(even, kept, sent))


def input_kernel(hw, main, out, input_grad, output):
    output[...] = out[...]
    input_grad[...] = conv_back(hw, 0, input_grad.shape[0], main).astype(BF16)


def quarters(rows):
    at = lax.axis_index("rows")
    quad = lax.rem(at // 2, 4)
    partners = [jnp.bitwise_xor(quad, jnp.where(lax.rem(at, 2) == 0, *turn)) for turn in TURNS]
    return [pl.ds(pl.multiple_of(partner * rows, rows), rows) for partner in [quad] + partners]


def sum_kernel(kept, got, out):
    out[...] = kept[...] + got[...].astype(F32)


def pack_kernel(kept1, got1, total2, mine, *sends):
    for k, rows in enumerate(quarters(mine.shape[3])):
        values = (kept1[:, :, rows, :] + got1[:, :, rows, :].astype(F32), total2[:, :, rows, :])
        for t, value in enumerate(values):
            if k == 0:
                mine[t] = value
            else:
                sends[k - 1][t] = value.astype(BF16)


def unpack_kernel(mine, *rest):
    out = rest[-1]
    for got, rows in zip((mine,) + rest[-2::-1], quarters(mine.shape[3])):
        out[:, :, :, rows, :] = got[...]


def last_kernel(factor, mine, theirs, *outs):
    even = lax.rem(lax.axis_index("rows"), 2) == 0
    rows = mine.shape[3]
    own_at = pl.ds(pl.multiple_of(jnp.where(even, 0, rows), rows), rows)
    their_at = pl.ds(pl.multiple_of(jnp.where(even, rows, 0), rows), rows)
    for t, out in enumerate(outs):
        out[:, :, own_at, :] = mine[t].astype(F32) * factor
        out[:, :, their_at, :] = theirs[t].astype(F32) * factor


def call(kernel, outs, scratch, args, flops):
    moved = sum(math.prod(a.shape) * a.dtype.itemsize for a in list(args) + outs)
    return pl.pallas_call(
        kernel,
        out_shape=outs,
        in_specs=[pl.BlockSpec(memory_space=pltpu.VMEM)] * len(args),
        out_specs=[pl.BlockSpec(memory_space=pltpu.VMEM)] * len(outs),
        scratch_shapes=scratch,
        cost_estimate=pl.CostEstimate(flops=flops, bytes_accessed=moved, transcendentals=0),
        compiler_params=pltpu.CompilerParams(vmem_limit_bytes=32 * 1024 * 1024),
    )(*args)


def body(incoming, cotangent, main_weight, second_weight):
    x, g, main, second = incoming[0], cotangent[0], main_weight[0], second_weight[0]
    own, columns, channels = x.shape
    segments, strips = lax.axis_size("segment"), lax.axis_size("rows")
    half = segments // 2
    row = lax.axis_index("rows")
    even = row % 2 == 0
    everyone = [(s, r) for s in range(segments) for r in range(strips)]

    def core(r):
        return r ^ 1

    def other(r):
        neighbour = r - 1 if r % 2 == 0 else r + 1
        return neighbour if 0 <= neighbour < strips else r

    def far(r):
        return other(core(r))

    def same(r):
        return r

    def swap(array, across, to):
        pairs = [
            (s * strips + r, ((s + half) % segments if across else s) * strips + to(r)) for s, r in everyone
        ]
        return lax.ppermute(array, ("segment", "rows"), pairs)

    def like(rows, dtype):
        return jax.ShapeDtypeStruct((rows, columns, channels), dtype)

    def wide(rows):
        return pltpu.VMEM((rows, columns, 3 * channels), BF16)

    def wide_out(rows):
        return jax.ShapeDtypeStruct((rows, columns, 3 * channels), BF16)

    work = 2 * columns * 9 * channels * channels
    (token,) = call(first_kernel, [jax.ShapeDtypeStruct((8, 128), F32)], [], (), 5 * 10**9)
    x_core = swap(x, False, core)
    g_core = swap(g, False, core)
    x_core, token = lax.optimization_barrier((x_core, token))
    x_far = swap(x_core, False, far)
    xa, near_first, ha, near_pre, near_here = call(
        functools.partial(near_kernel, segments),
        [wide_out(2 * own), like(2 * own - 2, F32), wide_out(2 * own - 2), like(2 * own - 4, F32), like(2 * own - 4, BF16)],
        [],
        (token, x, x_core, main, second),
        work * (4 * own - 6),
    )
    near_here, edge = lax.optimization_barrier((near_here, jnp.where(even, g_core[own - 2 :], g_core[:2])))
    near_there = swap(near_here, True, same)
    g_other = swap(edge, False, far)
    (g_rows,) = call(rows_kernel, [like(own + 4, BF16)], [], (g, g_core, g_other), 2 * 10**9)
    far_first, far_pre, far_here, hb = call(
        functools.partial(far_kernel, segments, strips),
        [like(own, F32), like(own, F32), like(own, BF16), wide_out(own + 2)],
        [wide(own + 2)],
        (xa, ha, x_far, main, second),
        work * 2 * own,
    )
    far_there = swap(far_here, True, same)
    (base,) = call(
        functools.partial(base_kernel, segments),
        [like(own + 2, F32)],
        [wide(own + 2)],
        (near_there, near_first, far_first, second),
        work * own,
    )
    out, gw, back, edge_other = call(
        functools.partial(middle_kernel, segments, strips),
        [like(own, BF16), wide_out(own + 2), like(own, BF16), like(2, BF16)],
        [wide(own + 2)],
        (near_here, far_here, far_there, base, g_rows, second),
        work * (2 * own + 2),
    )
    back_own = swap(back, True, same)
    back_other = swap(edge_other, True, other)
    back_core = swap(back_own, False, core)
    (edge_grad,) = call(
        functools.partial(edge_kernel, segments, strips), [like(2, BF16)], [], (g_rows, back_other, far_pre), 2 * 10**9
    )
    taps = (3, 3, channels, channels)
    halves = (3, 3, channels // 2, channels)
    terms = [jax.ShapeDtypeStruct(halves, F32), jax.ShapeDtypeStruct(halves, BF16)]
    kept2, sent2, e_own = call(
        functools.partial(second_kernel, segments),
        terms + [wide_out(own)],
        [],
        (g_rows, back_own, near_pre, far_pre, ha, hb, near_there, far_there, gw),
        work * own,
    )
    kept1, sent1, hw = call(
        functools.partial(main_kernel, segments, strips),
        terms + [wide_out(own + 2)],
        [wide(own + 4)],
        (x, g_rows, edge_grad, back_core, near_pre, near_first, far_first, e_own, gw, second),
        work * (2 * own + 2),
    )
    input_grad, output = call(input_kernel, [like(own, BF16)] * 2, [], (hw, main, out), work * own)
    factor = 1.0 / math.sqrt(own * strips * columns)

    def jump(array, bit):
        return swap(array, False, lambda r: r ^ (1 << bit))

    def meet(array, turn):
        return swap(array, False, lambda r: r ^ (turn[r % 2] << 1))

    bits = strips.bit_length() - 1
    quarter = (2, 3, 3, channels // 8, channels)
    (total2,) = call(sum_kernel, [jax.ShapeDtypeStruct(halves, F32)], [], (kept2, jump(sent2, 0)), 10**9)
    got1 = jump(sent1, 0)
    mine, *sends = call(
        pack_kernel,
        [jax.ShapeDtypeStruct(quarter, F32)] + [jax.ShapeDtypeStruct(quarter, BF16)] * 3,
        [],
        (kept1, got1, total2),
        kept1.size,
    )
    for turn, send in zip(TURNS, sends):
        mine = mine + meet(send, turn).astype(F32)
    for bit in range(3, bits):
        rounded = lax.optimization_barrier(mine.astype(BF16))
        mine = rounded.astype(F32) + jump(rounded, bit).astype(F32)
    mine = lax.optimization_barrier(mine.astype(BF16))
    gots = [meet(mine, turn) for turn in TURNS]
    (mine,) = call(
        unpack_kernel,
        [jax.ShapeDtypeStruct((2,) + halves, BF16)],
        [],
        (mine, *reversed(gots)),
        kept1.size,
    )
    theirs = jump(mine, 0)
    first_sum, second_sum = call(
        functools.partial(last_kernel, factor), [jax.ShapeDtypeStruct(taps, F32)] * 2, [], (mine, theirs), kept1.size
    )
    return (output[None], input_grad[None], first_sum[None], second_sum[None])


def solution(mesh):
    field = P("segment", "rows", None, None)
    weight = P("segment", None, None, None, None)
    return jax.shard_map(
        body,
        mesh=mesh,
        in_specs=(field, field, weight, weight),
        out_specs=(field, field, weight, weight),
        check_vma=False,
    )
```

```python
import functools
import math

import jax
import jax.numpy as jnp
from jax import lax
from jax.experimental import pallas as pl
from jax.experimental.pallas import tpu as pltpu
from jax.sharding import PartitionSpec as P

BF16 = jnp.bfloat16
F32 = jnp.float32
TAPS = [(ty, tx) for ty in range(3) for tx in range(3)]


TURNS = ((3, 3), (1, 2), (2, 1))


def silu(values):
    return values * jax.nn.sigmoid(values)


def slope(values):
    gate_value = jax.nn.sigmoid(values)
    return gate_value * (1.0 + values * (1.0 - gate_value))


def place(wide, row, values):
    columns, channels = values.shape
    column = lax.broadcasted_iota(jnp.int32, (columns, channels), 0)
    left = jnp.where(column == 0, 0.0, pltpu.roll(values, 1, 0))
    right = jnp.where(column == columns - 1, 0.0, pltpu.roll(values, columns - 1, 0))
    wide[row, :, 0:channels] = left.astype(BF16)
    wide[row, :, channels : 2 * channels] = values.astype(BF16)
    wide[row, :, 2 * channels : 3 * channels] = right.astype(BF16)


def stacked(wide, start, rows):
    parts = [wide[start + ty : start + ty + rows] for ty in range(3)]
    return jnp.concatenate([part.reshape(rows * part.shape[1], part.shape[2]) for part in parts], axis=1)


def conv(wide, start, rows, kernel):
    lhs = stacked(wide, start, rows)
    out = jnp.dot(lhs, kernel[...].reshape(-1, kernel.shape[-1]), preferred_element_type=F32)
    return out.reshape(rows, -1, out.shape[-1])


def conv_back(wide, start, rows, kernel):
    lhs = stacked(wide, start, rows)
    rhs = jnp.concatenate([kernel[2 - ty, 2 - tx] for ty, tx in TAPS], axis=1)
    out = lax.dot_general(lhs, rhs, (((1,), (1,)), ((), ())), preferred_element_type=F32)
    return out.reshape(rows, -1, out.shape[-1])


def conv_weight(field, wide, start, store):
    rows, columns, channels = field.shape
    lhs = field.reshape(rows * columns, channels)
    for ty in range(3):
        rhs = wide[start + 2 - ty : start + 2 - ty + rows]
        out = lax.dot_general(
            lhs, rhs.reshape(rows * columns, -1), (((0,), (0,)), ((), ())), preferred_element_type=F32
        )
        for tx in range(3):
            store(ty, tx, out[:, (2 - tx) * channels : (3 - tx) * channels])


def here(segments):
    row = lax.axis_index("rows")
    return lax.axis_index("segment") < segments // 2, row, lax.rem(row, 2) == 0


def inside(row, strips, own, offset):
    if offset < 0:
        return row > 0
    if offset >= own:
        return row < strips - 1
    return None


def masked(values, keep):
    return values if keep is None else jnp.where(keep, values, 0.0)


def first_kernel(token):
    token[...] = jnp.zeros_like(token)


def near_kernel(segments, token, x, x_core, main, second, xa, first, ha, pre, skip):
    encoder, _, even = here(segments)
    own = x.shape[0]
    for i in range(own):
        place(xa, jnp.where(even, 0, own) + i, x[i].astype(F32))
        place(xa, jnp.where(even, own, 0) + i, x_core[i].astype(F32))
    first[...] = conv(xa, 0, 2 * own - 2, main)

    @pl.when(encoder)
    def _():
        for i in range(2 * own - 2):
            place(ha, i, silu(first[i]))
        pre[...] = conv(ha, 0, 2 * own - 4, second)
        for i in range(2 * own - 4):
            skip[i] = silu(pre[i]).astype(BF16)


def far_kernel(segments, strips, xa, ha, x_far, main, second, first, pre, skip, hb, xb):
    encoder, row, even = here(segments)
    own = x_far.shape[0]
    near = ha.shape[0]
    columns, channels = x_far.shape[1:]
    far_in = jnp.where(even, row > 0, row < strips - 1)
    for i in range(own):
        place(xb, jnp.where(even, 0, 2) + i, masked(x_far[i].astype(F32), far_in))
    for i in range(2):
        xb[jnp.where(even, own, 0) + i] = xa[jnp.where(even, 0, 2 * own - 2) + i]
    first[...] = conv(xb, 0, own, main)

    @pl.when(encoder)
    def _():
        for i in range(own):
            keep = far_in
            if i == 0:
                keep = jnp.logical_or(far_in, jnp.logical_not(even))
            elif i == own - 1:
                keep = jnp.logical_or(far_in, even)
            place(hb, jnp.where(even, 0, 2) + i, masked(silu(first[i]), keep))
        for i in range(2):
            hb[jnp.where(even, own, 0) + i] = ha[jnp.where(even, 0, near - 2) + i]
        pre[...] = conv(hb, 0, own, second)
        for i in range(own):
            keep = jnp.logical_or(far_in, jnp.logical_not(even) if i < 2 else even)
            skip[i] = masked(silu(pre[i]), keep).astype(BF16)


def rows_kernel(g, g_core, g_other, out):
    even = lax.rem(lax.axis_index("rows"), 2) == 0
    own = g.shape[0]
    out[2 : own + 2] = g[...]
    out[0:2] = jnp.where(even, g_other[...], g_core[own - 2 :])
    out[own + 2 : own + 4] = jnp.where(even, g_core[:2], g_other[...])


def joined(even, near, far, i):
    half = near.shape[0]
    if i < half:
        return jnp.where(even, far[i], near[i])
    return jnp.where(even, near[i - half], far[i - half])


def joined_first(even, near, far, i):
    own = far.shape[0]
    t = own - 1 + i
    at_even = near[t - own - 1] if t > own else far[t - 1]
    at_odd = near[t - 1] if t < 2 * own - 1 else far[t - 2 * own + 1]
    return jnp.where(even, at_even, at_odd)


def part_conv(yw, rows, upper, kernel):
    own = rows.shape[0]
    zeros = jnp.zeros(yw.shape[1:], yw.dtype)
    for i in range(2):
        yw[jnp.where(upper, 0, own) + i] = zeros
    for i in range(own):
        place(yw, jnp.where(upper, 2, 0) + i, rows[i].astype(F32))
    return conv(yw, 0, own, kernel)


def part_row(part, upper, i):
    own = part.shape[0]
    zeros = jnp.zeros(part.shape[1:], part.dtype)
    return jnp.where(upper, part[i - 2] if i >= 2 else zeros, part[i] if i < own else zeros)


def base_kernel(segments, near, near_first, far_first, second, base, yw):
    encoder, _, even = here(segments)

    @pl.when(jnp.logical_not(encoder))
    def _():
        part = part_conv(yw, near, even, second)
        for i in range(base.shape[0]):
            base[i] = joined_first(even, near_first, far_first, i) + part_row(part, even, i)


def middle_kernel(
    segments, strips, near_here, far_here, far, base, g, second, out, gw, back, edge_other, yw
):
    encoder, row, even = here(segments)
    own = out.shape[0]

    @pl.when(encoder)
    def _():
        for i in range(own):
            out[i] = joined(even, near_here, far_here, i + 2)

    @pl.when(jnp.logical_not(encoder))
    def _():
        part = part_conv(yw, far, jnp.logical_not(even), second)
        for i in range(own + 2):
            pre = base[i] + part_row(part, jnp.logical_not(even), i)
            if 1 <= i <= own:
                out[i - 1] = silu(pre).astype(BF16)
            value = masked(g[i + 1].astype(F32) * slope(pre), inside(row, strips, own, i - 1))
            place(gw, i, value)
        back[...] = conv_back(gw, 0, own, second).astype(BF16)
        edge_other[...] = jnp.where(even, back[0:2], back[own - 2 : own])


def store(even, kept, sent):
    def put(ty, tx, values):
        half = values.shape[0] // 2
        kept[ty, tx] = jnp.where(even, values[:half], values[half:])
        sent[ty, tx] = jnp.where(even, values[half:], values[:half]).astype(BF16)

    return put


def far_edge_kernel(segments, strips, g, back_other, far_pre, edge_grad):
    encoder, row, even = here(segments)
    far_in = jnp.where(even, row > 0, row < strips - 1)

    @pl.when(encoder)
    def _():
        for i in range(2):
            value = g[jnp.where(even, 0, g.shape[0] - 2) + i].astype(F32) + back_other[i].astype(F32)
            value = value * slope(jnp.where(even, far_pre[i], far_pre[2 + i]))
            edge_grad[i] = masked(value, far_in).astype(BF16)


def core_edge_kernel(segments, g, back_core, near_pre, edge_grad):
    encoder, _, even = here(segments)
    own = back_core.shape[0]

    @pl.when(encoder)
    def _():
        for i in range(2):
            returned = jnp.where(even, back_core[i].astype(F32), back_core[own - 2 + i].astype(F32))
            value = g[jnp.where(even, g.shape[0] - 2, 0) + i].astype(F32) + returned
            value = value * slope(jnp.where(even, near_pre[2 + i], near_pre[i]))
            edge_grad[i] = value.astype(BF16)


def second_kernel(segments, g, back, near_pre, far_pre, ha, hb, near, far, gw, kept, sent, ew):
    encoder, _, even = here(segments)
    own = back.shape[0]

    @pl.when(encoder)
    def _():
        for i in range(own):
            value = g[i + 2].astype(F32) + back[i].astype(F32)
            place(ew, i, value * slope(joined(even, near_pre, far_pre, i + 2)))
        rows = []
        for i in range(own + 2):
            at_even = hb[own - 2 + i] if i < 2 else ha[i - 2]
            at_odd = ha[2 + i] if i < own else hb[i - 2]
            rows.append(jnp.where(even, at_even, at_odd))
        columns, channels = back.shape[1:]
        grad = ew[:, :, channels : 2 * channels].reshape(own * columns, channels)
        for ty in range(3):
            lhs = jnp.concatenate(rows[ty : ty + own], axis=0)
            out = lax.dot_general(lhs, grad, (((0,), (0,)), ((), ())), preferred_element_type=F32)
            for tx in range(3):
                store(even, kept, sent)(ty, tx, out[tx * channels : (tx + 1) * channels])

    @pl.when(jnp.logical_not(encoder))
    def _():
        skip = jnp.stack([joined(even, near, far, i + 2) for i in range(own)])
        conv_weight(skip, gw, 0, store(even, kept, sent))


def main_kernel(
    segments, strips, x, far_edge, core_edge, near_first, far_first, e_own, gw, second, kept, sent, hw, ew
):
    encoder, row, even = here(segments)
    own = x.shape[0]

    @pl.when(encoder)
    def _():
        ew[2 : own + 2] = e_own[...]
        for i in range(2):
            place(ew, jnp.where(even, 0, own + 2) + i, far_edge[i].astype(F32))
            place(ew, jnp.where(even, own + 2, 0) + i, core_edge[i].astype(F32))
        hidden_back = conv_back(ew, 0, own + 2, second)
        for i in range(own + 2):
            value = hidden_back[i] * slope(joined_first(even, near_first, far_first, i))
            place(hw, i, masked(value, inside(row, strips, own, i - 1)))

    @pl.when(jnp.logical_not(encoder))
    def _():
        hw[...] = gw[...]

    conv_weight(x[...], hw, 0, store(even, kept, sent))


def input_kernel(hw, main, out, input_grad, output):
    output[...] = out[...]
    input_grad[...] = conv_back(hw, 0, input_grad.shape[0], main).astype(BF16)


def quarters(rows):
    at = lax.axis_index("rows")
    quad = lax.rem(at // 2, 4)
    partners = [jnp.bitwise_xor(quad, jnp.where(lax.rem(at, 2) == 0, *turn)) for turn in TURNS]
    return [pl.ds(pl.multiple_of(partner * rows, rows), rows) for partner in [quad] + partners]


def sum_kernel(kept, got, out):
    out[...] = kept[...] + got[...].astype(F32)


def pack_kernel(kept1, got1, total2, mine, *sends):
    for k, rows in enumerate(quarters(mine.shape[3])):
        values = (kept1[:, :, rows, :] + got1[:, :, rows, :].astype(F32), total2[:, :, rows, :])
        for t, value in enumerate(values):
            if k == 0:
                mine[t] = value
            else:
                sends[k - 1][t] = value.astype(BF16)


def unpack_kernel(mine, *rest):
    out = rest[-1]
    for got, rows in zip((mine,) + rest[-2::-1], quarters(mine.shape[3])):
        out[:, :, :, rows, :] = got[...]


def last_kernel(factor, mine, theirs, *outs):
    even = lax.rem(lax.axis_index("rows"), 2) == 0
    rows = mine.shape[3]
    own_at = pl.ds(pl.multiple_of(jnp.where(even, 0, rows), rows), rows)
    their_at = pl.ds(pl.multiple_of(jnp.where(even, rows, 0), rows), rows)
    for t, out in enumerate(outs):
        out[:, :, own_at, :] = mine[t].astype(F32) * factor
        out[:, :, their_at, :] = theirs[t].astype(F32) * factor


def call(kernel, outs, scratch, args, flops):
    moved = sum(math.prod(a.shape) * a.dtype.itemsize for a in list(args) + outs)
    return pl.pallas_call(
        kernel,
        out_shape=outs,
        in_specs=[pl.BlockSpec(memory_space=pltpu.VMEM)] * len(args),
        out_specs=[pl.BlockSpec(memory_space=pltpu.VMEM)] * len(outs),
        scratch_shapes=scratch,
        cost_estimate=pl.CostEstimate(flops=flops, bytes_accessed=moved, transcendentals=0),
        compiler_params=pltpu.CompilerParams(vmem_limit_bytes=32 * 1024 * 1024),
    )(*args)


def body(incoming, cotangent, main_weight, second_weight):
    x, g, main, second = incoming[0], cotangent[0], main_weight[0], second_weight[0]
    own, columns, channels = x.shape
    segments, strips = lax.axis_size("segment"), lax.axis_size("rows")
    half = segments // 2
    row = lax.axis_index("rows")
    even = row % 2 == 0
    everyone = [(s, r) for s in range(segments) for r in range(strips)]

    def core(r):
        return r ^ 1

    def other(r):
        neighbour = r - 1 if r % 2 == 0 else r + 1
        return neighbour if 0 <= neighbour < strips else r

    def far(r):
        return other(core(r))

    def same(r):
        return r

    def swap(array, across, to):
        pairs = [
            (s * strips + r, ((s + half) % segments if across else s) * strips + to(r)) for s, r in everyone
        ]
        return lax.ppermute(array, ("segment", "rows"), pairs)

    def like(rows, dtype):
        return jax.ShapeDtypeStruct((rows, columns, channels), dtype)

    def wide(rows):
        return pltpu.VMEM((rows, columns, 3 * channels), BF16)

    def wide_out(rows):
        return jax.ShapeDtypeStruct((rows, columns, 3 * channels), BF16)

    work = 2 * columns * 9 * channels * channels
    (token,) = call(first_kernel, [jax.ShapeDtypeStruct((8, 128), F32)], [], (), 5 * 10**9)
    x_core = swap(x, False, core)
    g_core = swap(g, False, core)
    x_core, token = lax.optimization_barrier((x_core, token))
    x_far = swap(x_core, False, far)
    xa, near_first, ha, near_pre, near_here = call(
        functools.partial(near_kernel, segments),
        [wide_out(2 * own), like(2 * own - 2, F32), wide_out(2 * own - 2), like(2 * own - 4, F32), like(2 * own - 4, BF16)],
        [],
        (token, x, x_core, main, second),
        work * (4 * own - 6),
    )
    near_here, edge = lax.optimization_barrier((near_here, jnp.where(even, g_core[own - 2 :], g_core[:2])))
    near_there = swap(near_here, True, same)
    g_other = swap(edge, False, far)
    (g_rows,) = call(rows_kernel, [like(own + 4, BF16)], [], (g, g_core, g_other), 2 * 10**9)
    far_first, far_pre, far_here, hb = call(
        functools.partial(far_kernel, segments, strips),
        [like(own, F32), like(own, F32), like(own, BF16), wide_out(own + 2)],
        [wide(own + 2)],
        (xa, ha, x_far, main, second),
        work * 2 * own,
    )
    far_there = swap(far_here, True, same)
    (base,) = call(
        functools.partial(base_kernel, segments),
        [like(own + 2, F32)],
        [wide(own + 2)],
        (near_there, near_first, far_first, second),
        work * own,
    )
    out, gw, back, edge_other = call(
        functools.partial(middle_kernel, segments, strips),
        [like(own, BF16), wide_out(own + 2), like(own, BF16), like(2, BF16)],
        [wide(own + 2)],
        (near_here, far_here, far_there, base, g_rows, second),
        work * (2 * own + 2),
    )
    back_own = swap(back, True, same)
    back_other = swap(edge_other, True, other)
    back_core = swap(back_own, False, core)
    (far_edge,) = call(
        functools.partial(far_edge_kernel, segments, strips), [like(2, BF16)], [], (g_rows, back_other, far_pre), 10**9
    )
    (core_edge,) = call(
        functools.partial(core_edge_kernel, segments), [like(2, BF16)], [], (g_rows, back_core, near_pre), 10**6
    )
    taps = (3, 3, channels, channels)
    halves = (3, 3, channels // 2, channels)
    terms = [jax.ShapeDtypeStruct(halves, F32), jax.ShapeDtypeStruct(halves, BF16)]
    kept2, sent2, e_own = call(
        functools.partial(second_kernel, segments),
        terms + [wide_out(own)],
        [],
        (g_rows, back_own, near_pre, far_pre, ha, hb, near_there, far_there, gw),
        work * own,
    )
    kept1, sent1, hw = call(
        functools.partial(main_kernel, segments, strips),
        terms + [wide_out(own + 2)],
        [wide(own + 4)],
        (x, far_edge, core_edge, near_first, far_first, e_own, gw, second),
        work * (2 * own + 2),
    )
    input_grad, output = call(input_kernel, [like(own, BF16)] * 2, [], (hw, main, out), work * own)
    factor = 1.0 / math.sqrt(own * strips * columns)

    def jump(array, bit):
        return swap(array, False, lambda r: r ^ (1 << bit))

    def meet(array, turn):
        return swap(array, False, lambda r: r ^ (turn[r % 2] << 1))

    bits = strips.bit_length() - 1
    quarter = (2, 3, 3, channels // 8, channels)
    (total2,) = call(sum_kernel, [jax.ShapeDtypeStruct(halves, F32)], [], (kept2, jump(sent2, 0)), 6 * 10**9)
    got1 = jump(sent1, 0)
    mine, *sends = call(
        pack_kernel,
        [jax.ShapeDtypeStruct(quarter, F32)] + [jax.ShapeDtypeStruct(quarter, BF16)] * 3,
        [],
        (kept1, got1, total2),
        kept1.size,
    )
    for turn, send in zip(TURNS, sends):
        mine = mine + meet(send, turn).astype(F32)
    for bit in range(3, bits):
        rounded = lax.optimization_barrier(mine.astype(BF16))
        mine = rounded.astype(F32) + jump(rounded, bit).astype(F32)
    mine = lax.optimization_barrier(mine.astype(BF16))
    gots = [meet(mine, turn) for turn in TURNS]
    (mine,) = call(
        unpack_kernel,
        [jax.ShapeDtypeStruct((2,) + halves, BF16)],
        [],
        (mine, *reversed(gots)),
        kept1.size,
    )
    theirs = jump(mine, 0)
    first_sum, second_sum = call(
        functools.partial(last_kernel, factor), [jax.ShapeDtypeStruct(taps, F32)] * 2, [], (mine, theirs), kept1.size
    )
    return (output[None], input_grad[None], first_sum[None], second_sum[None])


def solution(mesh):
    field = P("segment", "rows", None, None)
    weight = P("segment", None, None, None, None)
    return jax.shard_map(
        body,
        mesh=mesh,
        in_specs=(field, field, weight, weight),
        out_specs=(field, field, weight, weight),
        check_vma=False,
    )
```

```python
import functools
import math

import jax
import jax.numpy as jnp
from jax import lax
from jax.experimental import pallas as pl
from jax.experimental.pallas import tpu as pltpu
from jax.sharding import PartitionSpec as P

BF16 = jnp.bfloat16
F32 = jnp.float32
TAPS = [(ty, tx) for ty in range(3) for tx in range(3)]


TURNS = ((3, 3), (2, 1), (1, 2))


def silu(values):
    return values * jax.nn.sigmoid(values)


def slope(values):
    gate_value = jax.nn.sigmoid(values)
    return gate_value * (1.0 + values * (1.0 - gate_value))


def place(wide, row, values):
    columns, channels = values.shape
    column = lax.broadcasted_iota(jnp.int32, (columns, channels), 0)
    left = jnp.where(column == 0, 0.0, pltpu.roll(values, 1, 0))
    right = jnp.where(column == columns - 1, 0.0, pltpu.roll(values, columns - 1, 0))
    wide[row, :, 0:channels] = left.astype(BF16)
    wide[row, :, channels : 2 * channels] = values.astype(BF16)
    wide[row, :, 2 * channels : 3 * channels] = right.astype(BF16)


def stacked(wide, start, rows):
    parts = [wide[start + ty : start + ty + rows] for ty in range(3)]
    return jnp.concatenate([part.reshape(rows * part.shape[1], part.shape[2]) for part in parts], axis=1)


def conv(wide, start, rows, kernel):
    lhs = stacked(wide, start, rows)
    out = jnp.dot(lhs, kernel[...].reshape(-1, kernel.shape[-1]), preferred_element_type=F32)
    return out.reshape(rows, -1, out.shape[-1])


def conv_back(wide, start, rows, kernel):
    lhs = stacked(wide, start, rows)
    rhs = jnp.concatenate([kernel[2 - ty, 2 - tx] for ty, tx in TAPS], axis=1)
    out = lax.dot_general(lhs, rhs, (((1,), (1,)), ((), ())), preferred_element_type=F32)
    return out.reshape(rows, -1, out.shape[-1])


def conv_weight(field, wide, start, store):
    rows, columns, channels = field.shape
    lhs = field.reshape(rows * columns, channels)
    for ty in range(3):
        rhs = wide[start + 2 - ty : start + 2 - ty + rows]
        out = lax.dot_general(
            lhs, rhs.reshape(rows * columns, -1), (((0,), (0,)), ((), ())), preferred_element_type=F32
        )
        for tx in range(3):
            store(ty, tx, out[:, (2 - tx) * channels : (3 - tx) * channels])


def here(segments):
    row = lax.axis_index("rows")
    return lax.axis_index("segment") < segments // 2, row, lax.rem(row, 2) == 0


def inside(row, strips, own, offset):
    if offset < 0:
        return row > 0
    if offset >= own:
        return row < strips - 1
    return None


def masked(values, keep):
    return values if keep is None else jnp.where(keep, values, 0.0)


def first_kernel(token):
    token[...] = jnp.zeros_like(token)


def near_kernel(segments, token, x, x_core, main, second, xa, first, ha, pre, skip):
    encoder, _, even = here(segments)
    own = x.shape[0]
    for i in range(own):
        place(xa, jnp.where(even, 0, own) + i, x[i].astype(F32))
        place(xa, jnp.where(even, own, 0) + i, x_core[i].astype(F32))
    first[...] = conv(xa, 0, 2 * own - 2, main)

    @pl.when(encoder)
    def _():
        for i in range(2 * own - 2):
            place(ha, i, silu(first[i]))
        pre[...] = conv(ha, 0, 2 * own - 4, second)
        for i in range(2 * own - 4):
            skip[i] = silu(pre[i]).astype(BF16)


def far_kernel(segments, strips, xa, ha, x_far, main, second, first, pre, skip, hb, xb):
    encoder, row, even = here(segments)
    own = x_far.shape[0]
    near = ha.shape[0]
    columns, channels = x_far.shape[1:]
    far_in = jnp.where(even, row > 0, row < strips - 1)
    for i in range(own):
        place(xb, jnp.where(even, 0, 2) + i, masked(x_far[i].astype(F32), far_in))
    for i in range(2):
        xb[jnp.where(even, own, 0) + i] = xa[jnp.where(even, 0, 2 * own - 2) + i]
    first[...] = conv(xb, 0, own, main)

    @pl.when(encoder)
    def _():
        for i in range(own):
            keep = far_in
            if i == 0:
                keep = jnp.logical_or(far_in, jnp.logical_not(even))
            elif i == own - 1:
                keep = jnp.logical_or(far_in, even)
            place(hb, jnp.where(even, 0, 2) + i, masked(silu(first[i]), keep))
        for i in range(2):
            hb[jnp.where(even, own, 0) + i] = ha[jnp.where(even, 0, near - 2) + i]
        pre[...] = conv(hb, 0, own, second)
        for i in range(own):
            keep = jnp.logical_or(far_in, jnp.logical_not(even) if i < 2 else even)
            skip[i] = masked(silu(pre[i]), keep).astype(BF16)


def rows_kernel(g, g_core, g_other, out):
    even = lax.rem(lax.axis_index("rows"), 2) == 0
    own = g.shape[0]
    out[2 : own + 2] = g[...]
    out[0:2] = jnp.where(even, g_other[...], g_core[own - 2 :])
    out[own + 2 : own + 4] = jnp.where(even, g_core[:2], g_other[...])


def joined(even, near, far, i):
    half = near.shape[0]
    if i < half:
        return jnp.where(even, far[i], near[i])
    return jnp.where(even, near[i - half], far[i - half])


def joined_first(even, near, far, i):
    own = far.shape[0]
    t = own - 1 + i
    at_even = near[t - own - 1] if t > own else far[t - 1]
    at_odd = near[t - 1] if t < 2 * own - 1 else far[t - 2 * own + 1]
    return jnp.where(even, at_even, at_odd)


def part_conv(yw, rows, upper, kernel):
    own = rows.shape[0]
    zeros = jnp.zeros(yw.shape[1:], yw.dtype)
    for i in range(2):
        yw[jnp.where(upper, 0, own) + i] = zeros
    for i in range(own):
        place(yw, jnp.where(upper, 2, 0) + i, rows[i].astype(F32))
    return conv(yw, 0, own, kernel)


def part_row(part, upper, i):
    own = part.shape[0]
    zeros = jnp.zeros(part.shape[1:], part.dtype)
    return jnp.where(upper, part[i - 2] if i >= 2 else zeros, part[i] if i < own else zeros)


def base_kernel(segments, near, near_first, far_first, second, base, yw):
    encoder, _, even = here(segments)

    @pl.when(jnp.logical_not(encoder))
    def _():
        part = part_conv(yw, near, even, second)
        for i in range(base.shape[0]):
            base[i] = joined_first(even, near_first, far_first, i) + part_row(part, even, i)


def middle_kernel(
    segments, strips, near_here, far_here, far, base, g, second, out, gw, back, edge_other, yw
):
    encoder, row, even = here(segments)
    own = out.shape[0]

    @pl.when(encoder)
    def _():
        for i in range(own):
            out[i] = joined(even, near_here, far_here, i + 2)

    @pl.when(jnp.logical_not(encoder))
    def _():
        part = part_conv(yw, far, jnp.logical_not(even), second)
        for i in range(own + 2):
            pre = base[i] + part_row(part, jnp.logical_not(even), i)
            if 1 <= i <= own:
                out[i - 1] = silu(pre).astype(BF16)
            value = masked(g[i + 1].astype(F32) * slope(pre), inside(row, strips, own, i - 1))
            place(gw, i, value)
        back[...] = conv_back(gw, 0, own, second).astype(BF16)
        edge_other[...] = jnp.where(even, back[0:2], back[own - 2 : own])


def store(even, kept, sent):
    def put(ty, tx, values):
        half = values.shape[0] // 2
        kept[ty, tx] = jnp.where(even, values[:half], values[half:])
        sent[ty, tx] = jnp.where(even, values[half:], values[:half]).astype(BF16)

    return put


def far_edge_kernel(segments, strips, g, back_other, far_pre, edge_grad):
    encoder, row, even = here(segments)
    far_in = jnp.where(even, row > 0, row < strips - 1)

    @pl.when(encoder)
    def _():
        for i in range(2):
            value = g[jnp.where(even, 0, g.shape[0] - 2) + i].astype(F32) + back_other[i].astype(F32)
            value = value * slope(jnp.where(even, far_pre[i], far_pre[2 + i]))
            edge_grad[i] = masked(value, far_in).astype(BF16)


def core_edge_kernel(segments, g, back_core, near_pre, edge_grad):
    encoder, _, even = here(segments)
    own = back_core.shape[0]

    @pl.when(encoder)
    def _():
        for i in range(2):
            returned = jnp.where(even, back_core[i].astype(F32), back_core[own - 2 + i].astype(F32))
            value = g[jnp.where(even, g.shape[0] - 2, 0) + i].astype(F32) + returned
            value = value * slope(jnp.where(even, near_pre[2 + i], near_pre[i]))
            edge_grad[i] = value.astype(BF16)


def second_kernel(segments, g, back, near_pre, far_pre, ha, hb, near, far, gw, kept, sent, ew):
    encoder, _, even = here(segments)
    own = back.shape[0]

    @pl.when(encoder)
    def _():
        for i in range(own):
            value = g[i + 2].astype(F32) + back[i].astype(F32)
            place(ew, i, value * slope(joined(even, near_pre, far_pre, i + 2)))
        rows = []
        for i in range(own + 2):
            at_even = hb[own - 2 + i] if i < 2 else ha[i - 2]
            at_odd = ha[2 + i] if i < own else hb[i - 2]
            rows.append(jnp.where(even, at_even, at_odd))
        columns, channels = back.shape[1:]
        grad = ew[:, :, channels : 2 * channels].reshape(own * columns, channels)
        for ty in range(3):
            lhs = jnp.concatenate(rows[ty : ty + own], axis=0)
            out = lax.dot_general(lhs, grad, (((0,), (0,)), ((), ())), preferred_element_type=F32)
            for tx in range(3):
                store(even, kept, sent)(ty, tx, out[tx * channels : (tx + 1) * channels])

    @pl.when(jnp.logical_not(encoder))
    def _():
        skip = jnp.stack([joined(even, near, far, i + 2) for i in range(own)])
        conv_weight(skip, gw, 0, store(even, kept, sent))


def main_kernel(
    segments, strips, x, far_edge, core_edge, near_first, far_first, e_own, gw, second, kept, sent, hw, ew
):
    encoder, row, even = here(segments)
    own = x.shape[0]

    @pl.when(encoder)
    def _():
        ew[2 : own + 2] = e_own[...]
        for i in range(2):
            place(ew, jnp.where(even, 0, own + 2) + i, far_edge[i].astype(F32))
            place(ew, jnp.where(even, own + 2, 0) + i, core_edge[i].astype(F32))
        hidden_back = conv_back(ew, 0, own + 2, second)
        for i in range(own + 2):
            value = hidden_back[i] * slope(joined_first(even, near_first, far_first, i))
            place(hw, i, masked(value, inside(row, strips, own, i - 1)))

    @pl.when(jnp.logical_not(encoder))
    def _():
        hw[...] = gw[...]

    conv_weight(x[...], hw, 0, store(even, kept, sent))


def input_kernel(hw, main, out, input_grad, output):
    output[...] = out[...]
    input_grad[...] = conv_back(hw, 0, input_grad.shape[0], main).astype(BF16)


def quarters(rows):
    at = lax.axis_index("rows")
    quad = lax.rem(at // 2, 4)
    partners = [jnp.bitwise_xor(quad, jnp.where(lax.rem(at, 2) == 0, *turn)) for turn in TURNS]
    return [pl.ds(pl.multiple_of(partner * rows, rows), rows) for partner in [quad] + partners]


def sum_kernel(kept, got, out):
    out[...] = kept[...] + got[...].astype(F32)


def pack_kernel(kept1, got1, total2, mine, *sends):
    for k, rows in enumerate(quarters(mine.shape[3])):
        values = (kept1[:, :, rows, :] + got1[:, :, rows, :].astype(F32), total2[:, :, rows, :])
        for t, value in enumerate(values):
            if k == 0:
                mine[t] = value
            else:
                sends[k - 1][t] = value.astype(BF16)


def unpack_kernel(mine, *rest):
    out = rest[-1]
    for got, rows in zip((mine,) + rest[-2::-1], quarters(mine.shape[3])):
        out[:, :, :, rows, :] = got[...]


def last_kernel(factor, mine, theirs, *outs):
    even = lax.rem(lax.axis_index("rows"), 2) == 0
    rows = mine.shape[3]
    own_at = pl.ds(pl.multiple_of(jnp.where(even, 0, rows), rows), rows)
    their_at = pl.ds(pl.multiple_of(jnp.where(even, rows, 0), rows), rows)
    for t, out in enumerate(outs):
        out[:, :, own_at, :] = mine[t].astype(F32) * factor
        out[:, :, their_at, :] = theirs[t].astype(F32) * factor


def call(kernel, outs, scratch, args, flops):
    moved = sum(math.prod(a.shape) * a.dtype.itemsize for a in list(args) + outs)
    return pl.pallas_call(
        kernel,
        out_shape=outs,
        in_specs=[pl.BlockSpec(memory_space=pltpu.VMEM)] * len(args),
        out_specs=[pl.BlockSpec(memory_space=pltpu.VMEM)] * len(outs),
        scratch_shapes=scratch,
        cost_estimate=pl.CostEstimate(flops=flops, bytes_accessed=moved, transcendentals=0),
        compiler_params=pltpu.CompilerParams(vmem_limit_bytes=32 * 1024 * 1024),
    )(*args)


def body(incoming, cotangent, main_weight, second_weight):
    x, g, main, second = incoming[0], cotangent[0], main_weight[0], second_weight[0]
    own, columns, channels = x.shape
    segments, strips = lax.axis_size("segment"), lax.axis_size("rows")
    half = segments // 2
    row = lax.axis_index("rows")
    even = row % 2 == 0
    everyone = [(s, r) for s in range(segments) for r in range(strips)]

    def core(r):
        return r ^ 1

    def other(r):
        neighbour = r - 1 if r % 2 == 0 else r + 1
        return neighbour if 0 <= neighbour < strips else r

    def far(r):
        return other(core(r))

    def same(r):
        return r

    def swap(array, across, to):
        pairs = [
            (s * strips + r, ((s + half) % segments if across else s) * strips + to(r)) for s, r in everyone
        ]
        return lax.ppermute(array, ("segment", "rows"), pairs)

    def like(rows, dtype):
        return jax.ShapeDtypeStruct((rows, columns, channels), dtype)

    def wide(rows):
        return pltpu.VMEM((rows, columns, 3 * channels), BF16)

    def wide_out(rows):
        return jax.ShapeDtypeStruct((rows, columns, 3 * channels), BF16)

    work = 2 * columns * 9 * channels * channels
    (token,) = call(first_kernel, [jax.ShapeDtypeStruct((8, 128), F32)], [], (), 5 * 10**9)
    x_core = swap(x, False, core)
    g_core = swap(g, False, core)
    x_core, token = lax.optimization_barrier((x_core, token))
    x_far = swap(x_core, False, far)
    xa, near_first, ha, near_pre, near_here = call(
        functools.partial(near_kernel, segments),
        [wide_out(2 * own), like(2 * own - 2, F32), wide_out(2 * own - 2), like(2 * own - 4, F32), like(2 * own - 4, BF16)],
        [],
        (token, x, x_core, main, second),
        work * (4 * own - 6),
    )
    near_here, edge = lax.optimization_barrier((near_here, jnp.where(even, g_core[own - 2 :], g_core[:2])))
    near_there = swap(near_here, True, same)
    g_other = swap(edge, False, far)
    (g_rows,) = call(rows_kernel, [like(own + 4, BF16)], [], (g, g_core, g_other), 2 * 10**9)
    far_first, far_pre, far_here, hb = call(
        functools.partial(far_kernel, segments, strips),
        [like(own, F32), like(own, F32), like(own, BF16), wide_out(own + 2)],
        [wide(own + 2)],
        (xa, ha, x_far, main, second),
        work * 2 * own,
    )
    far_there = swap(far_here, True, same)
    (base,) = call(
        functools.partial(base_kernel, segments),
        [like(own + 2, F32)],
        [wide(own + 2)],
        (near_there, near_first, far_first, second),
        work * own,
    )
    out, gw, back, edge_other = call(
        functools.partial(middle_kernel, segments, strips),
        [like(own, BF16), wide_out(own + 2), like(own, BF16), like(2, BF16)],
        [wide(own + 2)],
        (near_here, far_here, far_there, base, g_rows, second),
        work * (2 * own + 2),
    )
    back_own = swap(back, True, same)
    back_other = swap(edge_other, True, other)
    back_core = swap(back_own, False, core)
    (far_edge,) = call(
        functools.partial(far_edge_kernel, segments, strips), [like(2, BF16)], [], (g_rows, back_other, far_pre), 10**9
    )
    (core_edge,) = call(
        functools.partial(core_edge_kernel, segments), [like(2, BF16)], [], (g_rows, back_core, near_pre), 10**6
    )
    taps = (3, 3, channels, channels)
    halves = (3, 3, channels // 2, channels)
    terms = [jax.ShapeDtypeStruct(halves, F32), jax.ShapeDtypeStruct(halves, BF16)]
    kept2, sent2, e_own = call(
        functools.partial(second_kernel, segments),
        terms + [wide_out(own)],
        [],
        (g_rows, back_own, near_pre, far_pre, ha, hb, near_there, far_there, gw),
        work * own,
    )
    kept1, sent1, hw = call(
        functools.partial(main_kernel, segments, strips),
        terms + [wide_out(own + 2)],
        [wide(own + 4)],
        (x, far_edge, core_edge, near_first, far_first, e_own, gw, second),
        work * (2 * own + 2),
    )
    input_grad, output = call(input_kernel, [like(own, BF16)] * 2, [], (hw, main, out), work * own)
    factor = 1.0 / math.sqrt(own * strips * columns)

    def jump(array, bit):
        return swap(array, False, lambda r: r ^ (1 << bit))

    def meet(array, turn):
        return swap(array, False, lambda r: r ^ (turn[r % 2] << 1))

    bits = strips.bit_length() - 1
    quarter = (2, 3, 3, channels // 8, channels)
    (total2,) = call(sum_kernel, [jax.ShapeDtypeStruct(halves, F32)], [], (kept2, jump(sent2, 0)), 6 * 10**9)
    got1 = jump(sent1, 0)
    mine, *sends = call(
        pack_kernel,
        [jax.ShapeDtypeStruct(quarter, F32)] + [jax.ShapeDtypeStruct(quarter, BF16)] * 3,
        [],
        (kept1, got1, total2),
        kept1.size,
    )
    for turn, send in zip(TURNS, sends):
        mine = mine + meet(send, turn).astype(F32)
    for bit in range(3, bits):
        rounded = lax.optimization_barrier(mine.astype(BF16))
        mine = rounded.astype(F32) + jump(rounded, bit).astype(F32)
    mine = lax.optimization_barrier(mine.astype(BF16))
    gots = [meet(mine, turn) for turn in TURNS]
    (mine,) = call(
        unpack_kernel,
        [jax.ShapeDtypeStruct((2,) + halves, BF16)],
        [],
        (mine, *reversed(gots)),
        kept1.size,
    )
    theirs = jump(mine, 0)
    first_sum, second_sum = call(
        functools.partial(last_kernel, factor), [jax.ShapeDtypeStruct(taps, F32)] * 2, [], (mine, theirs), kept1.size
    )
    return (output[None], input_grad[None], first_sum[None], second_sum[None])


def solution(mesh):
    field = P("segment", "rows", None, None)
    weight = P("segment", None, None, None, None)
    return jax.shard_map(
        body,
        mesh=mesh,
        in_specs=(field, field, weight, weight),
        out_specs=(field, field, weight, weight),
        check_vma=False,
    )
```
